32 devices in a mesh: grow: 2 (over x), cy: 4 (over y, core), cz: 4 (over z).
Axes of the slice: x: 2, y: 2, z: 4, core: 2. Of those that a mesh axis runs over, the one named last changes fastest.
Arguments:
- labels: int32 [8, 512, 512], P('grow', 'cy', 'cz'), may hold values 0 or 1
- roughness: float32 [8, 512, 512], P('grow', 'cy', 'cz'), may hold values from 0 to 1
- potential: float32 [8, 512, 512], P('grow', 'cy', 'cz'), may hold values from 0 to 1
- displacement: float32 [3, 8, 512, 512], P(None, 'grow', 'cy', 'cz'), may hold values from -1.8 to 1.8
Outputs:
- phase_out: float32 [8, 512, 512], P('grow', 'cy', 'cz')
- potential_out: float32 [8, 512, 512], P('grow', 'cy', 'cz')
- displacement_out: float32 [3, 8, 512, 512], P(None, 'grow', 'cy', 'cz')
The draws below stay inside these ranges and needn't reach their ends.
All inputs are finite; a program needn't handle non-finite values. No bound on the sum of `labels` on one device may be relied on, other than what follows from the above.
Results may differ from the reference program's by a relative error of at most 0.00002.
Values sent between devices are 32-bit elements; how exact they have to be, the bound alone decides.
No kernel may reach another device: no remote copies, remote signals or barrier semaphores. Data moves between devices by JAX's collectives and lax.ppermute only.
A program may use at most 64 MiB of HBM per device.

```python
import jax
import jax.numpy as jnp

STEPS = 2
SWEEPS = 3
NX = 8
NY = 512
NZ = 512
SHIFT = 4


def set_ends(result, own_key, least, top_value):
    spot = [jax.random.randint(jax.random.fold_in(own_key, axis), (), 0, length) for axis, length in enumerate(result.shape)]
    widest = result.shape.index(max(result.shape))
    beside = spot[:widest] + [(spot[widest] + 1) % result.shape[widest]] + spot[widest + 1:]
    return result.at[tuple(spot)].set(least).at[tuple(beside)].set(top_value)


def block_scale(stream_key, shape, cuts, smallest, high):
    loudness, own = 1.0, jax.random.fold_in(stream_key, 6)
    for dim, parts in cuts:
        draws = jnp.exp(jax.random.uniform(jax.random.fold_in(own, dim), (parts,), jnp.float32, smallest / len(cuts), high / len(cuts)))
        loudness = loudness * jnp.repeat(draws, shape[dim] // parts).reshape([-1 if axis == dim else 1 for axis in range(len(shape))])
    return loudness


def bell_draw(own_key, dims, deviation, most, shards=(), held_as=jnp.bfloat16):
    gain = block_scale(own_key, dims, shards, -0.22, 0.18) if shards else 1.0
    values = jax.random.normal(own_key, dims, jnp.float32) * deviation * gain
    return jnp.minimum(jnp.maximum(values, -most), most).astype(held_as)


def setup_inputs(seed: int = 0) -> dict:
    key_of = jax.random.split(jax.random.key(seed), 5)
    labels = set_ends((jax.random.randint(key_of[0], (NX, NY, NZ), 0, 3) < 1).astype(jnp.int32), jax.random.fold_in(key_of[0], 1), 0, 1)
    roughness = jnp.clip(1.0 * jax.random.uniform(key_of[1], (NX, NY, NZ), jnp.float32) ** block_scale(key_of[1], (NX, NY, NZ), ((0, 2), (1, 4), (2, 4)), -0.2, 0.2), 0.0, 1.0)
    potential = jnp.clip(1.0 * jax.random.uniform(key_of[2], (NX, NY, NZ), jnp.float32) ** block_scale(key_of[2], (NX, NY, NZ), ((0, 2), (1, 4), (2, 4)), -0.2, 0.2), 0.0, 1.0)
    displacement = bell_draw(key_of[3], (3, NX, NY, NZ), 0.3, 1.8, ((1, 2), (2, 4), (3, 4)), jnp.float32)
    return dict(labels=labels, roughness=roughness, potential=potential, displacement=displacement)


TAU_P = 0.15
TAU_U = 0.08
SHEAR = 1.0
LAME_FIRST = 1.5
STIFF = 6.5
EIGEN = 0.1
COND_EL = 0.1
COND_LI = 0.9
V_HIGH = 1.0
TIME_STEP = 0.05
REST = 0.5
OMEGA_THIRD = 0.1
RATE = 0.5


def unit(direction, sign):
    offsets = [0, 0, 0]
    offsets[direction] = sign
    return offsets


def offset(field, offsets):
    lead_dims = field.ndim - 3
    slices = [slice(None)] * lead_dims
    for direction in range(3):
        extent = field.shape[lead_dims + direction]
        slices.append(slice(1 + offsets[direction], extent - 1 + offsets[direction]))
    return field[tuple(slices)]


def centre(field):
    return offset(field, (0, 0, 0))


def laplace(field):
    total = -6.0 * centre(field)
    for direction in range(3):
        total = total + offset(field, unit(direction, 1)) + offset(field, unit(direction, -1))
    return total


def interp(phase):
    return phase * phase * (3.0 - 2.0 * phase)


def interp_slope(phase):
    return 6.0 * phase * (1.0 - phase)


def potential_sweep(potential_pad, conduct_pad):
    here = centre(potential_pad)
    conduct_here = centre(conduct_pad)
    flux = jnp.zeros_like(here)
    for direction in range(3):
        for sign in (1, -1):
            moved = unit(direction, sign)
            flux = flux + 0.5 * (offset(conduct_pad, moved) + conduct_here) * (offset(potential_pad, moved) - here)
    return here + TAU_P * flux


def cross_term(field, first, second):
    total = jnp.zeros_like(centre(field))
    for sign_first in (1, -1):
        for sign_second in (1, -1):
            offsets = [0, 0, 0]
            offsets[first] = sign_first
            offsets[second] = sign_second
            total = total + (sign_first * sign_second) * offset(field, offsets)
    return 0.25 * total


def elastic_sweep(disp_pad, interp_pad):
    updated = []
    for component in range(3):
        own = disp_pad[component]
        grad_div = offset(own, unit(component, 1)) - 2.0 * centre(own) + offset(own, unit(component, -1))
        for other in range(3):
            if other != component:
                grad_div = grad_div + cross_term(disp_pad[other], component, other)
        slope = 0.5 * (offset(interp_pad, unit(component, 1)) - offset(interp_pad, unit(component, -1)))
        force = SHEAR * laplace(own) + (LAME_FIRST + SHEAR) * grad_div - STIFF * EIGEN * slope
        updated.append(centre(own) + TAU_U * force)
    return jnp.stack(updated)


def divergence(disp_pad):
    total = jnp.zeros_like(centre(disp_pad[0]))
    for component in range(3):
        total = total + 0.5 * (offset(disp_pad[component], unit(component, 1)) - offset(disp_pad[component], unit(component, -1)))
    return total


def phase_update(phase_pad, potential, div_disp):
    phase = centre(phase_pad)
    trace = STIFF * (div_disp - 3.0 * EIGEN * interp(phase))
    over = potential - REST + OMEGA_THIRD * trace
    drive = jnp.exp(over) - jnp.exp(-over)
    change = laplace(phase_pad) - 2.0 * phase * (1.0 - phase) * (1.0 - 2.0 * phase) - RATE * interp_slope(phase) * drive
    return phase + TIME_STEP * change


def pad_cells(field, width, low, high):
    lead_dims = field.ndim - 3
    widths = [(0, 0)] * lead_dims + [(width, width), (0, 0), (0, 0)]
    values = [(0.0, 0.0)] * lead_dims + [(low, high), (0.0, 0.0), (0.0, 0.0)]
    field = jnp.pad(field, widths, constant_values=values)
    widths = [(0, 0)] * lead_dims + [(0, 0), (width, width), (width, width)]
    return jnp.pad(field, widths, mode="wrap")


def reference(labels, roughness, potential, displacement):
    mark = labels.astype(jnp.float32)
    phase = mark * (1.0 - 0.3 * roughness) + (1.0 - mark) * (0.3 * roughness)
    for step_index in range(STEPS):
        phase_pad = pad_cells(phase, 1, 1.0, 0.0)
        interp_pad = interp(phase_pad)
        conduct_pad = COND_EL + COND_LI * interp_pad
        for repeat in range(SWEEPS):
            potential = potential_sweep(pad_cells(potential, 1, 0.0, V_HIGH), conduct_pad)
        for repeat in range(SWEEPS):
            displacement = elastic_sweep(pad_cells(displacement, 1, 0.0, 0.0), interp_pad)
        div_disp = divergence(pad_cells(displacement, 1, 0.0, 0.0))
        phase = phase_update(phase_pad, potential, div_disp)
    phase_out = jnp.concatenate([phase[SHIFT:], jnp.zeros((SHIFT, NY, NZ), jnp.float32)], axis=0)
    potential_out = jnp.concatenate([potential[SHIFT:], jnp.full((SHIFT, NY, NZ), V_HIGH, jnp.float32)], axis=0)
    displacement_out = jnp.concatenate([displacement[:, SHIFT:], jnp.zeros((3, SHIFT, NY, NZ), jnp.float32)], axis=1)
    return phase_out, potential_out, displacement_out
```

```python
import jax
import jax.numpy as jnp
from jax import lax
from jax.experimental import pallas as pl
from jax.experimental.pallas import tpu as pltpu
from jax.sharding import PartitionSpec as P

STEPS = 2
SWEEPS = 3


TAU_P = 0.15
TAU_U = 0.08
SHEAR = 1.0
LAME_FIRST = 1.5
STIFF = 6.5
EIGEN = 0.1
COND_EL = 0.1
COND_LI = 0.9
V_HIGH = 1.0
TIME_STEP = 0.05
REST = 0.5
OMEGA_THIRD = 0.1
RATE = 0.5


def extended(cells, sides, width, closed):
    for axis, dim in sides:
        count = lax.axis_size(axis)
        ends = count if closed else count - 1
        head = lax.slice_in_dim(cells, 0, width, axis=dim)
        tail = lax.slice_in_dim(cells, cells.shape[dim] - width, cells.shape[dim], axis=dim)
        cells = jnp.concatenate(
            [
                lax.ppermute(tail, axis, [(i, (i + 1) % count) for i in range(ends)]),
                cells,
                lax.ppermute(head, axis, [((i + 1) % count, i) for i in range(ends)]),
            ],
            axis=dim,
        )
    return cells


def from_behind(block, axis, distance):
    devices = range(lax.axis_size(axis))
    route = [(i - distance, i) for i in devices if i - distance in devices]
    return lax.ppermute(block, axis, route)


def unit(direction, sign):
    offsets = [0, 0, 0]
    offsets[direction] = sign
    return offsets


def offset(field, offsets):
    lead_dims = field.ndim - 3
    slices = [slice(None)] * lead_dims
    for direction in range(3):
        extent = field.shape[lead_dims + direction]
        slices.append(slice(1 + offsets[direction], extent - 1 + offsets[direction]))
    return field[tuple(slices)]


def centre(field):
    return offset(field, (0, 0, 0))


def laplace(field):
    total = -6.0 * centre(field)
    for direction in range(3):
        total = total + offset(field, unit(direction, 1)) + offset(field, unit(direction, -1))
    return total


def interp(phase):
    return phase * phase * (3.0 - 2.0 * phase)


def interp_slope(phase):
    return 6.0 * phase * (1.0 - phase)


def potential_sweep(potential_pad, conduct_pad):
    here = centre(potential_pad)
    conduct_here = centre(conduct_pad)
    flux = jnp.zeros_like(here)
    for direction in range(3):
        for sign in (1, -1):
            moved = unit(direction, sign)
            flux = flux + 0.5 * (offset(conduct_pad, moved) + conduct_here) * (
                offset(potential_pad, moved) - here
            )
    return here + TAU_P * flux


def cross_term(field, first, second):
    total = jnp.zeros_like(centre(field))
    for sign_first in (1, -1):
        for sign_second in (1, -1):
            offsets = [0, 0, 0]
            offsets[first] = sign_first
            offsets[second] = sign_second
            total = total + sign_first * sign_second * offset(field, offsets)
    return 0.25 * total


def elastic_sweep(disp_pad, interp_pad):
    updated = []
    for component in range(3):
        own = disp_pad[component]
        grad_div = (
            offset(own, unit(component, 1)) - 2.0 * centre(own) + offset(own, unit(component, -1))
        )
        for other in range(3):
            if other != component:
                grad_div = grad_div + cross_term(disp_pad[other], component, other)
        slope = 0.5 * (
            offset(interp_pad, unit(component, 1)) - offset(interp_pad, unit(component, -1))
        )
        force = SHEAR * laplace(own) + (LAME_FIRST + SHEAR) * grad_div - STIFF * EIGEN * slope
        updated.append(centre(own) + TAU_U * force)
    return jnp.stack(updated)


def divergence(disp_pad):
    total = jnp.zeros_like(centre(disp_pad[0]))
    for component in range(3):
        total = total + 0.5 * (
            offset(disp_pad[component], unit(component, 1))
            - offset(disp_pad[component], unit(component, -1))
        )
    return total


def phase_update(phase_pad, potential, div_disp):
    phase = centre(phase_pad)
    trace = STIFF * (div_disp - 3.0 * EIGEN * interp(phase))
    over = potential - REST + OMEGA_THIRD * trace
    drive = jnp.exp(over) - jnp.exp(-over)
    change = (
        laplace(phase_pad)
        - 2.0 * phase * (1.0 - phase) * (1.0 - 2.0 * phase)
        - RATE * interp_slope(phase) * drive
    )
    return phase + TIME_STEP * change


def pin_ends(field, width, slab, low, high):
    if width == 0:
        return field
    lead_dims = field.ndim - 3
    planes = field.shape[lead_dims]
    first = lax.axis_index("grow") * slab - width
    position = first + lax.broadcasted_iota(jnp.int32, (planes, 1, 1), 0)
    limit = slab * lax.axis_size("grow")
    result = jnp.where(position < 0, low, field)
    return jnp.where(position >= limit, high, result)


def column_values(values):
    return jnp.array(values, jnp.float32).reshape(len(values), 1, 1, 1)


def strip(field, count):
    for repeat in range(count):
        field = centre(field)
    return field


def shards(labels, roughness, potential, displacement):
    slab = labels.shape[0]
    rim = SWEEPS + 1
    mark = labels.astype(jnp.float32)
    phase = mark * (1.0 - 0.3 * roughness) + (1.0 - mark) * (0.3 * roughness)
    low_five = column_values([1.0, 0.0, 0.0, 0.0, 0.0])
    high_five = column_values([0.0, V_HIGH, 0.0, 0.0, 0.0])
    for step_index in range(STEPS):
        packed = jnp.concatenate([phase[None], potential[None], displacement], axis=0)
        packed = extended(packed, (("grow", 1),), SWEEPS + 1, False)
        packed = pin_ends(packed, SWEEPS + 1, slab, low_five, high_five)
        packed = extended(packed, (("cy", 2), ("cz", 3)), SWEEPS + 1, True)
        phase_pad = packed[0]
        interp_pad = interp(phase_pad)
        conduct_pad = COND_EL + COND_LI * interp_pad
        pot_pad = strip(packed[1], 1)
        conduct_now = centre(conduct_pad)
        for repeat in range(SWEEPS):
            pot_pad = pin_ends(
                potential_sweep(pot_pad, conduct_now), SWEEPS - 1 - repeat, slab, 0.0, V_HIGH
            )
            if repeat + 1 < SWEEPS:
                conduct_now = centre(conduct_now)
        potential = pot_pad
        disp_pad = packed[2:]
        interp_now = interp_pad
        for repeat in range(SWEEPS):
            disp_pad = pin_ends(
                elastic_sweep(disp_pad, interp_now), SWEEPS - repeat, slab, 0.0, 0.0
            )
            if repeat + 1 < SWEEPS:
                interp_now = centre(interp_now)
        div_disp = divergence(disp_pad)
        displacement = centre(disp_pad)
        phase = phase_update(strip(phase_pad, rim - 1), potential, div_disp)
    stacked = jnp.concatenate([phase[None], potential[None], displacement], axis=0)
    arrived = from_behind(stacked, "grow", -1)
    fresh = jnp.array([0.0, V_HIGH, 0.0, 0.0, 0.0], jnp.float32).reshape(5, 1, 1, 1)
    is_last = lax.axis_index("grow") == lax.axis_size("grow") - 1
    arrived = jnp.where(is_last, fresh, arrived)
    return (arrived[0], arrived[1], arrived[2:])


REACH = STEPS * (SWEEPS + 1)
TILE = 8
LEAD = 2 * TILE
FIELDS = 5


def lanes(shape):
    return lax.broadcasted_iota(jnp.int32, shape, 1)


def from_lane(first):
    lane = lanes((TILE, LANES))
    return jnp.logical_and(lane >= first, lane < first + REACH)


LANES = 128


def turned(block, amount):
    return pltpu.roll(block, lax.rem(amount + 2 * LANES, LANES), 1)


def half_of(side):
    low = lanes((TILE, LANES)) < LANES // 2
    return jnp.logical_xor(low, side == 1)


def field_reader(phase, potential, displacement):
    def read(field, plane, row):
        rows = pl.ds(row, TILE)
        if field == 0:
            return phase[plane, rows, :]
        if field == 1:
            return potential[plane, rows, :]
        return displacement[field - 2, plane, rows, :]

    return read


def prepare_kernel(labels, roughness, potential, displacement, phase, halves, first, last):
    slab, rows, _ = labels.shape
    theirs = jnp.logical_not(half_of(lax.axis_index("grow")))
    read = field_reader(phase, potential, displacement)
    mid = rows // 2
    for plane in range(slab):
        for row in range(0, rows, TILE):
            spot = (plane, pl.ds(row, TILE), slice(None))
            mark = labels[spot].astype(jnp.float32)
            rough = 0.3 * roughness[spot]
            phase[spot] = mark * (1.0 - rough) + (1.0 - mark) * rough
    for field in range(FIELDS):
        for plane in range(slab):
            which = field * slab + plane
            for row in range(0, mid, TILE):
                upper = read(field, plane, row)
                lower = turned(read(field, plane, row + mid), LANES // 2)
                halves[pl.ds(which * mid + row, TILE), :] = jnp.where(theirs, upper, lower)
            first[pl.ds(which * TILE, TILE), :] = read(field, plane, 0)
            last[pl.ds(which * TILE, TILE), :] = read(field, plane, rows - TILE)


def strips(read, above, below, slab, rows, base, out, start):
    count = FIELDS * slab
    spare = []
    for field in range(FIELDS):
        for plane in range(slab):
            which = field * slab + plane
            packed = jnp.zeros((TILE, LANES), jnp.float32)
            for group in range(rows // TILE):
                block = turned(read(field, plane, group * TILE), group * REACH - base)
                packed = jnp.where(from_lane(group * REACH), block, packed)
            out[pl.ds(start + which * TILE, TILE), :] = packed
            spot = pl.ds(which * TILE, TILE)
            spare.append(above[spot, :])
            spare.append(below[spot, :])
    strips_of_rims(spare, base, out, start + count * TILE)


def strips_of_rims(blocks, base, out, start):
    per = LANES // REACH
    for at in range(0, len(blocks), per):
        packed = jnp.zeros((TILE, LANES), jnp.float32)
        for group, block in enumerate(blocks[at : at + per]):
            packed = jnp.where(
                from_lane(group * REACH), turned(block, group * REACH - base), packed
            )
        out[pl.ds(start + at // per * TILE, TILE), :] = packed


def rim_rows(slab):
    count = FIELDS * slab
    return (count + -(-2 * count * REACH // LANES)) * TILE


def rims_kernel(phase, potential, displacement, above, below, across, same, other):
    slab, rows, _ = phase.shape
    side = lax.axis_index("grow")
    theirs = jnp.logical_not(half_of(side))
    read = field_reader(phase, potential, displacement)
    count = FIELDS * slab
    for which in range(count):
        spot = pl.ds(which * TILE, TILE)
        across[spot, :] = jnp.where(theirs, above[spot, :], turned(below[spot, :], LANES // 2))
    inner = LANES // 2 - REACH + REACH * side
    outer = LANES - REACH
    strips(read, above, below, slab, rows, inner, across, count * TILE)
    strips(read, above, below, slab, rows, outer * (1 - side), same, 0)
    strips(read, above, below, slab, rows, outer * side, other, 0)


def conduct_of(step):
    return COND_EL + COND_LI * step


def steps_kernel(
    phase_in, potential_in, displacement_in, above, below, halves, across, same, other,
    result, message, phase, pots, disps, slopes, cond_x, cond_y, cond_z,
):
    slab, rows, _ = phase_in.shape
    planes = 2 * slab
    side = lax.axis_index("grow")
    mine = half_of(side)
    mid = rows // 2
    count = FIELDS * slab
    read = field_reader(phase_in, potential_in, displacement_in)
    groups = rows // TILE
    per = LANES // REACH
    inner = LANES // 2 - REACH * side
    outer = (LANES - REACH) * (1 - side)
    in_inner, in_outer = from_lane(inner), from_lane(outer)

    def put(field, plane, row, value):
        spot = (plane, pl.ds(LEAD + row, TILE), slice(None))
        if field == 0:
            phase[spot] = value
        elif field == 1:
            pots[(0,) + spot] = value
        else:
            disps[(0, field - 2) + spot] = value

    for field in range(FIELDS):
        for plane in range(slab):
            which = field * slab + plane
            own, far = side * slab + plane, (1 - side) * slab + plane
            spot = pl.ds(which * TILE, TILE)
            from_same, from_other = same[spot, :], other[spot, :]
            strip = across[pl.ds((count + which) * TILE, TILE), :]
            for group in range(groups):
                row = group * TILE
                near = read(field, plane, row)
                back = outer - group * REACH
                put(field, own, row, jnp.where(in_outer, turned(from_same, back), near))
                block = halves[pl.ds(which * mid + row % mid, TILE), :]
                if row >= mid:
                    block = turned(block, LANES // 2)
                block = jnp.where(in_inner, turned(strip, inner - group * REACH), block)
                put(field, far, row, jnp.where(in_outer, turned(from_other, back), block))
            rim = across[spot, :]
            for end, row in ((0, -TILE), (1, rows)):
                at, group = divmod(2 * which + end, per)
                extra = pl.ds((count + at) * TILE, TILE)
                back = outer - group * REACH
                near = (below if end else above)[spot, :]
                put(field, own, row, jnp.where(in_outer, turned(same[extra, :], back), near))
                block = turned(rim, LANES // 2) if end else rim
                strip = across[pl.ds((2 * count + at) * TILE, TILE), :]
                block = jnp.where(in_inner, turned(strip, inner - group * REACH), block)
                put(field, far, row, jnp.where(in_outer, turned(other[extra, :], back), block))

    def over_rows(body, rim=1):
        def one(block, carry):
            body(pl.multiple_of(block * TILE, TILE))
            return carry

        lax.fori_loop(LEAD // TILE - rim, (LEAD + rows) // TILE + rim, one, 0)

    def at(ref, row, shift, *lead):
        return ref[lead + (pl.ds(row + shift, TILE), slice(None))]

    def up(block):
        return pltpu.roll(block, LANES - 1, 1)

    def down(block):
        return pltpu.roll(block, 1, 1)

    def set_conduct(row):
        face = 0.5 * TAU_P
        before = conduct_of(1.0)
        for plane in range(planes):
            step = interp(at(phase, row, 0, plane))
            here = conduct_of(step)
            slopes[plane, pl.ds(row, TILE), :] = (0.5 * TAU_U * STIFF * EIGEN) * step
            cond_x[plane, pl.ds(row, TILE), :] = face * (before + here)
            cond_y[plane, pl.ds(row, TILE), :] = face * (
                here + conduct_of(interp(at(phase, row, 1, plane)))
            )
            cond_z[plane, pl.ds(row, TILE), :] = face * (here + up(here))
            before = here
        cond_x[planes, pl.ds(row, TILE), :] = face * (before + conduct_of(0.0))

    def potential_pass(old, new, low):
        def body(row):
            here = at(pots, row, 0, old, low)
            before = at(pots, row, 0, old, low - 1) if low else 0.0
            entering = at(cond_x, row, 0, low) * (here - before)
            for plane in range(low, planes):
                after = at(pots, row, 0, old, plane + 1) if plane + 1 < planes else V_HIGH
                leaving = at(cond_x, row, 0, plane + 1) * (after - here)
                along_y = at(cond_y, row, 0, plane) * (at(pots, row, 1, old, plane) - here)
                along_y -= at(cond_y, row, -1, plane) * (here - at(pots, row, -1, old, plane))
                along_z = at(cond_z, row, 0, plane) * (up(here) - here)
                along_z -= down(along_z)
                pots[new, plane, pl.ds(row, TILE), :] = here + (
                    (leaving - entering) + along_y + along_z
                )
                here, entering = after, leaving

        return body

    grad = LAME_FIRST + SHEAR
    cross = 0.25 * TAU_U * grad
    side_on = TAU_U * SHEAR
    head_on = TAU_U * (SHEAR + grad)
    keep = 1.0 - TAU_U * (6.0 * SHEAR + 2.0 * grad)

    def elastic_pass(old, new, low):
        def body(row):
            def load(plane):
                if plane < 0 or plane >= planes:
                    edge = 0.5 * TAU_U * STIFF * EIGEN if plane < 0 else 0.0
                    return (0.0, 0.0, 0.0, 0.0, -edge)
                a, b, c = (at(disps, row, 0, old, part, plane) for part in range(3))
                diff = at(disps, row, 1, old, 0, plane) - at(disps, row, -1, old, 0, plane)
                b_up, b_down = at(disps, row, 1, old, 1, plane), at(disps, row, -1, old, 1, plane)
                slope = cross * (b_up - b_down) - at(slopes, row, 0, plane)
                return (a, b, c, diff, slope)

            before, here = load(low - 1), load(low)
            for plane in range(low, planes):
                after = load(plane + 1)
                a, b, c, _, slope = here
                sum_x = [after[part] + before[part] for part in range(3)]
                ends = [
                    [at(disps, row, shift, old, part, plane) for shift in (1, -1)]
                    for part in range(3)
                ]
                sum_y = [pair[0] + pair[1] for pair in ends]
                lift = cross * (after[2] - before[2])
                mid_a = side_on * a
                new_a = (
                    keep * a
                    + head_on * sum_x[0]
                    + side_on * sum_y[0]
                    + (up(mid_a + lift) + down(mid_a - lift))
                    + (after[4] - before[4])
                )
                lift = cross * (ends[2][0] - ends[2][1])
                mid_b = side_on * b
                new_b = (
                    keep * b
                    + head_on * sum_y[1]
                    + side_on * sum_x[1]
                    + (up(mid_b + lift) + down(mid_b - lift))
                    + cross * (after[3] - before[3])
                    - (at(slopes, row, 1, plane) - at(slopes, row, -1, plane))
                )
                lift = cross * (after[0] - before[0]) + slope
                mid_c = head_on * c
                new_c = (
                    keep * c
                    + side_on * (sum_x[2] + sum_y[2])
                    + (up(mid_c + lift) + down(mid_c - lift))
                )
                spot = (plane, pl.ds(row, TILE), slice(None))
                disps[(new, 0) + spot] = new_a
                disps[(new, 1) + spot] = new_b
                disps[(new, 2) + spot] = new_c
                before, here = here, after

        return body

    def phase_pass(pot_at, disp_at, low, store):
        def body(row):
            def load(plane):
                if plane < 0 or plane >= planes:
                    return (1.0 if plane < 0 else 0.0, 0.0)
                return (at(phase, row, 0, plane), at(disps, row, 0, disp_at, 0, plane))

            before, here = load(low - 1), load(low)
            for plane in range(low, planes):
                after = load(plane + 1)
                p = here[0]
                c = at(disps, row, 0, disp_at, 2, plane)
                div = (
                    (after[1] - before[1])
                    + (at(disps, row, 1, disp_at, 1, plane) - at(disps, row, -1, disp_at, 1, plane))
                    + (up(c) - down(c))
                )
                over = (
                    (at(pots, row, 0, pot_at, plane) - REST)
                    + (0.5 * OMEGA_THIRD * STIFF) * div
                    - (OMEGA_THIRD * STIFF * 3.0 * EIGEN) * interp(p)
                )
                drive = jnp.exp(over) - jnp.exp(-over)
                lap = (
                    (before[0] + after[0])
                    + (at(phase, row, 1, plane) + at(phase, row, -1, plane))
                    + (up(p) + down(p))
                    - 6.0 * p
                )
                well = p * (1.0 - p)
                change = lap - well * (2.0 * (1.0 - 2.0 * p) + (6.0 * RATE) * drive)
                store(plane, row, p + TIME_STEP * change)
                before, here = here, after

        return body

    def store_new(plane, row, value):
        pots[2, plane, pl.ds(row, TILE), :] = value

    def store_result(plane, row, value):
        to = (plane - slab, pl.ds(pl.multiple_of(row - LEAD, TILE), TILE), slice(None))
        result[(0,) + to] = value
        result[(1,) + to] = at(pots, row, 0, 0, plane)
        for part in range(3):
            result[(2 + part,) + to] = at(disps, row, 0, 0, part, plane)

    now = 0
    for step in range(STEPS):
        last = step == STEPS - 1
        over_rows(set_conduct)
        for sweep in range(SWEEPS):
            low = max(0, slab - (SWEEPS - 1 - sweep)) if last else 0
            over_rows(potential_pass(now, 1 - now, low))
            low = max(0, slab - (SWEEPS - sweep)) if last else 0
            over_rows(elastic_pass(now, 1 - now, low))
            now = 1 - now
        if last:
            over_rows(phase_pass(now, now, slab, store_result), 0)
        else:
            over_rows(phase_pass(now, now, 0, store_new))

            def copy(row):
                for plane in range(planes):
                    phase[plane, pl.ds(row, TILE), :] = at(pots, row, 0, 2, plane)

            over_rows(copy)
    for field in range(FIELDS):
        for plane in range(slab):
            for row in range(0, mid, TILE):
                upper = result[field, plane, pl.ds(row, TILE), :]
                lower = turned(result[field, plane, pl.ds(row + mid, TILE), :], LANES // 2)
                to = pl.ds((field * slab + plane) * mid + row, TILE)
                message[to, :] = jnp.where(mine, upper, lower)


def finish_kernel(result, message, phase, potential, displacement):
    _, slab, rows, _ = result.shape
    side = lax.axis_index("grow")
    mine = half_of(side)
    fresh = side == lax.axis_size("grow") - 1
    mid = rows // 2
    for field in range(FIELDS):
        out = (phase, potential, displacement, displacement, displacement)[field]
        for plane in range(slab):
            for row in range(0, mid, TILE):
                block = message[pl.ds((field * slab + plane) * mid + row, TILE), :]
                for place, piece in ((row, block), (row + mid, turned(block, LANES // 2))):
                    spot = (plane, pl.ds(place, TILE), slice(None))
                    whole = jnp.where(mine, result[(field,) + spot], piece)
                    whole = jnp.where(fresh, V_HIGH if field == 1 else 0.0, whole)
                    out[spot if field < 2 else (field - 2,) + spot] = whole


def call(kernel, outs, scratch=(), cost=0):
    return pl.pallas_call(
        kernel,
        out_shape=[jax.ShapeDtypeStruct(shape, jnp.float32) for shape in outs],
        scratch_shapes=[pltpu.VMEM(shape, jnp.float32) for shape in scratch],
        cost_estimate=pl.CostEstimate(flops=cost, bytes_accessed=4 * cost, transcendentals=0)
        if cost
        else None,
        compiler_params=pltpu.CompilerParams(vmem_limit_bytes=48 * 1024 * 1024),
    )


def pair_shards(labels, roughness, potential, displacement):
    slab, rows, _ = labels.shape
    count = FIELDS * slab
    mid = rows // 2
    sizes = {name: lax.axis_size(name) for name in ("grow", "cy", "cz")}

    def index(grow, cy, cz):
        cy, cz = cy % sizes["cy"], cz % sizes["cz"]
        return (grow * sizes["cy"] + cy) * sizes["cz"] + cz

    everyone = [
        (grow, cy, cz)
        for grow in range(sizes["grow"])
        for cy in range(sizes["cy"])
        for cz in range(sizes["cz"])
    ]

    def send(block, route):
        pairs = [(index(*at), index(*route(*at))) for at in everyone]
        return lax.ppermute(block, ("grow", "cy", "cz"), pairs)

    phase, halves, first, last = call(
        prepare_kernel,
        [labels.shape, (count * mid, LANES), (count * TILE, LANES), (count * TILE, LANES)],
    )(labels, roughness, potential, displacement)
    halves = send(halves, lambda grow, cy, cz: (1 - grow, cy, cz))
    above = send(last, lambda grow, cy, cz: (grow, cy + 1, cz))
    below = send(first, lambda grow, cy, cz: (grow, cy - 1, cz))
    extra = rim_rows(slab)
    across, same, other = call(
        rims_kernel, [(count * TILE + extra, LANES), (extra, LANES), (extra, LANES)]
    )(phase, potential, displacement, above, below)
    across = send(across, lambda grow, cy, cz: (1 - grow, cy, cz))
    same = send(same, lambda grow, cy, cz: (grow, cy, cz - 1 if grow else cz + 1))
    other = send(other, lambda grow, cy, cz: (1 - grow, cy, cz + 1 if grow else cz - 1))
    deep = (2 * slab, rows + 2 * LEAD, LANES)
    result, message = call(
        steps_kernel,
        [(FIELDS, slab, rows, LANES), (count * mid, LANES)],
        [deep, (3,) + deep, (2, 3) + deep, deep, (2 * slab + 1,) + deep[1:], deep, deep],
    )(phase, potential, displacement, above, below, halves, across, same, other)
    message = from_behind(message, "grow", -1)
    return call(finish_kernel, [labels.shape, labels.shape, displacement.shape])(result, message)


def fits_pair(labels):
    rows, columns = labels.shape[1:]
    blocks = rows % (2 * TILE) == 0 and rows // TILE * REACH <= LANES
    return lax.axis_size("grow") == 2 and columns == LANES and REACH == TILE and blocks


def whole(labels, roughness, potential, displacement):
    plan = pair_shards if fits_pair(labels) else shards
    return tuple(plan(labels, roughness, potential, displacement))


def solution(mesh):
    placed = (
        P("grow", "cy", "cz"),
        P("grow", "cy", "cz"),
        P("grow", "cy", "cz"),
        P(None, "grow", "cy", "cz"),
    )
    return jax.shard_map(
        whole,
        mesh=mesh,
        in_specs=placed,
        out_specs=(P("grow", "cy", "cz"), P("grow", "cy", "cz"), P(None, "grow", "cy", "cz")),
        check_vma=False,
    )
```

```python
import jax
import jax.numpy as jnp
from jax import lax
from jax.experimental import pallas as pl
from jax.experimental.pallas import tpu as pltpu
from jax.sharding import PartitionSpec as P

STEPS = 2
SWEEPS = 3


TAU_P = 0.15
TAU_U = 0.08
SHEAR = 1.0
LAME_FIRST = 1.5
STIFF = 6.5
EIGEN = 0.1
COND_EL = 0.1
COND_LI = 0.9
V_HIGH = 1.0
TIME_STEP = 0.05
REST = 0.5
OMEGA_THIRD = 0.1
RATE = 0.5


def extended(cells, sides, width, closed):
    for axis, dim in sides:
        count = lax.axis_size(axis)
        ends = count if closed else count - 1
        head = lax.slice_in_dim(cells, 0, width, axis=dim)
        tail = lax.slice_in_dim(cells, cells.shape[dim] - width, cells.shape[dim], axis=dim)
        cells = jnp.concatenate(
            [
                lax.ppermute(tail, axis, [(i, (i + 1) % count) for i in range(ends)]),
                cells,
                lax.ppermute(head, axis, [((i + 1) % count, i) for i in range(ends)]),
            ],
            axis=dim,
        )
    return cells


def from_behind(block, axis, distance):
    devices = range(lax.axis_size(axis))
    route = [(i - distance, i) for i in devices if i - distance in devices]
    return lax.ppermute(block, axis, route)


def unit(direction, sign):
    offsets = [0, 0, 0]
    offsets[direction] = sign
    return offsets


def offset(field, offsets):
    lead_dims = field.ndim - 3
    slices = [slice(None)] * lead_dims
    for direction in range(3):
        extent = field.shape[lead_dims + direction]
        slices.append(slice(1 + offsets[direction], extent - 1 + offsets[direction]))
    return field[tuple(slices)]


def centre(field):
    return offset(field, (0, 0, 0))


def laplace(field):
    total = -6.0 * centre(field)
    for direction in range(3):
        total = total + offset(field, unit(direction, 1)) + offset(field, unit(direction, -1))
    return total


def interp(phase):
    return phase * phase * (3.0 - 2.0 * phase)


def interp_slope(phase):
    return 6.0 * phase * (1.0 - phase)


def potential_sweep(potential_pad, conduct_pad):
    here = centre(potential_pad)
    conduct_here = centre(conduct_pad)
    flux = jnp.zeros_like(here)
    for direction in range(3):
        for sign in (1, -1):
            moved = unit(direction, sign)
            flux = flux + 0.5 * (offset(conduct_pad, moved) + conduct_here) * (
                offset(potential_pad, moved) - here
            )
    return here + TAU_P * flux


def cross_term(field, first, second):
    total = jnp.zeros_like(centre(field))
    for sign_first in (1, -1):
        for sign_second in (1, -1):
            offsets = [0, 0, 0]
            offsets[first] = sign_first
            offsets[second] = sign_second
            total = total + sign_first * sign_second * offset(field, offsets)
    return 0.25 * total


def elastic_sweep(disp_pad, interp_pad):
    updated = []
    for component in range(3):
        own = disp_pad[component]
        grad_div = (
            offset(own, unit(component, 1)) - 2.0 * centre(own) + offset(own, unit(component, -1))
        )
        for other in range(3):
            if other != component:
                grad_div = grad_div + cross_term(disp_pad[other], component, other)
        slope = 0.5 * (
            offset(interp_pad, unit(component, 1)) - offset(interp_pad, unit(component, -1))
        )
        force = SHEAR * laplace(own) + (LAME_FIRST + SHEAR) * grad_div - STIFF * EIGEN * slope
        updated.append(centre(own) + TAU_U * force)
    return jnp.stack(updated)


def divergence(disp_pad):
    total = jnp.zeros_like(centre(disp_pad[0]))
    for component in range(3):
        total = total + 0.5 * (
            offset(disp_pad[component], unit(component, 1))
            - offset(disp_pad[component], unit(component, -1))
        )
    return total


def phase_update(phase_pad, potential, div_disp):
    phase = centre(phase_pad)
    trace = STIFF * (div_disp - 3.0 * EIGEN * interp(phase))
    over = potential - REST + OMEGA_THIRD * trace
    drive = jnp.exp(over) - jnp.exp(-over)
    change = (
        laplace(phase_pad)
        - 2.0 * phase * (1.0 - phase) * (1.0 - 2.0 * phase)
        - RATE * interp_slope(phase) * drive
    )
    return phase + TIME_STEP * change


def pin_ends(field, width, slab, low, high):
    if width == 0:
        return field
    lead_dims = field.ndim - 3
    planes = field.shape[lead_dims]
    first = lax.axis_index("grow") * slab - width
    position = first + lax.broadcasted_iota(jnp.int32, (planes, 1, 1), 0)
    limit = slab * lax.axis_size("grow")
    result = jnp.where(position < 0, low, field)
    return jnp.where(position >= limit, high, result)


def column_values(values):
    return jnp.array(values, jnp.float32).reshape(len(values), 1, 1, 1)


def strip(field, count):
    for repeat in range(count):
        field = centre(field)
    return field


def shards(labels, roughness, potential, displacement):
    slab = labels.shape[0]
    rim = SWEEPS + 1
    mark = labels.astype(jnp.float32)
    phase = mark * (1.0 - 0.3 * roughness) + (1.0 - mark) * (0.3 * roughness)
    low_five = column_values([1.0, 0.0, 0.0, 0.0, 0.0])
    high_five = column_values([0.0, V_HIGH, 0.0, 0.0, 0.0])
    for step_index in range(STEPS):
        packed = jnp.concatenate([phase[None], potential[None], displacement], axis=0)
        packed = extended(packed, (("grow", 1),), SWEEPS + 1, False)
        packed = pin_ends(packed, SWEEPS + 1, slab, low_five, high_five)
        packed = extended(packed, (("cy", 2), ("cz", 3)), SWEEPS + 1, True)
        phase_pad = packed[0]
        interp_pad = interp(phase_pad)
        conduct_pad = COND_EL + COND_LI * interp_pad
        pot_pad = strip(packed[1], 1)
        conduct_now = centre(conduct_pad)
        for repeat in range(SWEEPS):
            pot_pad = pin_ends(
                potential_sweep(pot_pad, conduct_now), SWEEPS - 1 - repeat, slab, 0.0, V_HIGH
            )
            if repeat + 1 < SWEEPS:
                conduct_now = centre(conduct_now)
        potential = pot_pad
        disp_pad = packed[2:]
        interp_now = interp_pad
        for repeat in range(SWEEPS):
            disp_pad = pin_ends(
                elastic_sweep(disp_pad, interp_now), SWEEPS - repeat, slab, 0.0, 0.0
            )
            if repeat + 1 < SWEEPS:
                interp_now = centre(interp_now)
        div_disp = divergence(disp_pad)
        displacement = centre(disp_pad)
        phase = phase_update(strip(phase_pad, rim - 1), potential, div_disp)
    stacked = jnp.concatenate([phase[None], potential[None], displacement], axis=0)
    arrived = from_behind(stacked, "grow", -1)
    fresh = jnp.array([0.0, V_HIGH, 0.0, 0.0, 0.0], jnp.float32).reshape(5, 1, 1, 1)
    is_last = lax.axis_index("grow") == lax.axis_size("grow") - 1
    arrived = jnp.where(is_last, fresh, arrived)
    return (arrived[0], arrived[1], arrived[2:])


REACH = STEPS * (SWEEPS + 1)
TILE = 8
LEAD = 2 * TILE
FIELDS = 5


def lanes(shape):
    return lax.broadcasted_iota(jnp.int32, shape, 1)


def from_lane(first):
    lane = lanes((TILE, LANES))
    return jnp.logical_and(lane >= first, lane < first + REACH)


LANES = 128


def turned(block, amount):
    return pltpu.roll(block, lax.rem(amount + 2 * LANES, LANES), 1)


def half_of(side):
    low = lanes((TILE, LANES)) < LANES // 2
    return jnp.logical_xor(low, side == 1)


def prepare_kernel(
    labels, roughness, potential, displacement, fields, halves, first, last, marks, rough, arrived
):
    _, slab, rows, _ = fields.shape
    theirs = jnp.logical_not(half_of(lax.axis_index("grow")))
    mid = rows // 2
    copies = [
        pltpu.make_async_copy(source, target, arrived.at[which])
        for which, (source, target) in enumerate(
            (
                (labels, marks),
                (roughness, rough),
                (potential, fields.at[1]),
                (displacement, fields.at[pl.ds(2, 3)]),
            )
        )
    ]
    for copy in copies:
        copy.start()
    for copy in copies[:2]:
        copy.wait()
    for plane in range(slab):
        for row in range(0, rows, TILE):
            spot = (plane, pl.ds(row, TILE), slice(None))
            mark = marks[spot].astype(jnp.float32)
            part = 0.3 * rough[spot]
            fields[(0,) + spot] = mark * (1.0 - part) + (1.0 - mark) * part
    for copy in copies[2:]:
        copy.wait()
    for field in range(FIELDS):
        for plane in range(slab):
            which = field * slab + plane
            for row in range(0, mid, TILE):
                upper = fields[field, plane, pl.ds(row, TILE), :]
                lower = turned(fields[field, plane, pl.ds(row + mid, TILE), :], LANES // 2)
                halves[pl.ds(which * mid + row, TILE), :] = jnp.where(theirs, upper, lower)
            first[pl.ds(which * TILE, TILE), :] = fields[field, plane, pl.ds(0, TILE), :]
            last[pl.ds(which * TILE, TILE), :] = fields[field, plane, pl.ds(rows - TILE, TILE), :]


def strips(fields, above, below, base, out, start):
    _, slab, rows, _ = fields.shape
    count = FIELDS * slab
    spare = []
    for field in range(FIELDS):
        for plane in range(slab):
            which = field * slab + plane
            packed = jnp.zeros((TILE, LANES), jnp.float32)
            for group in range(rows // TILE):
                block = fields[field, plane, pl.ds(group * TILE, TILE), :]
                block = turned(block, group * REACH - base)
                packed = jnp.where(from_lane(group * REACH), block, packed)
            out[pl.ds(start + which * TILE, TILE), :] = packed
            spot = pl.ds(which * TILE, TILE)
            spare.append(above[spot, :])
            spare.append(below[spot, :])
    strips_of_rims(spare, base, out, start + count * TILE)


def strips_of_rims(blocks, base, out, start):
    per = LANES // REACH
    for at in range(0, len(blocks), per):
        packed = jnp.zeros((TILE, LANES), jnp.float32)
        for group, block in enumerate(blocks[at : at + per]):
            packed = jnp.where(
                from_lane(group * REACH), turned(block, group * REACH - base), packed
            )
        out[pl.ds(start + at // per * TILE, TILE), :] = packed


def rim_rows(slab):
    count = FIELDS * slab
    return (count + -(-2 * count * REACH // LANES)) * TILE


def rims_kernel(fields, above, below, across, same, other):
    slab = fields.shape[1]
    side = lax.axis_index("grow")
    theirs = jnp.logical_not(half_of(side))
    count = FIELDS * slab
    for which in range(count):
        spot = pl.ds(which * TILE, TILE)
        across[spot, :] = jnp.where(theirs, above[spot, :], turned(below[spot, :], LANES // 2))
    inner = LANES // 2 - REACH + REACH * side
    outer = LANES - REACH
    strips(fields, above, below, inner, across, count * TILE)
    strips(fields, above, below, outer * (1 - side), same, 0)
    strips(fields, above, below, outer * side, other, 0)


def conduct_of(step):
    return COND_EL + COND_LI * step


def steps_kernel(
    fields, above, below, halves, across, same, other, result, message,
    phase, phase_new, pot, pot_new, disp, disp_new,
    slopes, slopes_y, cond_x, cond_y, cond_y_back, cond_z,
):
    _, slab, rows, _ = fields.shape
    planes = 2 * slab
    side = lax.axis_index("grow")
    mine = half_of(side)
    mid = rows // 2
    count = FIELDS * slab
    groups = rows // TILE
    per = LANES // REACH
    inner = LANES // 2 - REACH * side
    outer = (LANES - REACH) * (1 - side)
    in_inner, in_outer = from_lane(inner), from_lane(outer)

    def put(field, plane, row, value):
        spot = (plane, pl.ds(LEAD + row, TILE), slice(None))
        if field == 0:
            phase[spot] = value
        elif field == 1:
            pot[spot] = value
        else:
            disp[(field - 2,) + spot] = value

    for field in range(FIELDS):
        for plane in range(slab):
            which = field * slab + plane
            own, far = side * slab + plane, (1 - side) * slab + plane
            spot = pl.ds(which * TILE, TILE)
            from_same, from_other = same[spot, :], other[spot, :]
            strip = across[pl.ds((count + which) * TILE, TILE), :]
            for group in range(groups):
                row = group * TILE
                near = fields[field, plane, pl.ds(row, TILE), :]
                back = outer - group * REACH
                put(field, own, row, jnp.where(in_outer, turned(from_same, back), near))
                block = halves[pl.ds(which * mid + row % mid, TILE), :]
                if row >= mid:
                    block = turned(block, LANES // 2)
                block = jnp.where(in_inner, turned(strip, inner - group * REACH), block)
                put(field, far, row, jnp.where(in_outer, turned(from_other, back), block))
            rim = across[spot, :]
            for end, row in ((0, -TILE), (1, rows)):
                at, group = divmod(2 * which + end, per)
                extra = pl.ds((count + at) * TILE, TILE)
                back = outer - group * REACH
                near = (below if end else above)[spot, :]
                put(field, own, row, jnp.where(in_outer, turned(same[extra, :], back), near))
                block = turned(rim, LANES // 2) if end else rim
                strip = across[pl.ds((2 * count + at) * TILE, TILE), :]
                block = jnp.where(in_inner, turned(strip, inner - group * REACH), block)
                put(field, far, row, jnp.where(in_outer, turned(other[extra, :], back), block))

    def over_rows(body, rim=1):
        def one(block, carry):
            row = pl.multiple_of(block * TILE, TILE)
            stores = body(row)
            for ref, lead, value in stores:
                ref[lead + (pl.ds(row, TILE), slice(None))] = value
            return carry

        lax.fori_loop(LEAD // TILE - rim, (LEAD + rows) // TILE + rim, one, 0)

    def at(ref, row, shift, *lead):
        return ref[lead + (pl.ds(row + shift, TILE), slice(None))]

    def up(block):
        return pltpu.roll(block, LANES - 1, 1)

    def down(block):
        return pltpu.roll(block, 1, 1)

    push = 0.5 * TAU_U * STIFF * EIGEN

    def conduct_pass(source):
        def body(row):
            stores = []
            face = 0.5 * TAU_P
            before = conduct_of(1.0)
            for plane in range(planes):
                step, above, below = (interp(at(source, row, shift, plane)) for shift in (0, 1, -1))
                here = conduct_of(step)
                stores += [
                    (slopes, (plane,), push * step),
                    (slopes_y, (plane,), push * (above - below)),
                    (cond_x, (plane,), face * (before + here)),
                    (cond_y, (plane,), face * (here + conduct_of(above))),
                    (cond_y_back, (plane,), face * (here + conduct_of(below))),
                    (cond_z, (plane,), face * (here + up(here))),
                ]
                before = here
            return stores + [(cond_x, (planes,), face * (before + conduct_of(0.0)))]

        return body

    def potential_pass(old, new, low):
        def body(row):
            stores = []
            here = at(old, row, 0, low)
            before = at(old, row, 0, low - 1) if low else 0.0
            entering = at(cond_x, row, 0, low) * (here - before)
            for plane in range(low, planes):
                after = at(old, row, 0, plane + 1) if plane + 1 < planes else V_HIGH
                leaving = at(cond_x, row, 0, plane + 1) * (after - here)
                along_y = at(cond_y, row, 0, plane) * (at(old, row, 1, plane) - here)
                along_y -= at(cond_y_back, row, 0, plane) * (here - at(old, row, -1, plane))
                along_z = at(cond_z, row, 0, plane) * (up(here) - here)
                along_z -= down(along_z)
                value = here + ((leaving - entering) + along_y + along_z)
                stores.append((new, (plane,), value))
                here, entering = after, leaving
            return stores

        return body

    grad = LAME_FIRST + SHEAR
    cross = 0.25 * TAU_U * grad
    side_on = TAU_U * SHEAR
    head_on = TAU_U * (SHEAR + grad)
    keep = 1.0 - TAU_U * (6.0 * SHEAR + 2.0 * grad)

    def elastic_pass(old, new, low):
        def body(row):
            def load(plane):
                if plane < 0 or plane >= planes:
                    return (0.0,) * 3, (0.0,) * 3, (0.0,) * 3, -push if plane < 0 else 0.0
                parts = [at(old, row, 0, part, plane) for part in range(3)]
                ahead = [at(old, row, 1, part, plane) for part in range(3)]
                back = [at(old, row, -1, part, plane) for part in range(3)]
                sums = [one + two for one, two in zip(ahead, back)]
                diffs = [one - two for one, two in zip(ahead, back)]
                return parts, sums, diffs, cross * diffs[1] - at(slopes, row, 0, plane)

            stores = []
            before, here = load(low - 1), load(low)
            for plane in range(low, planes):
                after = load(plane + 1)
                (a, b, c), sums, diffs, slope = here
                sum_x = [one + two for one, two in zip(after[0], before[0])]
                lift = cross * (after[0][2] - before[0][2])
                mid_a = side_on * a
                new_a = (
                    keep * a
                    + head_on * sum_x[0]
                    + side_on * sums[0]
                    + (up(mid_a + lift) + down(mid_a - lift))
                    + (after[3] - before[3])
                )
                lift = cross * diffs[2]
                mid_b = side_on * b
                new_b = (
                    keep * b
                    + head_on * sums[1]
                    + side_on * sum_x[1]
                    + (up(mid_b + lift) + down(mid_b - lift))
                    + (cross * (after[2][0] - before[2][0]) - at(slopes_y, row, 0, plane))
                )
                lift = cross * (after[0][0] - before[0][0]) + slope
                mid_c = head_on * c
                new_c = (
                    keep * c
                    + side_on * (sum_x[2] + sums[2])
                    + (up(mid_c + lift) + down(mid_c - lift))
                )
                stores += [(new, (0, plane), new_a), (new, (1, plane), new_b), (new, (2, plane), new_c)]
                before, here = here, after
            return stores

        return body

    def phase_pass(source, pot_now, disp_now, low, store):
        def body(row):
            def load(plane):
                if plane < 0 or plane >= planes:
                    return (1.0 if plane < 0 else 0.0, 0.0)
                return (at(source, row, 0, plane), at(disp_now, row, 0, 0, plane))

            stores = []
            before, here = load(low - 1), load(low)
            for plane in range(low, planes):
                after = load(plane + 1)
                p = here[0]
                c = at(disp_now, row, 0, 2, plane)
                div = (
                    (after[1] - before[1])
                    + (at(disp_now, row, 1, 1, plane) - at(disp_now, row, -1, 1, plane))
                    + (up(c) - down(c))
                )
                over = (
                    (at(pot_now, row, 0, plane) - REST)
                    + (0.5 * OMEGA_THIRD * STIFF) * div
                    - (OMEGA_THIRD * STIFF * 3.0 * EIGEN) * interp(p)
                )
                drive = jnp.exp(over) - jnp.exp(-over)
                lap = (
                    (before[0] + after[0])
                    + (at(source, row, 1, plane) + at(source, row, -1, plane))
                    + (up(p) + down(p))
                    - 6.0 * p
                )
                well = p * (1.0 - p)
                change = lap - well * (2.0 * (1.0 - 2.0 * p) + (6.0 * RATE) * drive)
                stores.append((store, (plane,), p + TIME_STEP * change))
                before, here = here, after
            return stores

        return body

    for step in range(STEPS):
        last = step == STEPS - 1
        over_rows(conduct_pass(phase))
        for sweep in range(SWEEPS):
            low = max(0, slab - (SWEEPS - 1 - sweep)) if last else 0
            over_rows(potential_pass(pot, pot_new, low))
            low = max(0, slab - (SWEEPS - sweep)) if last else 0
            over_rows(elastic_pass(disp, disp_new, low))
            pot, pot_new, disp, disp_new = pot_new, pot, disp_new, disp
        over_rows(phase_pass(phase, pot, disp, slab if last else 0, phase_new), 0 if last else 1)
        phase, phase_new = phase_new, phase
    for field in range(FIELDS):
        source = (phase, pot, disp.at[0], disp.at[1], disp.at[2])[field]
        for plane in range(slab):
            for row in range(0, mid, TILE):
                upper = source[slab + plane, pl.ds(LEAD + row, TILE), :]
                lower = source[slab + plane, pl.ds(LEAD + row + mid, TILE), :]
                result[field, plane, pl.ds(row, TILE), :] = upper
                result[field, plane, pl.ds(row + mid, TILE), :] = lower
                to = pl.ds((field * slab + plane) * mid + row, TILE)
                message[to, :] = jnp.where(mine, upper, turned(lower, LANES // 2))


def finish_kernel(result, message, phase, potential, displacement):
    _, slab, rows, _ = result.shape
    side = lax.axis_index("grow")
    mine = half_of(side)
    fresh = side == lax.axis_size("grow") - 1
    mid = rows // 2
    for field in range(FIELDS):
        out = (phase, potential, displacement, displacement, displacement)[field]
        for plane in range(slab):
            for row in range(0, mid, TILE):
                block = message[pl.ds((field * slab + plane) * mid + row, TILE), :]
                for place, piece in ((row, block), (row + mid, turned(block, LANES // 2))):
                    spot = (plane, pl.ds(place, TILE), slice(None))
                    whole = jnp.where(mine, result[(field,) + spot], piece)
                    whole = jnp.where(fresh, V_HIGH if field == 1 else 0.0, whole)
                    out[spot if field < 2 else (field - 2,) + spot] = whole


def call(kernel, outs, scratch=(), **how):
    return pl.pallas_call(
        kernel,
        out_shape=[jax.ShapeDtypeStruct(shape, jnp.float32) for shape in outs],
        scratch_shapes=[
            pltpu.VMEM(one, jnp.float32) if isinstance(one, tuple) else one for one in scratch
        ],
        **how,
        compiler_params=pltpu.CompilerParams(vmem_limit_bytes=48 * 1024 * 1024),
    )


def pair_shards(labels, roughness, potential, displacement):
    slab, rows, _ = labels.shape
    count = FIELDS * slab
    mid = rows // 2
    sizes = {name: lax.axis_size(name) for name in ("grow", "cy", "cz")}

    def index(grow, cy, cz):
        cy, cz = cy % sizes["cy"], cz % sizes["cz"]
        return (grow * sizes["cy"] + cy) * sizes["cz"] + cz

    everyone = [
        (grow, cy, cz)
        for grow in range(sizes["grow"])
        for cy in range(sizes["cy"])
        for cz in range(sizes["cz"])
    ]

    def send(block, route):
        pairs = [(index(*at), index(*route(*at))) for at in everyone]
        return lax.ppermute(block, ("grow", "cy", "cz"), pairs)

    fields, halves, first, last = call(
        prepare_kernel,
        [(FIELDS,) + labels.shape, (count * mid, LANES)] + [(count * TILE, LANES)] * 2,
        [pltpu.VMEM(labels.shape, labels.dtype), labels.shape, pltpu.SemaphoreType.DMA((4,))],
        in_specs=[pl.BlockSpec(memory_space=pltpu.HBM)] * 4,
    )(labels, roughness, potential, displacement)
    halves = send(halves, lambda grow, cy, cz: (1 - grow, cy, cz))
    above = send(last, lambda grow, cy, cz: (grow, cy + 1, cz))
    below = send(first, lambda grow, cy, cz: (grow, cy - 1, cz))
    extra = rim_rows(slab)
    across, same, other = call(
        rims_kernel, [(count * TILE + extra, LANES), (extra, LANES), (extra, LANES)]
    )(fields, above, below)
    across = send(across, lambda grow, cy, cz: (1 - grow, cy, cz))
    same = send(same, lambda grow, cy, cz: (grow, cy, cz - 1 if grow else cz + 1))
    other = send(other, lambda grow, cy, cz: (1 - grow, cy, cz + 1 if grow else cz - 1))
    deep = (2 * slab, rows + 2 * LEAD, LANES)
    result, message = call(
        steps_kernel,
        [(FIELDS, slab, rows, LANES), (count * mid, LANES)],
        [deep] * 4
        + [(3,) + deep] * 2
        + [deep, deep, (2 * slab + 1,) + deep[1:], deep, deep, deep],
    )(fields, above, below, halves, across, same, other)
    message = from_behind(message, "grow", -1)
    return call(finish_kernel, [labels.shape, labels.shape, displacement.shape])(result, message)


def fits_pair(labels):
    rows, columns = labels.shape[1:]
    blocks = rows % (2 * TILE) == 0 and rows // TILE * REACH <= LANES
    return lax.axis_size("grow") == 2 and columns == LANES and REACH == TILE and blocks


def whole(labels, roughness, potential, displacement):
    plan = pair_shards if fits_pair(labels) else shards
    return tuple(plan(labels, roughness, potential, displacement))


def solution(mesh):
    placed = (
        P("grow", "cy", "cz"),
        P("grow", "cy", "cz"),
        P("grow", "cy", "cz"),
        P(None, "grow", "cy", "cz"),
    )
    return jax.shard_map(
        whole,
        mesh=mesh,
        in_specs=placed,
        out_specs=(P("grow", "cy", "cz"), P("grow", "cy", "cz"), P(None, "grow", "cy", "cz")),
        check_vma=False,
    )
```

```python
import jax
import jax.numpy as jnp
from jax import lax
from jax.experimental import pallas as pl
from jax.experimental.pallas import tpu as pltpu
from jax.sharding import PartitionSpec as P

STEPS = 2
SWEEPS = 3


TAU_P = 0.15
TAU_U = 0.08
SHEAR = 1.0
LAME_FIRST = 1.5
STIFF = 6.5
EIGEN = 0.1
COND_EL = 0.1
COND_LI = 0.9
V_HIGH = 1.0
TIME_STEP = 0.05
REST = 0.5
OMEGA_THIRD = 0.1
RATE = 0.5


def extended(cells, sides, width, closed):
    for axis, dim in sides:
        count = lax.axis_size(axis)
        ends = count if closed else count - 1
        head = lax.slice_in_dim(cells, 0, width, axis=dim)
        tail = lax.slice_in_dim(cells, cells.shape[dim] - width, cells.shape[dim], axis=dim)
        cells = jnp.concatenate(
            [
                lax.ppermute(tail, axis, [(i, (i + 1) % count) for i in range(ends)]),
                cells,
                lax.ppermute(head, axis, [((i + 1) % count, i) for i in range(ends)]),
            ],
            axis=dim,
        )
    return cells


def from_behind(block, axis, distance):
    devices = range(lax.axis_size(axis))
    route = [(i - distance, i) for i in devices if i - distance in devices]
    return lax.ppermute(block, axis, route)


def unit(direction, sign):
    offsets = [0, 0, 0]
    offsets[direction] = sign
    return offsets


def offset(field, offsets):
    lead_dims = field.ndim - 3
    slices = [slice(None)] * lead_dims
    for direction in range(3):
        extent = field.shape[lead_dims + direction]
        slices.append(slice(1 + offsets[direction], extent - 1 + offsets[direction]))
    return field[tuple(slices)]


def centre(field):
    return offset(field, (0, 0, 0))


def laplace(field):
    total = -6.0 * centre(field)
    for direction in range(3):
        total = total + offset(field, unit(direction, 1)) + offset(field, unit(direction, -1))
    return total


def interp(phase):
    return phase * phase * (3.0 - 2.0 * phase)


def interp_slope(phase):
    return 6.0 * phase * (1.0 - phase)


def potential_sweep(potential_pad, conduct_pad):
    here = centre(potential_pad)
    conduct_here = centre(conduct_pad)
    flux = jnp.zeros_like(here)
    for direction in range(3):
        for sign in (1, -1):
            moved = unit(direction, sign)
            flux = flux + 0.5 * (offset(conduct_pad, moved) + conduct_here) * (
                offset(potential_pad, moved) - here
            )
    return here + TAU_P * flux


def cross_term(field, first, second):
    total = jnp.zeros_like(centre(field))
    for sign_first in (1, -1):
        for sign_second in (1, -1):
            offsets = [0, 0, 0]
            offsets[first] = sign_first
            offsets[second] = sign_second
            total = total + sign_first * sign_second * offset(field, offsets)
    return 0.25 * total


def elastic_sweep(disp_pad, interp_pad):
    updated = []
    for component in range(3):
        own = disp_pad[component]
        grad_div = (
            offset(own, unit(component, 1)) - 2.0 * centre(own) + offset(own, unit(component, -1))
        )
        for other in range(3):
            if other != component:
                grad_div = grad_div + cross_term(disp_pad[other], component, other)
        slope = 0.5 * (
            offset(interp_pad, unit(component, 1)) - offset(interp_pad, unit(component, -1))
        )
        force = SHEAR * laplace(own) + (LAME_FIRST + SHEAR) * grad_div - STIFF * EIGEN * slope
        updated.append(centre(own) + TAU_U * force)
    return jnp.stack(updated)


def divergence(disp_pad):
    total = jnp.zeros_like(centre(disp_pad[0]))
    for component in range(3):
        total = total + 0.5 * (
            offset(disp_pad[component], unit(component, 1))
            - offset(disp_pad[component], unit(component, -1))
        )
    return total


def phase_update(phase_pad, potential, div_disp):
    phase = centre(phase_pad)
    trace = STIFF * (div_disp - 3.0 * EIGEN * interp(phase))
    over = potential - REST + OMEGA_THIRD * trace
    drive = jnp.exp(over) - jnp.exp(-over)
    change = (
        laplace(phase_pad)
        - 2.0 * phase * (1.0 - phase) * (1.0 - 2.0 * phase)
        - RATE * interp_slope(phase) * drive
    )
    return phase + TIME_STEP * change


def pin_ends(field, width, slab, low, high):
    if width == 0:
        return field
    lead_dims = field.ndim - 3
    planes = field.shape[lead_dims]
    first = lax.axis_index("grow") * slab - width
    position = first + lax.broadcasted_iota(jnp.int32, (planes, 1, 1), 0)
    limit = slab * lax.axis_size("grow")
    result = jnp.where(position < 0, low, field)
    return jnp.where(position >= limit, high, result)


def column_values(values):
    return jnp.array(values, jnp.float32).reshape(len(values), 1, 1, 1)


def strip(field, count):
    for repeat in range(count):
        field = centre(field)
    return field


def shards(labels, roughness, potential, displacement):
    slab = labels.shape[0]
    rim = SWEEPS + 1
    mark = labels.astype(jnp.float32)
    phase = mark * (1.0 - 0.3 * roughness) + (1.0 - mark) * (0.3 * roughness)
    low_five = column_values([1.0, 0.0, 0.0, 0.0, 0.0])
    high_five = column_values([0.0, V_HIGH, 0.0, 0.0, 0.0])
    for step_index in range(STEPS):
        packed = jnp.concatenate([phase[None], potential[None], displacement], axis=0)
        packed = extended(packed, (("grow", 1),), SWEEPS + 1, False)
        packed = pin_ends(packed, SWEEPS + 1, slab, low_five, high_five)
        packed = extended(packed, (("cy", 2), ("cz", 3)), SWEEPS + 1, True)
        phase_pad = packed[0]
        interp_pad = interp(phase_pad)
        conduct_pad = COND_EL + COND_LI * interp_pad
        pot_pad = strip(packed[1], 1)
        conduct_now = centre(conduct_pad)
        for repeat in range(SWEEPS):
            pot_pad = pin_ends(
                potential_sweep(pot_pad, conduct_now), SWEEPS - 1 - repeat, slab, 0.0, V_HIGH
            )
            if repeat + 1 < SWEEPS:
                conduct_now = centre(conduct_now)
        potential = pot_pad
        disp_pad = packed[2:]
        interp_now = interp_pad
        for repeat in range(SWEEPS):
            disp_pad = pin_ends(
                elastic_sweep(disp_pad, interp_now), SWEEPS - repeat, slab, 0.0, 0.0
            )
            if repeat + 1 < SWEEPS:
                interp_now = centre(interp_now)
        div_disp = divergence(disp_pad)
        displacement = centre(disp_pad)
        phase = phase_update(strip(phase_pad, rim - 1), potential, div_disp)
    stacked = jnp.concatenate([phase[None], potential[None], displacement], axis=0)
    arrived = from_behind(stacked, "grow", -1)
    fresh = jnp.array([0.0, V_HIGH, 0.0, 0.0, 0.0], jnp.float32).reshape(5, 1, 1, 1)
    is_last = lax.axis_index("grow") == lax.axis_size("grow") - 1
    arrived = jnp.where(is_last, fresh, arrived)
    return (arrived[0], arrived[1], arrived[2:])


REACH = STEPS * (SWEEPS + 1)
TILE = 8
FIELDS = 5
LAG = 2


def lanes(shape):
    return lax.broadcasted_iota(jnp.int32, shape, 1)


def from_lane(first):
    lane = lanes((TILE, LANES))
    return jnp.logical_and(lane >= first, lane < first + REACH)


LANES = 128


def turned(block, amount):
    return pltpu.roll(block, lax.rem(amount + 2 * LANES, LANES), 1)


def half_of(side):
    low = lanes((TILE, LANES)) < LANES // 2
    return jnp.logical_xor(low, side == 1)


def prepare_kernel(
    labels, roughness, potential, displacement, fields, halves, first, last, marks, rough, arrived
):
    _, slab, rows, _ = fields.shape
    theirs = jnp.logical_not(half_of(lax.axis_index("grow")))
    mid = rows // 2
    copies = [
        pltpu.make_async_copy(source, target, arrived.at[which])
        for which, (source, target) in enumerate(
            (
                (labels, marks),
                (roughness, rough),
                (potential, fields.at[1]),
                (displacement, fields.at[pl.ds(2, 3)]),
            )
        )
    ]
    for copy in copies:
        copy.start()
    for copy in copies[:2]:
        copy.wait()
    for plane in range(slab):
        for row in range(0, rows, TILE):
            spot = (plane, pl.ds(row, TILE), slice(None))
            mark = marks[spot].astype(jnp.float32)
            part = 0.3 * rough[spot]
            fields[(0,) + spot] = mark * (1.0 - part) + (1.0 - mark) * part
    for copy in copies[2:]:
        copy.wait()
    for field in range(FIELDS):
        for plane in range(slab):
            which = field * slab + plane
            for row in range(0, mid, TILE):
                upper = fields[field, plane, pl.ds(row, TILE), :]
                lower = turned(fields[field, plane, pl.ds(row + mid, TILE), :], LANES // 2)
                halves[pl.ds(which * mid + row, TILE), :] = jnp.where(theirs, upper, lower)
            first[pl.ds(which * TILE, TILE), :] = fields[field, plane, pl.ds(0, TILE), :]
            last[pl.ds(which * TILE, TILE), :] = fields[field, plane, pl.ds(rows - TILE, TILE), :]


def strips(fields, above, below, base, out, start):
    _, slab, rows, _ = fields.shape
    count = FIELDS * slab
    spare = []
    for field in range(FIELDS):
        for plane in range(slab):
            which = field * slab + plane
            packed = jnp.zeros((TILE, LANES), jnp.float32)
            for group in range(rows // TILE):
                block = fields[field, plane, pl.ds(group * TILE, TILE), :]
                block = turned(block, group * REACH - base)
                packed = jnp.where(from_lane(group * REACH), block, packed)
            out[pl.ds(start + which * TILE, TILE), :] = packed
            spot = pl.ds(which * TILE, TILE)
            spare.append(above[spot, :])
            spare.append(below[spot, :])
    strips_of_rims(spare, base, out, start + count * TILE)


def strips_of_rims(blocks, base, out, start):
    per = LANES // REACH
    for at in range(0, len(blocks), per):
        packed = jnp.zeros((TILE, LANES), jnp.float32)
        for group, block in enumerate(blocks[at : at + per]):
            packed = jnp.where(
                from_lane(group * REACH), turned(block, group * REACH - base), packed
            )
        out[pl.ds(start + at // per * TILE, TILE), :] = packed


def rim_rows(slab):
    count = FIELDS * slab
    return (count + -(-2 * count * REACH // LANES)) * TILE


def rims_kernel(fields, above, below, across, same, other):
    slab = fields.shape[1]
    side = lax.axis_index("grow")
    theirs = jnp.logical_not(half_of(side))
    count = FIELDS * slab
    for which in range(count):
        spot = pl.ds(which * TILE, TILE)
        across[spot, :] = jnp.where(theirs, above[spot, :], turned(below[spot, :], LANES // 2))
    inner = LANES // 2 - REACH + REACH * side
    outer = LANES - REACH
    strips(fields, above, below, inner, across, count * TILE)
    strips(fields, above, below, outer * (1 - side), same, 0)
    strips(fields, above, below, outer * side, other, 0)


def conduct_of(step):
    return COND_EL + COND_LI * step


def steps_kernel(
    fields, above, below, halves, across, same, other, result, message,
    natural, phase, phase_new, pot, pot_new, disp, disp_new,
    slopes, slopes_y, cond_x, cond_y, cond_y_back, cond_z,
):
    _, slab, rows, _ = fields.shape
    planes = 2 * slab
    side = lax.axis_index("grow")
    mine = half_of(side)
    mid = rows // 2
    count = FIELDS * slab
    groups = rows // TILE
    per = LANES // REACH
    inner = LANES // 2 - REACH * side
    outer = (LANES - REACH) * (1 - side)
    in_inner, in_outer = from_lane(inner), from_lane(outer)
    segment = phase.shape[1] - 2

    for field in range(FIELDS):
        for plane in range(slab):
            which = field * slab + plane
            own, far = side * slab + plane, (1 - side) * slab + plane
            spot = pl.ds(which * TILE, TILE)
            from_same, from_other = same[spot, :], other[spot, :]
            strip = across[pl.ds((count + which) * TILE, TILE), :]
            for group in range(groups):
                row = group * TILE
                to = pl.ds(REACH + row, TILE)
                near = fields[field, plane, pl.ds(row, TILE), :]
                back = outer - group * REACH
                natural[field, own, to, :] = jnp.where(in_outer, turned(from_same, back), near)
                block = halves[pl.ds(which * mid + row % mid, TILE), :]
                if row >= mid:
                    block = turned(block, LANES // 2)
                block = jnp.where(in_inner, turned(strip, inner - group * REACH), block)
                natural[field, far, to, :] = jnp.where(in_outer, turned(from_other, back), block)
            rim = across[spot, :]
            for end, to in ((0, pl.ds(0, TILE)), (1, pl.ds(REACH + rows, TILE))):
                at, group = divmod(2 * which + end, per)
                extra = pl.ds((count + at) * TILE, TILE)
                back = outer - group * REACH
                near = (below if end else above)[spot, :]
                block = jnp.where(in_outer, turned(same[extra, :], back), near)
                natural[field, own, to, :] = block
                block = turned(rim, LANES // 2) if end else rim
                strip = across[pl.ds((2 * count + at) * TILE, TILE), :]
                block = jnp.where(in_inner, turned(strip, inner - group * REACH), block)
                block = jnp.where(in_outer, turned(other[extra, :], back), block)
                natural[field, far, to, :] = block

    def parts_of(phase, pot, disp):
        return (phase, pot, disp.at[0], disp.at[1], disp.at[2])

    def close(ref):
        for plane in range(planes):
            ref[plane, 0] = pltpu.roll(ref[plane, segment], 1, 0)
            ref[plane, segment + 1] = pltpu.roll(ref[plane, 1], TILE - 1, 0)

    for field, ref in enumerate(parts_of(phase, pot, disp)):
        for plane in range(planes):
            for row in range(segment):
                ref[plane, 1 + row] = natural[field, plane, pl.ds(row, TILE, stride=segment), :]
        close(ref)

    def over_rows(*bodies):
        def one(row, carry):
            waiting = []
            running = [body(row) for body in bodies]
            while running:
                for body in list(running):
                    stores = next(body, None)
                    if stores is None:
                        running.remove(body)
                    else:
                        waiting.append(stores)
                while len(waiting) > LAG * len(bodies) or (waiting and not running):
                    for ref, lead, value in waiting.pop(0):
                        ref[lead + (row,)] = value
            return carry

        lax.fori_loop(1, segment + 1, one, 0)

    def up(block):
        return pltpu.roll(block, LANES - 1, 1)

    def down(block):
        return pltpu.roll(block, 1, 1)

    push = 0.5 * TAU_U * STIFF * EIGEN

    def conduct_pass(source):
        def body(row):
            face = 0.5 * TAU_P
            before = conduct_of(1.0)
            for plane in range(planes):
                step, ahead, back = (interp(source[plane, row + shift]) for shift in (0, 1, -1))
                here = conduct_of(step)
                yield [
                    (slopes, (plane,), push * step),
                    (slopes_y, (plane,), push * (ahead - back)),
                    (cond_x, (plane,), face * (before + here)),
                    (cond_y, (plane,), face * (here + conduct_of(ahead))),
                    (cond_y_back, (plane,), face * (here + conduct_of(back))),
                    (cond_z, (plane,), face * (here + up(here))),
                ]
                before = here
            yield [(cond_x, (planes,), face * (before + conduct_of(0.0)))]

        return body

    def potential_pass(old, new, low):
        def body(row):
            here = old[low, row]
            before = old[low - 1, row] if low else 0.0
            entering = cond_x[low, row] * (here - before)
            for plane in range(low, planes):
                after = old[plane + 1, row] if plane + 1 < planes else V_HIGH
                leaving = cond_x[plane + 1, row] * (after - here)
                along_y = cond_y[plane, row] * (old[plane, row + 1] - here)
                along_y -= cond_y_back[plane, row] * (here - old[plane, row - 1])
                along_z = cond_z[plane, row] * (up(here) - here)
                along_z -= down(along_z)
                yield [(new, (plane,), here + ((leaving - entering) + along_y + along_z))]
                here, entering = after, leaving

        return body

    grad = LAME_FIRST + SHEAR
    cross = 0.25 * TAU_U * grad
    side_on = TAU_U * SHEAR
    head_on = TAU_U * (SHEAR + grad)
    keep = 1.0 - TAU_U * (6.0 * SHEAR + 2.0 * grad)

    def elastic_pass(old, new, low):
        def body(row):
            def load(plane):
                if plane < 0 or plane >= planes:
                    return (0.0,) * 3, (0.0,) * 3, (0.0,) * 3, -push if plane < 0 else 0.0
                parts = [old[part, plane, row] for part in range(3)]
                ahead = [old[part, plane, row + 1] for part in range(3)]
                back = [old[part, plane, row - 1] for part in range(3)]
                sums = [one + two for one, two in zip(ahead, back)]
                diffs = [one - two for one, two in zip(ahead, back)]
                return parts, sums, diffs, cross * diffs[1] - slopes[plane, row]

            before, here = load(low - 1), load(low)
            for plane in range(low, planes):
                after = load(plane + 1)
                (a, b, c), sums, diffs, slope = here
                sum_x = [one + two for one, two in zip(after[0], before[0])]
                lift = cross * (after[0][2] - before[0][2])
                mid_a = side_on * a
                new_a = (
                    keep * a
                    + head_on * sum_x[0]
                    + side_on * sums[0]
                    + (up(mid_a + lift) + down(mid_a - lift))
                    + (after[3] - before[3])
                )
                lift = cross * diffs[2]
                mid_b = side_on * b
                new_b = (
                    keep * b
                    + head_on * sums[1]
                    + side_on * sum_x[1]
                    + (up(mid_b + lift) + down(mid_b - lift))
                    + (cross * (after[2][0] - before[2][0]) - slopes_y[plane, row])
                )
                lift = cross * (after[0][0] - before[0][0]) + slope
                mid_c = head_on * c
                new_c = (
                    keep * c
                    + side_on * (sum_x[2] + sums[2])
                    + (up(mid_c + lift) + down(mid_c - lift))
                )
                yield [(new, (part, plane), value) for part, value in enumerate((new_a, new_b, new_c))]
                before, here = here, after

        return body

    def phase_pass(source, pot_now, disp_now, low, new):
        def body(row):
            def load(plane):
                if plane < 0 or plane >= planes:
                    return (1.0 if plane < 0 else 0.0, 0.0)
                return (source[plane, row], disp_now[0, plane, row])

            before, here = load(low - 1), load(low)
            for plane in range(low, planes):
                after = load(plane + 1)
                p = here[0]
                c = disp_now[2, plane, row]
                div = (
                    (after[1] - before[1])
                    + (disp_now[1, plane, row + 1] - disp_now[1, plane, row - 1])
                    + (up(c) - down(c))
                )
                over = (
                    (pot_now[plane, row] - REST)
                    + (0.5 * OMEGA_THIRD * STIFF) * div
                    - (OMEGA_THIRD * STIFF * 3.0 * EIGEN) * interp(p)
                )
                drive = jnp.exp(over) - jnp.exp(-over)
                lap = (
                    (before[0] + after[0])
                    + (source[plane, row + 1] + source[plane, row - 1])
                    + (up(p) + down(p))
                    - 6.0 * p
                )
                well = p * (1.0 - p)
                change = lap - well * (2.0 * (1.0 - 2.0 * p) + (6.0 * RATE) * drive)
                yield [(new, (plane,), p + TIME_STEP * change)]
                before, here = here, after

        return body

    for step in range(STEPS):
        last = step == STEPS - 1
        over_rows(conduct_pass(phase))
        for sweep in range(SWEEPS):
            ahead = SWEEPS - 1 - sweep
            over_rows(
                potential_pass(pot, pot_new, max(0, slab - ahead) if last else 0),
                elastic_pass(disp, disp_new, max(0, slab - ahead - 1) if last else 0),
            )
            pot, pot_new, disp, disp_new = pot_new, pot, disp_new, disp
            for ref in (pot, disp.at[0], disp.at[1], disp.at[2]):
                close(ref)
        over_rows(phase_pass(phase, pot, disp, slab if last else 0, phase_new))
        phase, phase_new = phase_new, phase
        if not last:
            close(phase)
    for field, ref in enumerate(parts_of(phase, pot, disp)):
        for plane in range(slab):
            for row in range(segment):
                to = pl.ds(row, TILE, stride=segment)
                natural[field, plane, to, :] = ref[slab + plane, 1 + row]
            for row in range(0, mid, TILE):
                upper = natural[field, plane, pl.ds(REACH + row, TILE), :]
                lower = natural[field, plane, pl.ds(REACH + row + mid, TILE), :]
                result[field, plane, pl.ds(row, TILE), :] = upper
                result[field, plane, pl.ds(row + mid, TILE), :] = lower
                to = pl.ds((field * slab + plane) * mid + row, TILE)
                message[to, :] = jnp.where(mine, upper, turned(lower, LANES // 2))


def finish_kernel(result, message, phase, potential, displacement):
    _, slab, rows, _ = result.shape
    side = lax.axis_index("grow")
    mine = half_of(side)
    fresh = side == lax.axis_size("grow") - 1
    mid = rows // 2
    for field in range(FIELDS):
        out = (phase, potential, displacement, displacement, displacement)[field]
        for plane in range(slab):
            for row in range(0, mid, TILE):
                block = message[pl.ds((field * slab + plane) * mid + row, TILE), :]
                for place, piece in ((row, block), (row + mid, turned(block, LANES // 2))):
                    spot = (plane, pl.ds(place, TILE), slice(None))
                    whole = jnp.where(mine, result[(field,) + spot], piece)
                    whole = jnp.where(fresh, V_HIGH if field == 1 else 0.0, whole)
                    out[spot if field < 2 else (field - 2,) + spot] = whole


def call(kernel, outs, scratch=(), **how):
    return pl.pallas_call(
        kernel,
        out_shape=[jax.ShapeDtypeStruct(shape, jnp.float32) for shape in outs],
        scratch_shapes=[
            pltpu.VMEM(one, jnp.float32) if isinstance(one, tuple) else one for one in scratch
        ],
        **how,
        compiler_params=pltpu.CompilerParams(vmem_limit_bytes=48 * 1024 * 1024),
    )


def pair_shards(labels, roughness, potential, displacement):
    slab, rows, _ = labels.shape
    count = FIELDS * slab
    mid = rows // 2
    sizes = {name: lax.axis_size(name) for name in ("grow", "cy", "cz")}

    def index(grow, cy, cz):
        cy, cz = cy % sizes["cy"], cz % sizes["cz"]
        return (grow * sizes["cy"] + cy) * sizes["cz"] + cz

    everyone = [
        (grow, cy, cz)
        for grow in range(sizes["grow"])
        for cy in range(sizes["cy"])
        for cz in range(sizes["cz"])
    ]

    def send(block, route):
        pairs = [(index(*at), index(*route(*at))) for at in everyone]
        return lax.ppermute(block, ("grow", "cy", "cz"), pairs)

    fields, halves, first, last = call(
        prepare_kernel,
        [(FIELDS,) + labels.shape, (count * mid, LANES)] + [(count * TILE, LANES)] * 2,
        [pltpu.VMEM(labels.shape, labels.dtype), labels.shape, pltpu.SemaphoreType.DMA((4,))],
        in_specs=[pl.BlockSpec(memory_space=pltpu.HBM)] * 4,
    )(labels, roughness, potential, displacement)
    halves = send(halves, lambda grow, cy, cz: (1 - grow, cy, cz))
    above = send(last, lambda grow, cy, cz: (grow, cy + 1, cz))
    below = send(first, lambda grow, cy, cz: (grow, cy - 1, cz))
    extra = rim_rows(slab)
    across, same, other = call(
        rims_kernel, [(count * TILE + extra, LANES), (extra, LANES), (extra, LANES)]
    )(fields, above, below)
    across = send(across, lambda grow, cy, cz: (1 - grow, cy, cz))
    same = send(same, lambda grow, cy, cz: (grow, cy, cz - 1 if grow else cz + 1))
    other = send(other, lambda grow, cy, cz: (1 - grow, cy, cz + 1 if grow else cz - 1))
    span = rows + 2 * REACH
    deep = (2 * slab, span // TILE + 2, TILE, LANES)
    result, message = call(
        steps_kernel,
        [(FIELDS, slab, rows, LANES), (count * mid, LANES)],
        [(FIELDS, 2 * slab, span, LANES)]
        + [deep] * 4
        + [(3,) + deep] * 2
        + [deep, deep, (2 * slab + 1,) + deep[1:], deep, deep, deep],
    )(fields, above, below, halves, across, same, other)
    message = from_behind(message, "grow", -1)
    return call(finish_kernel, [labels.shape, labels.shape, displacement.shape])(result, message)


def fits_pair(labels):
    rows, columns = labels.shape[1:]
    blocks = rows % (2 * TILE) == 0 and rows // TILE * REACH <= LANES
    return lax.axis_size("grow") == 2 and columns == LANES and REACH == TILE and blocks


def whole(labels, roughness, potential, displacement):
    plan = pair_shards if fits_pair(labels) else shards
    return tuple(plan(labels, roughness, potential, displacement))


def solution(mesh):
    placed = (
        P("grow", "cy", "cz"),
        P("grow", "cy", "cz"),
        P("grow", "cy", "cz"),
        P(None, "grow", "cy", "cz"),
    )
    return jax.shard_map(
        whole,
        mesh=mesh,
        in_specs=placed,
        out_specs=(P("grow", "cy", "cz"), P("grow", "cy", "cz"), P(None, "grow", "cy", "cz")),
        check_vma=False,
    )
```

```python
import jax
import jax.numpy as jnp
from jax import lax
from jax.experimental import pallas as pl
from jax.experimental.pallas import tpu as pltpu
from jax.sharding import PartitionSpec as P

STEPS = 2
SWEEPS = 3


TAU_P = 0.15
TAU_U = 0.08
SHEAR = 1.0
LAME_FIRST = 1.5
STIFF = 6.5
EIGEN = 0.1
COND_EL = 0.1
COND_LI = 0.9
V_HIGH = 1.0
TIME_STEP = 0.05
REST = 0.5
OMEGA_THIRD = 0.1
RATE = 0.5


def extended(cells, sides, width, closed):
    for axis, dim in sides:
        count = lax.axis_size(axis)
        ends = count if closed else count - 1
        head = lax.slice_in_dim(cells, 0, width, axis=dim)
        tail = lax.slice_in_dim(cells, cells.shape[dim] - width, cells.shape[dim], axis=dim)
        cells = jnp.concatenate(
            [
                lax.ppermute(tail, axis, [(i, (i + 1) % count) for i in range(ends)]),
                cells,
                lax.ppermute(head, axis, [((i + 1) % count, i) for i in range(ends)]),
            ],
            axis=dim,
        )
    return cells


def from_behind(block, axis, distance):
    devices = range(lax.axis_size(axis))
    route = [(i - distance, i) for i in devices if i - distance in devices]
    return lax.ppermute(block, axis, route)


def unit(direction, sign):
    offsets = [0, 0, 0]
    offsets[direction] = sign
    return offsets


def offset(field, offsets):
    lead_dims = field.ndim - 3
    slices = [slice(None)] * lead_dims
    for direction in range(3):
        extent = field.shape[lead_dims + direction]
        slices.append(slice(1 + offsets[direction], extent - 1 + offsets[direction]))
    return field[tuple(slices)]


def centre(field):
    return offset(field, (0, 0, 0))


def laplace(field):
    total = -6.0 * centre(field)
    for direction in range(3):
        total = total + offset(field, unit(direction, 1)) + offset(field, unit(direction, -1))
    return total


def interp(phase):
    return phase * phase * (3.0 - 2.0 * phase)


def interp_slope(phase):
    return 6.0 * phase * (1.0 - phase)


def potential_sweep(potential_pad, conduct_pad):
    here = centre(potential_pad)
    conduct_here = centre(conduct_pad)
    flux = jnp.zeros_like(here)
    for direction in range(3):
        for sign in (1, -1):
            moved = unit(direction, sign)
            flux = flux + 0.5 * (offset(conduct_pad, moved) + conduct_here) * (
                offset(potential_pad, moved) - here
            )
    return here + TAU_P * flux


def cross_term(field, first, second):
    total = jnp.zeros_like(centre(field))
    for sign_first in (1, -1):
        for sign_second in (1, -1):
            offsets = [0, 0, 0]
            offsets[first] = sign_first
            offsets[second] = sign_second
            total = total + sign_first * sign_second * offset(field, offsets)
    return 0.25 * total


def elastic_sweep(disp_pad, interp_pad):
    updated = []
    for component in range(3):
        own = disp_pad[component]
        grad_div = (
            offset(own, unit(component, 1)) - 2.0 * centre(own) + offset(own, unit(component, -1))
        )
        for other in range(3):
            if other != component:
                grad_div = grad_div + cross_term(disp_pad[other], component, other)
        slope = 0.5 * (
            offset(interp_pad, unit(component, 1)) - offset(interp_pad, unit(component, -1))
        )
        force = SHEAR * laplace(own) + (LAME_FIRST + SHEAR) * grad_div - STIFF * EIGEN * slope
        updated.append(centre(own) + TAU_U * force)
    return jnp.stack(updated)


def divergence(disp_pad):
    total = jnp.zeros_like(centre(disp_pad[0]))
    for component in range(3):
        total = total + 0.5 * (
            offset(disp_pad[component], unit(component, 1))
            - offset(disp_pad[component], unit(component, -1))
        )
    return total


def phase_update(phase_pad, potential, div_disp):
    phase = centre(phase_pad)
    trace = STIFF * (div_disp - 3.0 * EIGEN * interp(phase))
    over = potential - REST + OMEGA_THIRD * trace
    drive = jnp.exp(over) - jnp.exp(-over)
    change = (
        laplace(phase_pad)
        - 2.0 * phase * (1.0 - phase) * (1.0 - 2.0 * phase)
        - RATE * interp_slope(phase) * drive
    )
    return phase + TIME_STEP * change


def pin_ends(field, width, slab, low, high):
    if width == 0:
        return field
    lead_dims = field.ndim - 3
    planes = field.shape[lead_dims]
    first = lax.axis_index("grow") * slab - width
    position = first + lax.broadcasted_iota(jnp.int32, (planes, 1, 1), 0)
    limit = slab * lax.axis_size("grow")
    result = jnp.where(position < 0, low, field)
    return jnp.where(position >= limit, high, result)


def column_values(values):
    return jnp.array(values, jnp.float32).reshape(len(values), 1, 1, 1)


def strip(field, count):
    for repeat in range(count):
        field = centre(field)
    return field


def shards(labels, roughness, potential, displacement):
    slab = labels.shape[0]
    rim = SWEEPS + 1
    mark = labels.astype(jnp.float32)
    phase = mark * (1.0 - 0.3 * roughness) + (1.0 - mark) * (0.3 * roughness)
    low_five = column_values([1.0, 0.0, 0.0, 0.0, 0.0])
    high_five = column_values([0.0, V_HIGH, 0.0, 0.0, 0.0])
    for step_index in range(STEPS):
        packed = jnp.concatenate([phase[None], potential[None], displacement], axis=0)
        packed = extended(packed, (("grow", 1),), SWEEPS + 1, False)
        packed = pin_ends(packed, SWEEPS + 1, slab, low_five, high_five)
        packed = extended(packed, (("cy", 2), ("cz", 3)), SWEEPS + 1, True)
        phase_pad = packed[0]
        interp_pad = interp(phase_pad)
        conduct_pad = COND_EL + COND_LI * interp_pad
        pot_pad = strip(packed[1], 1)
        conduct_now = centre(conduct_pad)
        for repeat in range(SWEEPS):
            pot_pad = pin_ends(
                potential_sweep(pot_pad, conduct_now), SWEEPS - 1 - repeat, slab, 0.0, V_HIGH
            )
            if repeat + 1 < SWEEPS:
                conduct_now = centre(conduct_now)
        potential = pot_pad
        disp_pad = packed[2:]
        interp_now = interp_pad
        for repeat in range(SWEEPS):
            disp_pad = pin_ends(
                elastic_sweep(disp_pad, interp_now), SWEEPS - repeat, slab, 0.0, 0.0
            )
            if repeat + 1 < SWEEPS:
                interp_now = centre(interp_now)
        div_disp = divergence(disp_pad)
        displacement = centre(disp_pad)
        phase = phase_update(strip(phase_pad, rim - 1), potential, div_disp)
    stacked = jnp.concatenate([phase[None], potential[None], displacement], axis=0)
    arrived = from_behind(stacked, "grow", -1)
    fresh = jnp.array([0.0, V_HIGH, 0.0, 0.0, 0.0], jnp.float32).reshape(5, 1, 1, 1)
    is_last = lax.axis_index("grow") == lax.axis_size("grow") - 1
    arrived = jnp.where(is_last, fresh, arrived)
    return (arrived[0], arrived[1], arrived[2:])


REACH = STEPS * (SWEEPS + 1)
TILE = 8
FIELDS = 5
LAG = 99


def lanes(shape):
    return lax.broadcasted_iota(jnp.int32, shape, 1)


def from_lane(first):
    lane = lanes((TILE, LANES))
    return jnp.logical_and(lane >= first, lane < first + REACH)


LANES = 128


def turned(block, amount):
    return pltpu.roll(block, lax.rem(amount + 2 * LANES, LANES), 1)


def half_of(side):
    low = lanes((TILE, LANES)) < LANES // 2
    return jnp.logical_xor(low, side == 1)


def prepare_kernel(
    labels, roughness, potential, displacement, fields, halves, first, last, marks, rough, arrived
):
    _, slab, rows, _ = fields.shape
    theirs = jnp.logical_not(half_of(lax.axis_index("grow")))
    mid = rows // 2
    copies = [
        pltpu.make_async_copy(source, target, arrived.at[which])
        for which, (source, target) in enumerate(
            (
                (labels, marks),
                (roughness, rough),
                (potential, fields.at[1]),
                (displacement, fields.at[pl.ds(2, 3)]),
            )
        )
    ]
    for copy in copies:
        copy.start()
    for copy in copies[:2]:
        copy.wait()
    for plane in range(slab):
        for row in range(0, rows, TILE):
            spot = (plane, pl.ds(row, TILE), slice(None))
            mark = marks[spot].astype(jnp.float32)
            part = 0.3 * rough[spot]
            fields[(0,) + spot] = mark * (1.0 - part) + (1.0 - mark) * part
    for copy in copies[2:]:
        copy.wait()
    for field in range(FIELDS):
        for plane in range(slab):
            which = field * slab + plane
            for row in range(0, mid, TILE):
                upper = fields[field, plane, pl.ds(row, TILE), :]
                lower = turned(fields[field, plane, pl.ds(row + mid, TILE), :], LANES // 2)
                halves[pl.ds(which * mid + row, TILE), :] = jnp.where(theirs, upper, lower)
            first[pl.ds(which * TILE, TILE), :] = fields[field, plane, pl.ds(0, TILE), :]
            last[pl.ds(which * TILE, TILE), :] = fields[field, plane, pl.ds(rows - TILE, TILE), :]


def strips(fields, above, below, base, out, start):
    _, slab, rows, _ = fields.shape
    count = FIELDS * slab
    spare = []
    for field in range(FIELDS):
        for plane in range(slab):
            which = field * slab + plane
            packed = jnp.zeros((TILE, LANES), jnp.float32)
            for group in range(rows // TILE):
                block = fields[field, plane, pl.ds(group * TILE, TILE), :]
                block = turned(block, group * REACH - base)
                packed = jnp.where(from_lane(group * REACH), block, packed)
            out[pl.ds(start + which * TILE, TILE), :] = packed
            spot = pl.ds(which * TILE, TILE)
            spare.append(above[spot, :])
            spare.append(below[spot, :])
    strips_of_rims(spare, base, out, start + count * TILE)


def strips_of_rims(blocks, base, out, start):
    per = LANES // REACH
    for at in range(0, len(blocks), per):
        packed = jnp.zeros((TILE, LANES), jnp.float32)
        for group, block in enumerate(blocks[at : at + per]):
            packed = jnp.where(
                from_lane(group * REACH), turned(block, group * REACH - base), packed
            )
        out[pl.ds(start + at // per * TILE, TILE), :] = packed


def rim_rows(slab):
    count = FIELDS * slab
    return (count + -(-2 * count * REACH // LANES)) * TILE


def rims_kernel(fields, above, below, across, same, other):
    slab = fields.shape[1]
    side = lax.axis_index("grow")
    theirs = jnp.logical_not(half_of(side))
    count = FIELDS * slab
    for which in range(count):
        spot = pl.ds(which * TILE, TILE)
        across[spot, :] = jnp.where(theirs, above[spot, :], turned(below[spot, :], LANES // 2))
    inner = LANES // 2 - REACH + REACH * side
    outer = LANES - REACH
    strips(fields, above, below, inner, across, count * TILE)
    strips(fields, above, below, outer * (1 - side), same, 0)
    strips(fields, above, below, outer * side, other, 0)


def conduct_of(step):
    return COND_EL + COND_LI * step


def steps_kernel(
    fields, above, below, halves, across, same, other, result, message,
    natural, phase, phase_new, pot, pot_new, disp, disp_new,
    slopes, slopes_y, cond_x, cond_y, cond_y_back, cond_z,
):
    _, slab, rows, _ = fields.shape
    planes = 2 * slab
    side = lax.axis_index("grow")
    mine = half_of(side)
    mid = rows // 2
    count = FIELDS * slab
    groups = rows // TILE
    per = LANES // REACH
    inner = LANES // 2 - REACH * side
    outer = (LANES - REACH) * (1 - side)
    in_inner, in_outer = from_lane(inner), from_lane(outer)
    segment = phase.shape[1] - 2

    for field in range(FIELDS):
        for plane in range(slab):
            which = field * slab + plane
            own, far = side * slab + plane, (1 - side) * slab + plane
            spot = pl.ds(which * TILE, TILE)
            from_same, from_other = same[spot, :], other[spot, :]
            strip = across[pl.ds((count + which) * TILE, TILE), :]
            for group in range(groups):
                row = group * TILE
                to = pl.ds(REACH + row, TILE)
                near = fields[field, plane, pl.ds(row, TILE), :]
                back = outer - group * REACH
                natural[field, own, to, :] = jnp.where(in_outer, turned(from_same, back), near)
                block = halves[pl.ds(which * mid + row % mid, TILE), :]
                if row >= mid:
                    block = turned(block, LANES // 2)
                block = jnp.where(in_inner, turned(strip, inner - group * REACH), block)
                natural[field, far, to, :] = jnp.where(in_outer, turned(from_other, back), block)
            rim = across[spot, :]
            for end, to in ((0, pl.ds(0, TILE)), (1, pl.ds(REACH + rows, TILE))):
                at, group = divmod(2 * which + end, per)
                extra = pl.ds((count + at) * TILE, TILE)
                back = outer - group * REACH
                near = (below if end else above)[spot, :]
                block = jnp.where(in_outer, turned(same[extra, :], back), near)
                natural[field, own, to, :] = block
                block = turned(rim, LANES // 2) if end else rim
                strip = across[pl.ds((2 * count + at) * TILE, TILE), :]
                block = jnp.where(in_inner, turned(strip, inner - group * REACH), block)
                block = jnp.where(in_outer, turned(other[extra, :], back), block)
                natural[field, far, to, :] = block

    def parts_of(phase, pot, disp):
        return (phase, pot, disp.at[0], disp.at[1], disp.at[2])

    def close(ref):
        for plane in range(planes):
            ref[plane, 0] = pltpu.roll(ref[plane, segment], 1, 0)
            ref[plane, segment + 1] = pltpu.roll(ref[plane, 1], TILE - 1, 0)

    for field, ref in enumerate(parts_of(phase, pot, disp)):
        for plane in range(planes):
            for row in range(segment):
                ref[plane, 1 + row] = natural[field, plane, pl.ds(row, TILE, stride=segment), :]
        close(ref)

    def over_rows(*bodies):
        def one(row, carry):
            waiting = []
            running = [body(row) for body in bodies]
            while running:
                for body in list(running):
                    stores = next(body, None)
                    if stores is None:
                        running.remove(body)
                    else:
                        waiting.append(stores)
                while len(waiting) > LAG * len(bodies) or (waiting and not running):
                    for ref, lead, value in waiting.pop(0):
                        ref[lead + (row,)] = value
            return carry

        lax.fori_loop(1, segment + 1, one, 0)

    def up(block):
        return pltpu.roll(block, LANES - 1, 1)

    def down(block):
        return pltpu.roll(block, 1, 1)

    push = 0.5 * TAU_U * STIFF * EIGEN

    def conduct_pass(source):
        def body(row):
            face = 0.5 * TAU_P
            before = conduct_of(1.0)
            for plane in range(planes):
                step, ahead, back = (interp(source[plane, row + shift]) for shift in (0, 1, -1))
                here = conduct_of(step)
                yield [
                    (slopes, (plane,), push * step),
                    (slopes_y, (plane,), push * (ahead - back)),
                    (cond_x, (plane,), face * (before + here)),
                    (cond_y, (plane,), face * (here + conduct_of(ahead))),
                    (cond_y_back, (plane,), face * (here + conduct_of(back))),
                    (cond_z, (plane,), face * (here + up(here))),
                ]
                before = here
            yield [(cond_x, (planes,), face * (before + conduct_of(0.0)))]

        return body

    def potential_pass(old, new, low):
        def body(row):
            here = old[low, row]
            before = old[low - 1, row] if low else 0.0
            entering = cond_x[low, row] * (here - before)
            for plane in range(low, planes):
                after = old[plane + 1, row] if plane + 1 < planes else V_HIGH
                leaving = cond_x[plane + 1, row] * (after - here)
                along_y = cond_y[plane, row] * (old[plane, row + 1] - here)
                along_y -= cond_y_back[plane, row] * (here - old[plane, row - 1])
                along_z = cond_z[plane, row] * (up(here) - here)
                along_z -= down(along_z)
                yield [(new, (plane,), here + ((leaving - entering) + along_y + along_z))]
                here, entering = after, leaving

        return body

    grad = LAME_FIRST + SHEAR
    cross = 0.25 * TAU_U * grad
    side_on = TAU_U * SHEAR
    head_on = TAU_U * (SHEAR + grad)
    keep = 1.0 - TAU_U * (6.0 * SHEAR + 2.0 * grad)

    def elastic_pass(old, new, low):
        def body(row):
            def load(plane):
                if plane < 0 or plane >= planes:
                    return (0.0,) * 3, (0.0,) * 3, (0.0,) * 3, -push if plane < 0 else 0.0
                parts = [old[part, plane, row] for part in range(3)]
                ahead = [old[part, plane, row + 1] for part in range(3)]
                back = [old[part, plane, row - 1] for part in range(3)]
                sums = [one + two for one, two in zip(ahead, back)]
                diffs = [one - two for one, two in zip(ahead, back)]
                return parts, sums, diffs, cross * diffs[1] - slopes[plane, row]

            before, here = load(low - 1), load(low)
            for plane in range(low, planes):
                after = load(plane + 1)
                (a, b, c), sums, diffs, slope = here
                sum_x = [one + two for one, two in zip(after[0], before[0])]
                lift = cross * (after[0][2] - before[0][2])
                mid_a = side_on * a
                new_a = (
                    keep * a
                    + head_on * sum_x[0]
                    + side_on * sums[0]
                    + (up(mid_a + lift) + down(mid_a - lift))
                    + (after[3] - before[3])
                )
                lift = cross * diffs[2]
                mid_b = side_on * b
                new_b = (
                    keep * b
                    + head_on * sums[1]
                    + side_on * sum_x[1]
                    + (up(mid_b + lift) + down(mid_b - lift))
                    + (cross * (after[2][0] - before[2][0]) - slopes_y[plane, row])
                )
                lift = cross * (after[0][0] - before[0][0]) + slope
                mid_c = head_on * c
                new_c = (
                    keep * c
                    + side_on * (sum_x[2] + sums[2])
                    + (up(mid_c + lift) + down(mid_c - lift))
                )
                yield [(new, (part, plane), value) for part, value in enumerate((new_a, new_b, new_c))]
                before, here = here, after

        return body

    def phase_pass(source, pot_now, disp_now, low, new):
        def body(row):
            def load(plane):
                if plane < 0 or plane >= planes:
                    return (1.0 if plane < 0 else 0.0, 0.0)
                return (source[plane, row], disp_now[0, plane, row])

            before, here = load(low - 1), load(low)
            for plane in range(low, planes):
                after = load(plane + 1)
                p = here[0]
                c = disp_now[2, plane, row]
                div = (
                    (after[1] - before[1])
                    + (disp_now[1, plane, row + 1] - disp_now[1, plane, row - 1])
                    + (up(c) - down(c))
                )
                over = (
                    (pot_now[plane, row] - REST)
                    + (0.5 * OMEGA_THIRD * STIFF) * div
                    - (OMEGA_THIRD * STIFF * 3.0 * EIGEN) * interp(p)
                )
                drive = jnp.exp(over) - jnp.exp(-over)
                lap = (
                    (before[0] + after[0])
                    + (source[plane, row + 1] + source[plane, row - 1])
                    + (up(p) + down(p))
                    - 6.0 * p
                )
                well = p * (1.0 - p)
                change = lap - well * (2.0 * (1.0 - 2.0 * p) + (6.0 * RATE) * drive)
                yield [(new, (plane,), p + TIME_STEP * change)]
                before, here = here, after

        return body

    for step in range(STEPS):
        last = step == STEPS - 1
        over_rows(conduct_pass(phase))
        for sweep in range(SWEEPS):
            ahead = SWEEPS - 1 - sweep
            over_rows(
                potential_pass(pot, pot_new, max(0, slab - ahead) if last else 0),
                elastic_pass(disp, disp_new, max(0, slab - ahead - 1) if last else 0),
            )
            pot, pot_new, disp, disp_new = pot_new, pot, disp_new, disp
            for ref in (pot, disp.at[0], disp.at[1], disp.at[2]):
                close(ref)
        over_rows(phase_pass(phase, pot, disp, slab if last else 0, phase_new))
        phase, phase_new = phase_new, phase
        if not last:
            close(phase)
    for field, ref in enumerate(parts_of(phase, pot, disp)):
        for plane in range(slab):
            for row in range(segment):
                to = pl.ds(row, TILE, stride=segment)
                natural[field, plane, to, :] = ref[slab + plane, 1 + row]
            for row in range(0, mid, TILE):
                upper = natural[field, plane, pl.ds(REACH + row, TILE), :]
                lower = natural[field, plane, pl.ds(REACH + row + mid, TILE), :]
                result[field, plane, pl.ds(row, TILE), :] = upper
                result[field, plane, pl.ds(row + mid, TILE), :] = lower
                to = pl.ds((field * slab + plane) * mid + row, TILE)
                message[to, :] = jnp.where(mine, upper, turned(lower, LANES // 2))


def finish_kernel(result, message, phase, potential, displacement):
    _, slab, rows, _ = result.shape
    side = lax.axis_index("grow")
    mine = half_of(side)
    fresh = side == lax.axis_size("grow") - 1
    mid = rows // 2
    for field in range(FIELDS):
        out = (phase, potential, displacement, displacement, displacement)[field]
        for plane in range(slab):
            for row in range(0, mid, TILE):
                block = message[pl.ds((field * slab + plane) * mid + row, TILE), :]
                for place, piece in ((row, block), (row + mid, turned(block, LANES // 2))):
                    spot = (plane, pl.ds(place, TILE), slice(None))
                    whole = jnp.where(mine, result[(field,) + spot], piece)
                    whole = jnp.where(fresh, V_HIGH if field == 1 else 0.0, whole)
                    out[spot if field < 2 else (field - 2,) + spot] = whole


def call(kernel, outs, scratch=(), limit=48, **how):
    return pl.pallas_call(
        kernel,
        out_shape=[jax.ShapeDtypeStruct(shape, jnp.float32) for shape in outs],
        scratch_shapes=[
            pltpu.VMEM(one, jnp.float32) if isinstance(one, tuple) else one for one in scratch
        ],
        **how,
        compiler_params=pltpu.CompilerParams(vmem_limit_bytes=limit * 1024 * 1024),
    )


def pair_shards(labels, roughness, potential, displacement):
    slab, rows, _ = labels.shape
    count = FIELDS * slab
    mid = rows // 2
    sizes = {name: lax.axis_size(name) for name in ("grow", "cy", "cz")}

    def index(grow, cy, cz):
        cy, cz = cy % sizes["cy"], cz % sizes["cz"]
        return (grow * sizes["cy"] + cy) * sizes["cz"] + cz

    everyone = [
        (grow, cy, cz)
        for grow in range(sizes["grow"])
        for cy in range(sizes["cy"])
        for cz in range(sizes["cz"])
    ]

    def send(block, route):
        pairs = [(index(*at), index(*route(*at))) for at in everyone]
        return lax.ppermute(block, ("grow", "cy", "cz"), pairs)

    fields, halves, first, last = call(
        prepare_kernel,
        [(FIELDS,) + labels.shape, (count * mid, LANES)] + [(count * TILE, LANES)] * 2,
        [pltpu.VMEM(labels.shape, labels.dtype), labels.shape, pltpu.SemaphoreType.DMA((4,))],
        limit=54,
        in_specs=[pl.BlockSpec(memory_space=pltpu.HBM)] * 4,
    )(labels, roughness, potential, displacement)
    halves = send(halves, lambda grow, cy, cz: (1 - grow, cy, cz))
    above = send(last, lambda grow, cy, cz: (grow, cy + 1, cz))
    below = send(first, lambda grow, cy, cz: (grow, cy - 1, cz))
    extra = rim_rows(slab)
    across, same, other = call(
        rims_kernel, [(count * TILE + extra, LANES), (extra, LANES), (extra, LANES)]
    )(fields, above, below)
    across = send(across, lambda grow, cy, cz: (1 - grow, cy, cz))
    same = send(same, lambda grow, cy, cz: (grow, cy, cz - 1 if grow else cz + 1))
    other = send(other, lambda grow, cy, cz: (1 - grow, cy, cz + 1 if grow else cz - 1))
    span = rows + 2 * REACH
    deep = (2 * slab, span // TILE + 2, TILE, LANES)
    result, message = call(
        steps_kernel,
        [(FIELDS, slab, rows, LANES), (count * mid, LANES)],
        [(FIELDS, 2 * slab, span, LANES)]
        + [deep] * 4
        + [(3,) + deep] * 2
        + [deep, deep, (2 * slab + 1,) + deep[1:], deep, deep, deep],
    )(fields, above, below, halves, across, same, other)
    message = from_behind(message, "grow", -1)
    return call(finish_kernel, [labels.shape, labels.shape, displacement.shape])(result, message)


def fits_pair(labels):
    rows, columns = labels.shape[1:]
    blocks = rows % (2 * TILE) == 0 and rows // TILE * REACH <= LANES
    return lax.axis_size("grow") == 2 and columns == LANES and REACH == TILE and blocks


def whole(labels, roughness, potential, displacement):
    plan = pair_shards if fits_pair(labels) else shards
    return tuple(plan(labels, roughness, potential, displacement))


def solution(mesh):
    placed = (
        P("grow", "cy", "cz"),
        P("grow", "cy", "cz"),
        P("grow", "cy", "cz"),
        P(None, "grow", "cy", "cz"),
    )
    return jax.shard_map(
        whole,
        mesh=mesh,
        in_specs=placed,
        out_specs=(P("grow", "cy", "cz"), P("grow", "cy", "cz"), P(None, "grow", "cy", "cz")),
        check_vma=False,
    )
```

```python
import jax
import jax.numpy as jnp
from jax import lax
from jax.experimental import pallas as pl
from jax.experimental.pallas import tpu as pltpu
from jax.sharding import PartitionSpec as P

STEPS = 2
SWEEPS = 3


TAU_P = 0.15
TAU_U = 0.08
SHEAR = 1.0
LAME_FIRST = 1.5
STIFF = 6.5
EIGEN = 0.1
COND_EL = 0.1
COND_LI = 0.9
V_HIGH = 1.0
TIME_STEP = 0.05
REST = 0.5
OMEGA_THIRD = 0.1
RATE = 0.5


def extended(cells, sides, width, closed):
    for axis, dim in sides:
        count = lax.axis_size(axis)
        ends = count if closed else count - 1
        head = lax.slice_in_dim(cells, 0, width, axis=dim)
        tail = lax.slice_in_dim(cells, cells.shape[dim] - width, cells.shape[dim], axis=dim)
        cells = jnp.concatenate(
            [
                lax.ppermute(tail, axis, [(i, (i + 1) % count) for i in range(ends)]),
                cells,
                lax.ppermute(head, axis, [((i + 1) % count, i) for i in range(ends)]),
            ],
            axis=dim,
        )
    return cells


def from_behind(block, axis, distance):
    devices = range(lax.axis_size(axis))
    route = [(i - distance, i) for i in devices if i - distance in devices]
    return lax.ppermute(block, axis, route)


def unit(direction, sign):
    offsets = [0, 0, 0]
    offsets[direction] = sign
    return offsets


def offset(field, offsets):
    lead_dims = field.ndim - 3
    slices = [slice(None)] * lead_dims
    for direction in range(3):
        extent = field.shape[lead_dims + direction]
        slices.append(slice(1 + offsets[direction], extent - 1 + offsets[direction]))
    return field[tuple(slices)]


def centre(field):
    return offset(field, (0, 0, 0))


def laplace(field):
    total = -6.0 * centre(field)
    for direction in range(3):
        total = total + offset(field, unit(direction, 1)) + offset(field, unit(direction, -1))
    return total


def interp(phase):
    return phase * phase * (3.0 - 2.0 * phase)


def interp_slope(phase):
    return 6.0 * phase * (1.0 - phase)


def potential_sweep(potential_pad, conduct_pad):
    here = centre(potential_pad)
    conduct_here = centre(conduct_pad)
    flux = jnp.zeros_like(here)
    for direction in range(3):
        for sign in (1, -1):
            moved = unit(direction, sign)
            flux = flux + 0.5 * (offset(conduct_pad, moved) + conduct_here) * (
                offset(potential_pad, moved) - here
            )
    return here + TAU_P * flux


def cross_term(field, first, second):
    total = jnp.zeros_like(centre(field))
    for sign_first in (1, -1):
        for sign_second in (1, -1):
            offsets = [0, 0, 0]
            offsets[first] = sign_first
            offsets[second] = sign_second
            total = total + sign_first * sign_second * offset(field, offsets)
    return 0.25 * total


def elastic_sweep(disp_pad, interp_pad):
    updated = []
    for component in range(3):
        own = disp_pad[component]
        grad_div = (
            offset(own, unit(component, 1)) - 2.0 * centre(own) + offset(own, unit(component, -1))
        )
        for other in range(3):
            if other != component:
                grad_div = grad_div + cross_term(disp_pad[other], component, other)
        slope = 0.5 * (
            offset(interp_pad, unit(component, 1)) - offset(interp_pad, unit(component, -1))
        )
        force = SHEAR * laplace(own) + (LAME_FIRST + SHEAR) * grad_div - STIFF * EIGEN * slope
        updated.append(centre(own) + TAU_U * force)
    return jnp.stack(updated)


def divergence(disp_pad):
    total = jnp.zeros_like(centre(disp_pad[0]))
    for component in range(3):
        total = total + 0.5 * (
            offset(disp_pad[component], unit(component, 1))
            - offset(disp_pad[component], unit(component, -1))
        )
    return total


def phase_update(phase_pad, potential, div_disp):
    phase = centre(phase_pad)
    trace = STIFF * (div_disp - 3.0 * EIGEN * interp(phase))
    over = potential - REST + OMEGA_THIRD * trace
    drive = jnp.exp(over) - jnp.exp(-over)
    change = (
        laplace(phase_pad)
        - 2.0 * phase * (1.0 - phase) * (1.0 - 2.0 * phase)
        - RATE * interp_slope(phase) * drive
    )
    return phase + TIME_STEP * change


def pin_ends(field, width, slab, low, high):
    if width == 0:
        return field
    lead_dims = field.ndim - 3
    planes = field.shape[lead_dims]
    first = lax.axis_index("grow") * slab - width
    position = first + lax.broadcasted_iota(jnp.int32, (planes, 1, 1), 0)
    limit = slab * lax.axis_size("grow")
    result = jnp.where(position < 0, low, field)
    return jnp.where(position >= limit, high, result)


def column_values(values):
    return jnp.array(values, jnp.float32).reshape(len(values), 1, 1, 1)


def strip(field, count):
    for repeat in range(count):
        field = centre(field)
    return field


def shards(labels, roughness, potential, displacement):
    slab = labels.shape[0]
    rim = SWEEPS + 1
    mark = labels.astype(jnp.float32)
    phase = mark * (1.0 - 0.3 * roughness) + (1.0 - mark) * (0.3 * roughness)
    low_five = column_values([1.0, 0.0, 0.0, 0.0, 0.0])
    high_five = column_values([0.0, V_HIGH, 0.0, 0.0, 0.0])
    for step_index in range(STEPS):
        packed = jnp.concatenate([phase[None], potential[None], displacement], axis=0)
        packed = extended(packed, (("grow", 1),), SWEEPS + 1, False)
        packed = pin_ends(packed, SWEEPS + 1, slab, low_five, high_five)
        packed = extended(packed, (("cy", 2), ("cz", 3)), SWEEPS + 1, True)
        phase_pad = packed[0]
        interp_pad = interp(phase_pad)
        conduct_pad = COND_EL + COND_LI * interp_pad
        pot_pad = strip(packed[1], 1)
        conduct_now = centre(conduct_pad)
        for repeat in range(SWEEPS):
            pot_pad = pin_ends(
                potential_sweep(pot_pad, conduct_now), SWEEPS - 1 - repeat, slab, 0.0, V_HIGH
            )
            if repeat + 1 < SWEEPS:
                conduct_now = centre(conduct_now)
        potential = pot_pad
        disp_pad = packed[2:]
        interp_now = interp_pad
        for repeat in range(SWEEPS):
            disp_pad = pin_ends(
                elastic_sweep(disp_pad, interp_now), SWEEPS - repeat, slab, 0.0, 0.0
            )
            if repeat + 1 < SWEEPS:
                interp_now = centre(interp_now)
        div_disp = divergence(disp_pad)
        displacement = centre(disp_pad)
        phase = phase_update(strip(phase_pad, rim - 1), potential, div_disp)
    stacked = jnp.concatenate([phase[None], potential[None], displacement], axis=0)
    arrived = from_behind(stacked, "grow", -1)
    fresh = jnp.array([0.0, V_HIGH, 0.0, 0.0, 0.0], jnp.float32).reshape(5, 1, 1, 1)
    is_last = lax.axis_index("grow") == lax.axis_size("grow") - 1
    arrived = jnp.where(is_last, fresh, arrived)
    return (arrived[0], arrived[1], arrived[2:])


REACH = STEPS * (SWEEPS + 1)
TILE = 8
FIELDS = 5
LAG = 2
TOGETHER = 6


def lanes(shape):
    return lax.broadcasted_iota(jnp.int32, shape, 1)


def from_lane(first):
    lane = lanes((TILE, LANES))
    return jnp.logical_and(lane >= first, lane < first + REACH)


LANES = 128


def turned(block, amount):
    return pltpu.roll(block, lax.rem(amount + 2 * LANES, LANES), 1)


def half_of(side):
    low = lanes((TILE, LANES)) < LANES // 2
    return jnp.logical_xor(low, side == 1)


def prepare_kernel(
    labels, roughness, potential, displacement, fields, halves, first, last, marks, rough, arrived
):
    _, slab, rows, _ = fields.shape
    theirs = jnp.logical_not(half_of(lax.axis_index("grow")))
    mid = rows // 2
    copies = [
        pltpu.make_async_copy(source, target, arrived.at[which])
        for which, (source, target) in enumerate(
            (
                (labels, marks),
                (roughness, rough),
                (potential, fields.at[1]),
                (displacement, fields.at[pl.ds(2, 3)]),
            )
        )
    ]
    for copy in copies:
        copy.start()
    for copy in copies[:2]:
        copy.wait()
    for plane in range(slab):
        for row in range(0, rows, TILE):
            spot = (plane, pl.ds(row, TILE), slice(None))
            mark = marks[spot].astype(jnp.float32)
            part = 0.3 * rough[spot]
            fields[(0,) + spot] = mark * (1.0 - part) + (1.0 - mark) * part
    for copy in copies[2:]:
        copy.wait()
    for field in range(FIELDS):
        for plane in range(slab):
            which = field * slab + plane
            for row in range(0, mid, TILE):
                upper = fields[field, plane, pl.ds(row, TILE), :]
                lower = turned(fields[field, plane, pl.ds(row + mid, TILE), :], LANES // 2)
                halves[pl.ds(which * mid + row, TILE), :] = jnp.where(theirs, upper, lower)
            first[pl.ds(which * TILE, TILE), :] = fields[field, plane, pl.ds(0, TILE), :]
            last[pl.ds(which * TILE, TILE), :] = fields[field, plane, pl.ds(rows - TILE, TILE), :]


def strips(fields, above, below, base, out, start):
    _, slab, rows, _ = fields.shape
    count = FIELDS * slab
    spare = []
    for field in range(FIELDS):
        for plane in range(slab):
            which = field * slab + plane
            packed = jnp.zeros((TILE, LANES), jnp.float32)
            for group in range(rows // TILE):
                block = fields[field, plane, pl.ds(group * TILE, TILE), :]
                block = turned(block, group * REACH - base)
                packed = jnp.where(from_lane(group * REACH), block, packed)
            out[pl.ds(start + which * TILE, TILE), :] = packed
            spot = pl.ds(which * TILE, TILE)
            spare.append(above[spot, :])
            spare.append(below[spot, :])
    strips_of_rims(spare, base, out, start + count * TILE)


def strips_of_rims(blocks, base, out, start):
    per = LANES // REACH
    for at in range(0, len(blocks), per):
        packed = jnp.zeros((TILE, LANES), jnp.float32)
        for group, block in enumerate(blocks[at : at + per]):
            packed = jnp.where(
                from_lane(group * REACH), turned(block, group * REACH - base), packed
            )
        out[pl.ds(start + at // per * TILE, TILE), :] = packed


def rim_rows(slab):
    count = FIELDS * slab
    return (count + -(-2 * count * REACH // LANES)) * TILE


def rims_kernel(fields, above, below, across, same, other):
    slab = fields.shape[1]
    side = lax.axis_index("grow")
    theirs = jnp.logical_not(half_of(side))
    count = FIELDS * slab
    for which in range(count):
        spot = pl.ds(which * TILE, TILE)
        across[spot, :] = jnp.where(theirs, above[spot, :], turned(below[spot, :], LANES // 2))
    inner = LANES // 2 - REACH + REACH * side
    outer = LANES - REACH
    strips(fields, above, below, inner, across, count * TILE)
    strips(fields, above, below, outer * (1 - side), same, 0)
    strips(fields, above, below, outer * side, other, 0)


def conduct_of(step):
    return COND_EL + COND_LI * step


def steps_kernel(
    fields, above, below, halves, across, same, other, result, message,
    natural, phase, phase_new, pot, pot_new, disp, disp_new,
    slopes, slopes_y, cond_x, cond_y, cond_y_back, cond_z,
):
    _, slab, rows, _ = fields.shape
    planes = 2 * slab
    side = lax.axis_index("grow")
    mine = half_of(side)
    mid = rows // 2
    count = FIELDS * slab
    groups = rows // TILE
    per = LANES // REACH
    inner = LANES // 2 - REACH * side
    outer = (LANES - REACH) * (1 - side)
    in_inner, in_outer = from_lane(inner), from_lane(outer)
    segment = phase.shape[1] - 2

    for field in range(FIELDS):
        for plane in range(slab):
            which = field * slab + plane
            own, far = side * slab + plane, (1 - side) * slab + plane
            spot = pl.ds(which * TILE, TILE)
            from_same, from_other = same[spot, :], other[spot, :]
            strip = across[pl.ds((count + which) * TILE, TILE), :]
            for group in range(groups):
                row = group * TILE
                to = pl.ds(REACH + row, TILE)
                near = fields[field, plane, pl.ds(row, TILE), :]
                back = outer - group * REACH
                natural[field, own, to, :] = jnp.where(in_outer, turned(from_same, back), near)
                block = halves[pl.ds(which * mid + row % mid, TILE), :]
                if row >= mid:
                    block = turned(block, LANES // 2)
                block = jnp.where(in_inner, turned(strip, inner - group * REACH), block)
                natural[field, far, to, :] = jnp.where(in_outer, turned(from_other, back), block)
            rim = across[spot, :]
            for end, to in ((0, pl.ds(0, TILE)), (1, pl.ds(REACH + rows, TILE))):
                at, group = divmod(2 * which + end, per)
                extra = pl.ds((count + at) * TILE, TILE)
                back = outer - group * REACH
                near = (below if end else above)[spot, :]
                block = jnp.where(in_outer, turned(same[extra, :], back), near)
                natural[field, own, to, :] = block
                block = turned(rim, LANES // 2) if end else rim
                strip = across[pl.ds((2 * count + at) * TILE, TILE), :]
                block = jnp.where(in_inner, turned(strip, inner - group * REACH), block)
                block = jnp.where(in_outer, turned(other[extra, :], back), block)
                natural[field, far, to, :] = block

    def parts_of(phase, pot, disp):
        return (phase, pot, disp.at[0], disp.at[1], disp.at[2])

    def close(ref):
        for plane in range(planes):
            ref[plane, 0] = pltpu.roll(ref[plane, segment], 1, 0)
            ref[plane, segment + 1] = pltpu.roll(ref[plane, 1], TILE - 1, 0)

    for field, ref in enumerate(parts_of(phase, pot, disp)):
        for plane in range(planes):
            for row in range(segment):
                ref[plane, 1 + row] = natural[field, plane, pl.ds(row, TILE, stride=segment), :]
        close(ref)

    def one_row(row, bodies):
        waiting = []
        running = [body(row) for body in bodies]
        while running:
            for body in list(running):
                stores = next(body, None)
                if stores is None:
                    running.remove(body)
                else:
                    waiting.append(stores)
            while len(waiting) > LAG * len(bodies) or (waiting and not running):
                for ref, lead, value in waiting.pop(0):
                    ref[lead + (row,)] = value

    def over_rows(*bodies):
        together = max(n for n in range(1, TOGETHER + 1) if segment % n == 0)

        def some(turn, carry):
            for more in range(together):
                one_row(1 + turn * together + more, bodies)
            return carry

        lax.fori_loop(0, segment // together, some, 0)

    def up(block):
        return pltpu.roll(block, LANES - 1, 1)

    def down(block):
        return pltpu.roll(block, 1, 1)

    push = 0.5 * TAU_U * STIFF * EIGEN

    def conduct_pass(source):
        def body(row):
            face = 0.5 * TAU_P
            before = conduct_of(1.0)
            for plane in range(planes):
                step, ahead, back = (interp(source[plane, row + shift]) for shift in (0, 1, -1))
                here = conduct_of(step)
                yield [
                    (slopes, (plane,), push * step),
                    (slopes_y, (plane,), push * (ahead - back)),
                    (cond_x, (plane,), face * (before + here)),
                    (cond_y, (plane,), face * (here + conduct_of(ahead))),
                    (cond_y_back, (plane,), face * (here + conduct_of(back))),
                    (cond_z, (plane,), face * (here + up(here))),
                ]
                before = here
            yield [(cond_x, (planes,), face * (before + conduct_of(0.0)))]

        return body

    def potential_pass(old, new, low):
        def body(row):
            here = old[low, row]
            before = old[low - 1, row] if low else 0.0
            entering = cond_x[low, row] * (here - before)
            for plane in range(low, planes):
                after = old[plane + 1, row] if plane + 1 < planes else V_HIGH
                leaving = cond_x[plane + 1, row] * (after - here)
                along_y = cond_y[plane, row] * (old[plane, row + 1] - here)
                along_y -= cond_y_back[plane, row] * (here - old[plane, row - 1])
                along_z = cond_z[plane, row] * (up(here) - here)
                along_z -= down(along_z)
                yield [(new, (plane,), here + ((leaving - entering) + along_y + along_z))]
                here, entering = after, leaving

        return body

    grad = LAME_FIRST + SHEAR
    cross = 0.25 * TAU_U * grad
    side_on = TAU_U * SHEAR
    head_on = TAU_U * (SHEAR + grad)
    keep = 1.0 - TAU_U * (6.0 * SHEAR + 2.0 * grad)

    def elastic_pass(old, new, low):
        def body(row):
            def load(plane):
                if plane < 0 or plane >= planes:
                    return (0.0,) * 3, (0.0,) * 3, (0.0,) * 3, -push if plane < 0 else 0.0
                parts = [old[part, plane, row] for part in range(3)]
                ahead = [old[part, plane, row + 1] for part in range(3)]
                back = [old[part, plane, row - 1] for part in range(3)]
                sums = [one + two for one, two in zip(ahead, back)]
                diffs = [one - two for one, two in zip(ahead, back)]
                return parts, sums, diffs, cross * diffs[1] - slopes[plane, row]

            before, here = load(low - 1), load(low)
            for plane in range(low, planes):
                after = load(plane + 1)
                (a, b, c), sums, diffs, slope = here
                sum_x = [one + two for one, two in zip(after[0], before[0])]
                lift = cross * (after[0][2] - before[0][2])
                mid_a = side_on * a
                new_a = (
                    keep * a
                    + head_on * sum_x[0]
                    + side_on * sums[0]
                    + (up(mid_a + lift) + down(mid_a - lift))
                    + (after[3] - before[3])
                )
                lift = cross * diffs[2]
                mid_b = side_on * b
                new_b = (
                    keep * b
                    + head_on * sums[1]
                    + side_on * sum_x[1]
                    + (up(mid_b + lift) + down(mid_b - lift))
                    + (cross * (after[2][0] - before[2][0]) - slopes_y[plane, row])
                )
                lift = cross * (after[0][0] - before[0][0]) + slope
                mid_c = head_on * c
                new_c = (
                    keep * c
                    + side_on * (sum_x[2] + sums[2])
                    + (up(mid_c + lift) + down(mid_c - lift))
                )
                yield [(new, (part, plane), value) for part, value in enumerate((new_a, new_b, new_c))]
                before, here = here, after

        return body

    def phase_pass(source, pot_now, disp_now, low, new):
        def body(row):
            def load(plane):
                if plane < 0 or plane >= planes:
                    return (1.0 if plane < 0 else 0.0, 0.0)
                return (source[plane, row], disp_now[0, plane, row])

            before, here = load(low - 1), load(low)
            for plane in range(low, planes):
                after = load(plane + 1)
                p = here[0]
                c = disp_now[2, plane, row]
                div = (
                    (after[1] - before[1])
                    + (disp_now[1, plane, row + 1] - disp_now[1, plane, row - 1])
                    + (up(c) - down(c))
                )
                over = (
                    (pot_now[plane, row] - REST)
                    + (0.5 * OMEGA_THIRD * STIFF) * div
                    - (OMEGA_THIRD * STIFF * 3.0 * EIGEN) * interp(p)
                )
                drive = jnp.exp(over) - jnp.exp(-over)
                lap = (
                    (before[0] + after[0])
                    + (source[plane, row + 1] + source[plane, row - 1])
                    + (up(p) + down(p))
                    - 6.0 * p
                )
                well = p * (1.0 - p)
                change = lap - well * (2.0 * (1.0 - 2.0 * p) + (6.0 * RATE) * drive)
                yield [(new, (plane,), p + TIME_STEP * change)]
                before, here = here, after

        return body

    for step in range(STEPS):
        last = step == STEPS - 1
        over_rows(conduct_pass(phase))
        for sweep in range(SWEEPS):
            ahead = SWEEPS - 1 - sweep
            over_rows(
                potential_pass(pot, pot_new, max(0, slab - ahead) if last else 0),
                elastic_pass(disp, disp_new, max(0, slab - ahead - 1) if last else 0),
            )
            pot, pot_new, disp, disp_new = pot_new, pot, disp_new, disp
            for ref in (pot, disp.at[0], disp.at[1], disp.at[2]):
                close(ref)
        over_rows(phase_pass(phase, pot, disp, slab if last else 0, phase_new))
        phase, phase_new = phase_new, phase
        if not last:
            close(phase)
    for field, ref in enumerate(parts_of(phase, pot, disp)):
        for plane in range(slab):
            for row in range(segment):
                to = pl.ds(row, TILE, stride=segment)
                natural[field, plane, to, :] = ref[slab + plane, 1 + row]
            for row in range(0, mid, TILE):
                upper = natural[field, plane, pl.ds(REACH + row, TILE), :]
                lower = natural[field, plane, pl.ds(REACH + row + mid, TILE), :]
                result[field, plane, pl.ds(row, TILE), :] = upper
                result[field, plane, pl.ds(row + mid, TILE), :] = lower
                to = pl.ds((field * slab + plane) * mid + row, TILE)
                message[to, :] = jnp.where(mine, upper, turned(lower, LANES // 2))


def finish_kernel(result, message, phase, potential, displacement):
    _, slab, rows, _ = result.shape
    side = lax.axis_index("grow")
    mine = half_of(side)
    fresh = side == lax.axis_size("grow") - 1
    mid = rows // 2
    for field in range(FIELDS):
        out = (phase, potential, displacement, displacement, displacement)[field]
        for plane in range(slab):
            for row in range(0, mid, TILE):
                block = message[pl.ds((field * slab + plane) * mid + row, TILE), :]
                for place, piece in ((row, block), (row + mid, turned(block, LANES // 2))):
                    spot = (plane, pl.ds(place, TILE), slice(None))
                    whole = jnp.where(mine, result[(field,) + spot], piece)
                    whole = jnp.where(fresh, V_HIGH if field == 1 else 0.0, whole)
                    out[spot if field < 2 else (field - 2,) + spot] = whole


def call(kernel, outs, scratch=(), limit=48, **how):
    return pl.pallas_call(
        kernel,
        out_shape=[jax.ShapeDtypeStruct(shape, jnp.float32) for shape in outs],
        scratch_shapes=[
            pltpu.VMEM(one, jnp.float32) if isinstance(one, tuple) else one for one in scratch
        ],
        **how,
        compiler_params=pltpu.CompilerParams(vmem_limit_bytes=limit * 1024 * 1024),
    )


def pair_shards(labels, roughness, potential, displacement):
    slab, rows, _ = labels.shape
    count = FIELDS * slab
    mid = rows // 2
    sizes = {name: lax.axis_size(name) for name in ("grow", "cy", "cz")}

    def index(grow, cy, cz):
        cy, cz = cy % sizes["cy"], cz % sizes["cz"]
        return (grow * sizes["cy"] + cy) * sizes["cz"] + cz

    everyone = [
        (grow, cy, cz)
        for grow in range(sizes["grow"])
        for cy in range(sizes["cy"])
        for cz in range(sizes["cz"])
    ]

    def send(block, route):
        pairs = [(index(*at), index(*route(*at))) for at in everyone]
        return lax.ppermute(block, ("grow", "cy", "cz"), pairs)

    fields, halves, first, last = call(
        prepare_kernel,
        [(FIELDS,) + labels.shape, (count * mid, LANES)] + [(count * TILE, LANES)] * 2,
        [pltpu.VMEM(labels.shape, labels.dtype), labels.shape, pltpu.SemaphoreType.DMA((4,))],
        limit=54,
        in_specs=[pl.BlockSpec(memory_space=pltpu.HBM)] * 4,
    )(labels, roughness, potential, displacement)
    halves = send(halves, lambda grow, cy, cz: (1 - grow, cy, cz))
    above = send(last, lambda grow, cy, cz: (grow, cy + 1, cz))
    below = send(first, lambda grow, cy, cz: (grow, cy - 1, cz))
    extra = rim_rows(slab)
    across, same, other = call(
        rims_kernel, [(count * TILE + extra, LANES), (extra, LANES), (extra, LANES)]
    )(fields, above, below)
    across = send(across, lambda grow, cy, cz: (1 - grow, cy, cz))
    same = send(same, lambda grow, cy, cz: (grow, cy, cz - 1 if grow else cz + 1))
    other = send(other, lambda grow, cy, cz: (1 - grow, cy, cz + 1 if grow else cz - 1))
    span = rows + 2 * REACH
    deep = (2 * slab, span // TILE + 2, TILE, LANES)
    result, message = call(
        steps_kernel,
        [(FIELDS, slab, rows, LANES), (count * mid, LANES)],
        [(FIELDS, 2 * slab, span, LANES)]
        + [deep] * 4
        + [(3,) + deep] * 2
        + [deep, deep, (2 * slab + 1,) + deep[1:], deep, deep, deep],
    )(fields, above, below, halves, across, same, other)
    message = from_behind(message, "grow", -1)
    return call(finish_kernel, [labels.shape, labels.shape, displacement.shape])(result, message)


def fits_pair(labels):
    rows, columns = labels.shape[1:]
    blocks = rows % (2 * TILE) == 0 and rows // TILE * REACH <= LANES
    return lax.axis_size("grow") == 2 and columns == LANES and REACH == TILE and blocks


def whole(labels, roughness, potential, displacement):
    plan = pair_shards if fits_pair(labels) else shards
    return tuple(plan(labels, roughness, potential, displacement))


def solution(mesh):
    placed = (
        P("grow", "cy", "cz"),
        P("grow", "cy", "cz"),
        P("grow", "cy", "cz"),
        P(None, "grow", "cy", "cz"),
    )
    return jax.shard_map(
        whole,
        mesh=mesh,
        in_specs=placed,
        out_specs=(P("grow", "cy", "cz"), P("grow", "cy", "cz"), P(None, "grow", "cy", "cz")),
        check_vma=False,
    )
```

```python
import functools

import jax
import jax.numpy as jnp
from jax import lax
from jax.experimental import pallas as pl
from jax.experimental.pallas import tpu as pltpu
from jax.sharding import PartitionSpec as P

STEPS = 2
SWEEPS = 3


TAU_P = 0.15
TAU_U = 0.08
SHEAR = 1.0
LAME_FIRST = 1.5
STIFF = 6.5
EIGEN = 0.1
COND_EL = 0.1
COND_LI = 0.9
V_HIGH = 1.0
TIME_STEP = 0.05
REST = 0.5
OMEGA_THIRD = 0.1
RATE = 0.5


def extended(cells, sides, width, closed):
    for axis, dim in sides:
        count = lax.axis_size(axis)
        ends = count if closed else count - 1
        head = lax.slice_in_dim(cells, 0, width, axis=dim)
        tail = lax.slice_in_dim(cells, cells.shape[dim] - width, cells.shape[dim], axis=dim)
        cells = jnp.concatenate(
            [
                lax.ppermute(tail, axis, [(i, (i + 1) % count) for i in range(ends)]),
                cells,
                lax.ppermute(head, axis, [((i + 1) % count, i) for i in range(ends)]),
            ],
            axis=dim,
        )
    return cells


def from_behind(block, axis, distance):
    devices = range(lax.axis_size(axis))
    route = [(i - distance, i) for i in devices if i - distance in devices]
    return lax.ppermute(block, axis, route)


def unit(direction, sign):
    offsets = [0, 0, 0]
    offsets[direction] = sign
    return offsets


def offset(field, offsets):
    lead_dims = field.ndim - 3
    slices = [slice(None)] * lead_dims
    for direction in range(3):
        extent = field.shape[lead_dims + direction]
        slices.append(slice(1 + offsets[direction], extent - 1 + offsets[direction]))
    return field[tuple(slices)]


def centre(field):
    return offset(field, (0, 0, 0))


def laplace(field):
    total = -6.0 * centre(field)
    for direction in range(3):
        total = total + offset(field, unit(direction, 1)) + offset(field, unit(direction, -1))
    return total


def interp(phase):
    return phase * phase * (3.0 - 2.0 * phase)


def interp_slope(phase):
    return 6.0 * phase * (1.0 - phase)


def potential_sweep(potential_pad, conduct_pad):
    here = centre(potential_pad)
    conduct_here = centre(conduct_pad)
    flux = jnp.zeros_like(here)
    for direction in range(3):
        for sign in (1, -1):
            moved = unit(direction, sign)
            flux = flux + 0.5 * (offset(conduct_pad, moved) + conduct_here) * (
                offset(potential_pad, moved) - here
            )
    return here + TAU_P * flux


def cross_term(field, first, second):
    total = jnp.zeros_like(centre(field))
    for sign_first in (1, -1):
        for sign_second in (1, -1):
            offsets = [0, 0, 0]
            offsets[first] = sign_first
            offsets[second] = sign_second
            total = total + sign_first * sign_second * offset(field, offsets)
    return 0.25 * total


def elastic_sweep(disp_pad, interp_pad):
    updated = []
    for component in range(3):
        own = disp_pad[component]
        grad_div = (
            offset(own, unit(component, 1)) - 2.0 * centre(own) + offset(own, unit(component, -1))
        )
        for other in range(3):
            if other != component:
                grad_div = grad_div + cross_term(disp_pad[other], component, other)
        slope = 0.5 * (
            offset(interp_pad, unit(component, 1)) - offset(interp_pad, unit(component, -1))
        )
        force = SHEAR * laplace(own) + (LAME_FIRST + SHEAR) * grad_div - STIFF * EIGEN * slope
        updated.append(centre(own) + TAU_U * force)
    return jnp.stack(updated)


def divergence(disp_pad):
    total = jnp.zeros_like(centre(disp_pad[0]))
    for component in range(3):
        total = total + 0.5 * (
            offset(disp_pad[component], unit(component, 1))
            - offset(disp_pad[component], unit(component, -1))
        )
    return total


def phase_update(phase_pad, potential, div_disp):
    phase = centre(phase_pad)
    trace = STIFF * (div_disp - 3.0 * EIGEN * interp(phase))
    over = potential - REST + OMEGA_THIRD * trace
    drive = jnp.exp(over) - jnp.exp(-over)
    change = (
        laplace(phase_pad)
        - 2.0 * phase * (1.0 - phase) * (1.0 - 2.0 * phase)
        - RATE * interp_slope(phase) * drive
    )
    return phase + TIME_STEP * change


def pin_ends(field, width, slab, low, high):
    if width == 0:
        return field
    lead_dims = field.ndim - 3
    planes = field.shape[lead_dims]
    first = lax.axis_index("grow") * slab - width
    position = first + lax.broadcasted_iota(jnp.int32, (planes, 1, 1), 0)
    limit = slab * lax.axis_size("grow")
    result = jnp.where(position < 0, low, field)
    return jnp.where(position >= limit, high, result)


def column_values(values):
    return jnp.array(values, jnp.float32).reshape(len(values), 1, 1, 1)


def strip(field, count):
    for repeat in range(count):
        field = centre(field)
    return field


def shards(labels, roughness, potential, displacement):
    slab = labels.shape[0]
    rim = SWEEPS + 1
    mark = labels.astype(jnp.float32)
    phase = mark * (1.0 - 0.3 * roughness) + (1.0 - mark) * (0.3 * roughness)
    low_five = column_values([1.0, 0.0, 0.0, 0.0, 0.0])
    high_five = column_values([0.0, V_HIGH, 0.0, 0.0, 0.0])
    for step_index in range(STEPS):
        packed = jnp.concatenate([phase[None], potential[None], displacement], axis=0)
        packed = extended(packed, (("grow", 1),), SWEEPS + 1, False)
        packed = pin_ends(packed, SWEEPS + 1, slab, low_five, high_five)
        packed = extended(packed, (("cy", 2), ("cz", 3)), SWEEPS + 1, True)
        phase_pad = packed[0]
        interp_pad = interp(phase_pad)
        conduct_pad = COND_EL + COND_LI * interp_pad
        pot_pad = strip(packed[1], 1)
        conduct_now = centre(conduct_pad)
        for repeat in range(SWEEPS):
            pot_pad = pin_ends(
                potential_sweep(pot_pad, conduct_now), SWEEPS - 1 - repeat, slab, 0.0, V_HIGH
            )
            if repeat + 1 < SWEEPS:
                conduct_now = centre(conduct_now)
        potential = pot_pad
        disp_pad = packed[2:]
        interp_now = interp_pad
        for repeat in range(SWEEPS):
            disp_pad = pin_ends(
                elastic_sweep(disp_pad, interp_now), SWEEPS - repeat, slab, 0.0, 0.0
            )
            if repeat + 1 < SWEEPS:
                interp_now = centre(interp_now)
        div_disp = divergence(disp_pad)
        displacement = centre(disp_pad)
        phase = phase_update(strip(phase_pad, rim - 1), potential, div_disp)
    stacked = jnp.concatenate([phase[None], potential[None], displacement], axis=0)
    arrived = from_behind(stacked, "grow", -1)
    fresh = jnp.array([0.0, V_HIGH, 0.0, 0.0, 0.0], jnp.float32).reshape(5, 1, 1, 1)
    is_last = lax.axis_index("grow") == lax.axis_size("grow") - 1
    arrived = jnp.where(is_last, fresh, arrived)
    return (arrived[0], arrived[1], arrived[2:])


REACH = STEPS * (SWEEPS + 1)
TILE = 8
FIELDS = 5
LAG = 2
TOGETHER = 10


def lanes(shape):
    return lax.broadcasted_iota(jnp.int32, shape, 1)


def from_lane(first):
    lane = lanes((TILE, LANES))
    return jnp.logical_and(lane >= first, lane < first + REACH)


LANES = 128


def turned(block, amount):
    return pltpu.roll(block, lax.rem(amount + 2 * LANES, LANES), 1)


def half_of(side):
    low = lanes((TILE, LANES)) < LANES // 2
    return jnp.logical_xor(low, side == 1)


def pack_halves(fields, start, theirs, out):
    _, slab, _, _ = fields.shape
    mid = out.shape[0] // (FIELDS * slab)
    for field in range(FIELDS):
        for plane in range(slab):
            for row in range(0, mid, TILE):
                upper = fields[field, plane, pl.ds(start + row, TILE), :]
                lower = fields[field, plane, pl.ds(start + mid + row, TILE), :]
                to = pl.ds((field * slab + plane) * mid + row, TILE)
                out[to, :] = jnp.where(theirs, upper, turned(lower, LANES // 2))


def prepare_kernel(
    labels, roughness, potential, displacement, fields, halves, first, last, marks, rough, arrived
):
    _, slab, rows, _ = fields.shape
    theirs = jnp.logical_not(half_of(lax.axis_index("grow")))
    copies = [
        pltpu.make_async_copy(source, target, arrived.at[which])
        for which, (source, target) in enumerate(
            (
                (labels, marks),
                (roughness, rough),
                (potential, fields.at[1]),
                (displacement, fields.at[pl.ds(2, 3)]),
            )
        )
    ]
    for copy in copies:
        copy.start()
    for copy in copies[:2]:
        copy.wait()
    for plane in range(slab):
        for row in range(0, rows, TILE):
            spot = (plane, pl.ds(row, TILE), slice(None))
            mark = marks[spot].astype(jnp.float32)
            part = 0.3 * rough[spot]
            fields[(0,) + spot] = mark * (1.0 - part) + (1.0 - mark) * part
    for copy in copies[2:]:
        copy.wait()
    pack_halves(fields, 0, theirs, halves)
    for field in range(FIELDS):
        for plane in range(slab):
            which = field * slab + plane
            first[pl.ds(which * TILE, TILE), :] = fields[field, plane, pl.ds(0, TILE), :]
            last[pl.ds(which * TILE, TILE), :] = fields[field, plane, pl.ds(rows - TILE, TILE), :]


def strips(fields, above, below, base, out, start):
    _, slab, rows, _ = fields.shape
    count = FIELDS * slab
    spare = []
    for field in range(FIELDS):
        for plane in range(slab):
            which = field * slab + plane
            packed = jnp.zeros((TILE, LANES), jnp.float32)
            for group in range(rows // TILE):
                block = fields[field, plane, pl.ds(group * TILE, TILE), :]
                block = turned(block, group * REACH - base)
                packed = jnp.where(from_lane(group * REACH), block, packed)
            out[pl.ds(start + which * TILE, TILE), :] = packed
            spot = pl.ds(which * TILE, TILE)
            spare.append(above[spot, :])
            spare.append(below[spot, :])
    strips_of_rims(spare, base, out, start + count * TILE)


def strips_of_rims(blocks, base, out, start):
    per = LANES // REACH
    for at in range(0, len(blocks), per):
        packed = jnp.zeros((TILE, LANES), jnp.float32)
        for group, block in enumerate(blocks[at : at + per]):
            packed = jnp.where(
                from_lane(group * REACH), turned(block, group * REACH - base), packed
            )
        out[pl.ds(start + at // per * TILE, TILE), :] = packed


def rim_rows(slab):
    count = FIELDS * slab
    return (count + -(-2 * count * REACH // LANES)) * TILE


def rims_kernel(fields, above, below, across, same, other):
    slab = fields.shape[1]
    side = lax.axis_index("grow")
    theirs = jnp.logical_not(half_of(side))
    count = FIELDS * slab
    for which in range(count):
        spot = pl.ds(which * TILE, TILE)
        across[spot, :] = jnp.where(theirs, above[spot, :], turned(below[spot, :], LANES // 2))
    inner = LANES // 2 - REACH + REACH * side
    outer = LANES - REACH
    strips(fields, above, below, inner, across, count * TILE)
    strips(fields, above, below, outer * (1 - side), same, 0)
    strips(fields, above, below, outer * side, other, 0)


def rest_kernel(fields, across, other, early, near_a, near_b, rest):
    pack_halves(
        fields,
        fields.shape[2] - 2 * (rest.shape[0] // (FIELDS * fields.shape[1])),
        jnp.logical_not(half_of(lax.axis_index("grow"))),
        rest,
    )


def own_kernel(fields, above, below, same, part_a, part_b, natural):
    _, slab, rows, _ = fields.shape
    side = lax.axis_index("grow")
    count = FIELDS * slab
    per = LANES // REACH
    outer = (LANES - REACH) * (1 - side)
    in_outer = from_lane(outer)
    segment = part_a.shape[2] - 2
    for field in range(FIELDS):
        for plane in range(slab):
            which = field * slab + plane
            spot = pl.ds(which * TILE, TILE)
            for at in range(0, rows + 2 * REACH, TILE):
                row = at - REACH
                if 0 <= row < rows:
                    near = fields[field, plane, pl.ds(row, TILE), :]
                    piece, group = same[spot, :], row // TILE
                else:
                    end = int(row > 0)
                    near = (below if end else above)[spot, :]
                    extra, group = divmod(2 * which + end, per)
                    piece = same[pl.ds((count + extra) * TILE, TILE), :]
                piece = turned(piece, outer - group * REACH)
                natural[which, pl.ds(at, TILE), :] = jnp.where(in_outer, piece, near)
            for start, part in ((0, part_a), (rows // 2, part_b)):
                blocks = [
                    natural[which, pl.ds(start + row, TILE, stride=segment), :]
                    for row in range(segment)
                ]
                blocks = [
                    pltpu.roll(blocks[-1], 1, 0),
                    *blocks,
                    pltpu.roll(blocks[0], TILE - 1, 0),
                ]
                for row, block in enumerate(blocks):
                    part[field, plane, row] = block


def conduct_of(step):
    return COND_EL + COND_LI * step


def steps_kernel(part, near, across, other, *refs):
    halves, refs = refs[: 1 + part], refs[1 + 2 * part :]
    result, message, natural, phase, phase_new, pot, pot_new, disp, disp_new = refs[:9]
    slopes, slopes_y, cond_x, cond_y, cond_y_back, cond_z = refs[9:]
    _, slab, rows, _ = result.shape
    all_rows = 2 * rows
    planes = 2 * slab
    side = lax.axis_index("grow")
    mine = half_of(side)
    mid = rows // 2
    count = FIELDS * slab
    per = LANES // REACH
    inner = LANES // 2 - REACH * side
    outer = (LANES - REACH) * (1 - side)
    in_inner, in_outer = from_lane(inner), from_lane(outer)
    segment = phase.shape[1] - 2

    def arrived_half(which, row):
        for ref in halves:
            half = ref.shape[0] // count
            if row < 2 * half:
                block = ref[pl.ds(which * half + row % half, TILE), :]
                return turned(block, LANES // 2) if row >= half else block
            row -= 2 * half

    for field in range(FIELDS):
        for plane in range(slab):
            which = field * slab + plane
            for at in range(0, rows + 2 * REACH, TILE):
                row = part * rows + at - REACH
                if 0 <= row < all_rows:
                    spot, group = pl.ds(which * TILE, TILE), row // TILE
                    strip = across[pl.ds((count + which) * TILE, TILE), :]
                    block = arrived_half(which, row)
                else:
                    end = int(row > 0)
                    extra, group = divmod(2 * which + end, per)
                    spot = pl.ds((count + extra) * TILE, TILE)
                    strip = across[pl.ds((2 * count + extra) * TILE, TILE), :]
                    block = across[pl.ds(which * TILE, TILE), :]
                    block = turned(block, LANES // 2) if end else block
                block = jnp.where(in_inner, turned(strip, inner - group * REACH), block)
                back = outer - group * REACH
                block = jnp.where(in_outer, turned(other[spot, :], back), block)
                natural[field, plane, pl.ds(at, TILE), :] = block

    def parts_of(phase, pot, disp):
        return (phase, pot, disp.at[0], disp.at[1], disp.at[2])

    def close(ref):
        for plane in range(planes):
            ref[plane, 0] = pltpu.roll(ref[plane, segment], 1, 0)
            ref[plane, segment + 1] = pltpu.roll(ref[plane, 1], TILE - 1, 0)

    for field, ref in enumerate(parts_of(phase, pot, disp)):
        for plane in range(slab):
            own, far = side * slab + plane, (1 - side) * slab + plane
            for row in range(segment + 2):
                ref[own, row] = near[field, plane, row]
            for row in range(segment):
                ref[far, 1 + row] = natural[field, plane, pl.ds(row, TILE, stride=segment), :]
            ref[far, 0] = pltpu.roll(ref[far, segment], 1, 0)
            ref[far, segment + 1] = pltpu.roll(ref[far, 1], TILE - 1, 0)

    def one_row(row, bodies):
        waiting = []
        running = [body(row) for body in bodies]
        while running:
            for body in list(running):
                stores = next(body, None)
                if stores is None:
                    running.remove(body)
                else:
                    waiting.append(stores)
            while len(waiting) > LAG * len(bodies) or (waiting and not running):
                for ref, lead, value in waiting.pop(0):
                    ref[lead + (row,)] = value

    def over_rows(*bodies):
        together = max(n for n in range(1, TOGETHER + 1) if segment % n == 0)

        def some(turn, carry):
            for more in range(together):
                one_row(1 + turn * together + more, bodies)
            return carry

        if together == segment:
            some(0, 0)
        else:
            lax.fori_loop(0, segment // together, some, 0)

    def up(block):
        return pltpu.roll(block, LANES - 1, 1)

    def down(block):
        return pltpu.roll(block, 1, 1)

    push = 0.5 * TAU_U * STIFF * EIGEN

    def conduct_pass(source):
        def body(row):
            face = 0.5 * TAU_P
            before = conduct_of(1.0)
            for plane in range(planes):
                step, ahead, back = (interp(source[plane, row + shift]) for shift in (0, 1, -1))
                here = conduct_of(step)
                yield [
                    (slopes, (plane,), push * step),
                    (slopes_y, (plane,), push * (ahead - back)),
                    (cond_x, (plane,), face * (before + here)),
                    (cond_y, (plane,), face * (here + conduct_of(ahead))),
                    (cond_y_back, (plane,), face * (here + conduct_of(back))),
                    (cond_z, (plane,), face * (here + up(here))),
                ]
                before = here
            yield [(cond_x, (planes,), face * (before + conduct_of(0.0)))]

        return body

    def potential_pass(old, new, low):
        def body(row):
            here = old[low, row]
            before = old[low - 1, row] if low else 0.0
            entering = cond_x[low, row] * (here - before)
            for plane in range(low, planes):
                after = old[plane + 1, row] if plane + 1 < planes else V_HIGH
                leaving = cond_x[plane + 1, row] * (after - here)
                along_y = cond_y[plane, row] * (old[plane, row + 1] - here)
                along_y -= cond_y_back[plane, row] * (here - old[plane, row - 1])
                along_z = cond_z[plane, row] * (up(here) - here)
                along_z -= down(along_z)
                yield [(new, (plane,), here + ((leaving - entering) + along_y + along_z))]
                here, entering = after, leaving

        return body

    grad = LAME_FIRST + SHEAR
    cross = 0.25 * TAU_U * grad
    side_on = TAU_U * SHEAR
    head_on = TAU_U * (SHEAR + grad)
    keep = 1.0 - TAU_U * (6.0 * SHEAR + 2.0 * grad)

    def elastic_pass(old, new, low):
        def body(row):
            def load(plane):
                if plane < 0 or plane >= planes:
                    return (0.0,) * 3, (0.0,) * 3, (0.0,) * 3, -push if plane < 0 else 0.0
                parts = [old[part, plane, row] for part in range(3)]
                ahead = [old[part, plane, row + 1] for part in range(3)]
                back = [old[part, plane, row - 1] for part in range(3)]
                sums = [one + two for one, two in zip(ahead, back)]
                diffs = [one - two for one, two in zip(ahead, back)]
                return parts, sums, diffs, cross * diffs[1] - slopes[plane, row]

            before, here = load(low - 1), load(low)
            for plane in range(low, planes):
                after = load(plane + 1)
                (a, b, c), sums, diffs, slope = here
                sum_x = [one + two for one, two in zip(after[0], before[0])]
                lift = cross * (after[0][2] - before[0][2])
                mid_a = side_on * a
                new_a = (
                    keep * a
                    + head_on * sum_x[0]
                    + side_on * sums[0]
                    + (up(mid_a + lift) + down(mid_a - lift))
                    + (after[3] - before[3])
                )
                lift = cross * diffs[2]
                mid_b = side_on * b
                new_b = (
                    keep * b
                    + head_on * sums[1]
                    + side_on * sum_x[1]
                    + (up(mid_b + lift) + down(mid_b - lift))
                    + (cross * (after[2][0] - before[2][0]) - slopes_y[plane, row])
                )
                lift = cross * (after[0][0] - before[0][0]) + slope
                mid_c = head_on * c
                new_c = (
                    keep * c
                    + side_on * (sum_x[2] + sums[2])
                    + (up(mid_c + lift) + down(mid_c - lift))
                )
                yield [(new, (part, plane), value) for part, value in enumerate((new_a, new_b, new_c))]
                before, here = here, after

        return body

    def phase_pass(source, pot_now, disp_now, low, new):
        def body(row):
            def load(plane):
                if plane < 0 or plane >= planes:
                    return (1.0 if plane < 0 else 0.0, 0.0)
                return (source[plane, row], disp_now[0, plane, row])

            before, here = load(low - 1), load(low)
            for plane in range(low, planes):
                after = load(plane + 1)
                p = here[0]
                c = disp_now[2, plane, row]
                div = (
                    (after[1] - before[1])
                    + (disp_now[1, plane, row + 1] - disp_now[1, plane, row - 1])
                    + (up(c) - down(c))
                )
                over = (
                    (pot_now[plane, row] - REST)
                    + (0.5 * OMEGA_THIRD * STIFF) * div
                    - (OMEGA_THIRD * STIFF * 3.0 * EIGEN) * interp(p)
                )
                drive = jnp.exp(over) - jnp.exp(-over)
                lap = (
                    (before[0] + after[0])
                    + (source[plane, row + 1] + source[plane, row - 1])
                    + (up(p) + down(p))
                    - 6.0 * p
                )
                well = p * (1.0 - p)
                change = lap - well * (2.0 * (1.0 - 2.0 * p) + (6.0 * RATE) * drive)
                yield [(new, (plane,), p + TIME_STEP * change)]
                before, here = here, after

        return body

    for step in range(STEPS):
        last = step == STEPS - 1
        over_rows(conduct_pass(phase))
        for sweep in range(SWEEPS):
            ahead = SWEEPS - 1 - sweep
            over_rows(
                potential_pass(pot, pot_new, max(0, slab - ahead) if last else 0),
                elastic_pass(disp, disp_new, max(0, slab - ahead - 1) if last else 0),
            )
            pot, pot_new, disp, disp_new = pot_new, pot, disp_new, disp
            for ref in (pot, disp.at[0], disp.at[1], disp.at[2]):
                close(ref)
        over_rows(phase_pass(phase, pot, disp, slab if last else 0, phase_new))
        phase, phase_new = phase_new, phase
        if not last:
            close(phase)
    for field, ref in enumerate(parts_of(phase, pot, disp)):
        for plane in range(slab):
            for row in range(segment):
                to = pl.ds(row, TILE, stride=segment)
                natural[field, plane, to, :] = ref[slab + plane, 1 + row]
            for row in range(0, mid, TILE):
                upper = natural[field, plane, pl.ds(REACH + row, TILE), :]
                lower = natural[field, plane, pl.ds(REACH + row + mid, TILE), :]
                result[field, plane, pl.ds(row, TILE), :] = upper
                result[field, plane, pl.ds(row + mid, TILE), :] = lower
                to = pl.ds((field * slab + plane) * mid + row, TILE)
                message[to, :] = jnp.where(mine, upper, turned(lower, LANES // 2))


def finish_kernel(result_a, result_b, message_a, message_b, phase, potential, displacement):
    slab, rows = result_a.shape[1:3]
    side = lax.axis_index("grow")
    mine = half_of(side)
    fresh = side == lax.axis_size("grow") - 1
    mid = rows // 2
    for part, (result, message) in enumerate(((result_a, message_a), (result_b, message_b))):
        for field in range(FIELDS):
            out = (phase, potential, displacement, displacement, displacement)[field]
            for plane in range(slab):
                for row in range(0, mid, TILE):
                    block = message[pl.ds((field * slab + plane) * mid + row, TILE), :]
                    for place, piece in ((row, block), (row + mid, turned(block, LANES // 2))):
                        own = result[field, plane, pl.ds(place, TILE), :]
                        whole = jnp.where(mine, own, piece)
                        whole = jnp.where(fresh, V_HIGH if field == 1 else 0.0, whole)
                        spot = (plane, pl.ds(part * rows + place, TILE), slice(None))
                        out[spot if field < 2 else (field - 2,) + spot] = whole


def call(kernel, outs, scratch=(), limit=48, **how):
    return pl.pallas_call(
        kernel,
        out_shape=[jax.ShapeDtypeStruct(shape, jnp.float32) for shape in outs],
        scratch_shapes=[
            pltpu.VMEM(one, jnp.float32) if isinstance(one, tuple) else one for one in scratch
        ],
        **{"cost_estimate": pl.CostEstimate(flops=1, bytes_accessed=1, transcendentals=0), **how},
        compiler_params=pltpu.CompilerParams(vmem_limit_bytes=limit * 1024 * 1024),
    )


def pair_shards(labels, roughness, potential, displacement):
    slab, rows, _ = labels.shape
    count = FIELDS * slab
    early = (rows // TILE // 2 + 2) // 2 * TILE
    late = rows // 2 - early
    sizes = {name: lax.axis_size(name) for name in ("grow", "cy", "cz")}

    def index(grow, cy, cz):
        cy, cz = cy % sizes["cy"], cz % sizes["cz"]
        return (grow * sizes["cy"] + cy) * sizes["cz"] + cz

    everyone = [
        (grow, cy, cz)
        for grow in range(sizes["grow"])
        for cy in range(sizes["cy"])
        for cz in range(sizes["cz"])
    ]

    def send(block, route):
        pairs = [(index(*at), index(*route(*at))) for at in everyone]
        return lax.ppermute(block, ("grow", "cy", "cz"), pairs)

    fields, halves, first, last = call(
        prepare_kernel,
        [(FIELDS,) + labels.shape, (count * early, LANES)] + [(count * TILE, LANES)] * 2,
        [pltpu.VMEM(labels.shape, labels.dtype), labels.shape, pltpu.SemaphoreType.DMA((4,))],
        limit=54,
        in_specs=[pl.BlockSpec(memory_space=pltpu.HBM)] * 4,
    )(labels, roughness, potential, displacement)
    halves = [send(halves, lambda grow, cy, cz: (1 - grow, cy, cz))]
    above = send(last, lambda grow, cy, cz: (grow, cy + 1, cz))
    below = send(first, lambda grow, cy, cz: (grow, cy - 1, cz))
    extra = rim_rows(slab)
    across, same, other = call(
        rims_kernel, [(count * TILE + extra, LANES)] + [(extra, LANES)] * 2
    )(fields, above, below)
    across = send(across, lambda grow, cy, cz: (1 - grow, cy, cz))
    same = send(same, lambda grow, cy, cz: (grow, cy, cz - 1 if grow else cz + 1))
    other = send(other, lambda grow, cy, cz: (1 - grow, cy, cz + 1 if grow else cz - 1))
    span = rows // 2 + 2 * REACH
    near = (FIELDS, slab, span // TILE + 2, TILE, LANES)
    near = call(own_kernel, [near, near], [(count, rows + 2 * REACH, LANES)])(
        fields, above, below, same
    )
    deep = (2 * slab, span // TILE + 2, TILE, LANES)
    results, messages = [], []
    in_vmem, anywhere = (pl.BlockSpec(memory_space=space) for space in (pltpu.VMEM, pl.ANY))
    (rest,) = call(rest_kernel, [(count * late, LANES)], in_specs=[in_vmem] + [anywhere] * 5)(
        fields, across, other, *halves, *near
    )
    halves.append(send(rest, lambda grow, cy, cz: (1 - grow, cy, cz)))
    for part in range(2):
        result, message = call(
            functools.partial(steps_kernel, part),
            [(FIELDS, slab, rows // 2, LANES), (count * rows // 4, LANES)],
            [(FIELDS, slab, span, LANES)]
            + [deep] * 4
            + [(3,) + deep] * 2
            + [deep, deep, (2 * slab + 1,) + deep[1:], deep, deep, deep],
            in_specs=[in_vmem] * (4 + part) + [anywhere] * part,
            cost_estimate=pl.CostEstimate(
                flops=STEPS * SWEEPS * 160 * span * 2 * slab * LANES,
                bytes_accessed=STEPS * SWEEPS * 40 * span * 2 * slab * LANES,
                transcendentals=STEPS * 2 * span * 2 * slab * LANES,
            ),
        )(near[part], across, other, *halves[: 1 + part], *results)
        results.append(result)
        messages.append(from_behind(message, "grow", -1))
    return call(finish_kernel, [labels.shape, labels.shape, displacement.shape])(
        *results, *messages
    )


def fits_pair(labels):
    rows, columns = labels.shape[1:]
    blocks = rows % (4 * TILE) == 0 and rows >= 8 * TILE and rows // TILE * REACH <= LANES
    return lax.axis_size("grow") == 2 and columns == LANES and REACH == TILE and blocks


def whole(labels, roughness, potential, displacement):
    plan = pair_shards if fits_pair(labels) else shards
    return tuple(plan(labels, roughness, potential, displacement))


def solution(mesh):
    placed = (
        P("grow", "cy", "cz"),
        P("grow", "cy", "cz"),
        P("grow", "cy", "cz"),
        P(None, "grow", "cy", "cz"),
    )
    return jax.shard_map(
        whole,
        mesh=mesh,
        in_specs=placed,
        out_specs=(P("grow", "cy", "cz"), P("grow", "cy", "cz"), P(None, "grow", "cy", "cz")),
        check_vma=False,
    )
```

```python
import functools

import jax
import jax.numpy as jnp
from jax import lax
from jax.experimental import pallas as pl
from jax.experimental.pallas import tpu as pltpu
from jax.sharding import PartitionSpec as P

STEPS = 2
SWEEPS = 3


TAU_P = 0.15
TAU_U = 0.08
SHEAR = 1.0
LAME_FIRST = 1.5
STIFF = 6.5
EIGEN = 0.1
COND_EL = 0.1
COND_LI = 0.9
V_HIGH = 1.0
TIME_STEP = 0.05
REST = 0.5
OMEGA_THIRD = 0.1
RATE = 0.5


def extended(cells, sides, width, closed):
    for axis, dim in sides:
        count = lax.axis_size(axis)
        ends = count if closed else count - 1
        head = lax.slice_in_dim(cells, 0, width, axis=dim)
        tail = lax.slice_in_dim(cells, cells.shape[dim] - width, cells.shape[dim], axis=dim)
        cells = jnp.concatenate(
            [
                lax.ppermute(tail, axis, [(i, (i + 1) % count) for i in range(ends)]),
                cells,
                lax.ppermute(head, axis, [((i + 1) % count, i) for i in range(ends)]),
            ],
            axis=dim,
        )
    return cells


def from_behind(block, axis, distance):
    devices = range(lax.axis_size(axis))
    route = [(i - distance, i) for i in devices if i - distance in devices]
    return lax.ppermute(block, axis, route)


def unit(direction, sign):
    offsets = [0, 0, 0]
    offsets[direction] = sign
    return offsets


def offset(field, offsets):
    lead_dims = field.ndim - 3
    slices = [slice(None)] * lead_dims
    for direction in range(3):
        extent = field.shape[lead_dims + direction]
        slices.append(slice(1 + offsets[direction], extent - 1 + offsets[direction]))
    return field[tuple(slices)]


def centre(field):
    return offset(field, (0, 0, 0))


def laplace(field):
    total = -6.0 * centre(field)
    for direction in range(3):
        total = total + offset(field, unit(direction, 1)) + offset(field, unit(direction, -1))
    return total


def interp(phase):
    return phase * phase * (3.0 - 2.0 * phase)


def interp_slope(phase):
    return 6.0 * phase * (1.0 - phase)


def potential_sweep(potential_pad, conduct_pad):
    here = centre(potential_pad)
    conduct_here = centre(conduct_pad)
    flux = jnp.zeros_like(here)
    for direction in range(3):
        for sign in (1, -1):
            moved = unit(direction, sign)
            flux = flux + 0.5 * (offset(conduct_pad, moved) + conduct_here) * (
                offset(potential_pad, moved) - here
            )
    return here + TAU_P * flux


def cross_term(field, first, second):
    total = jnp.zeros_like(centre(field))
    for sign_first in (1, -1):
        for sign_second in (1, -1):
            offsets = [0, 0, 0]
            offsets[first] = sign_first
            offsets[second] = sign_second
            total = total + sign_first * sign_second * offset(field, offsets)
    return 0.25 * total


def elastic_sweep(disp_pad, interp_pad):
    updated = []
    for component in range(3):
        own = disp_pad[component]
        grad_div = (
            offset(own, unit(component, 1)) - 2.0 * centre(own) + offset(own, unit(component, -1))
        )
        for other in range(3):
            if other != component:
                grad_div = grad_div + cross_term(disp_pad[other], component, other)
        slope = 0.5 * (
            offset(interp_pad, unit(component, 1)) - offset(interp_pad, unit(component, -1))
        )
        force = SHEAR * laplace(own) + (LAME_FIRST + SHEAR) * grad_div - STIFF * EIGEN * slope
        updated.append(centre(own) + TAU_U * force)
    return jnp.stack(updated)


def divergence(disp_pad):
    total = jnp.zeros_like(centre(disp_pad[0]))
    for component in range(3):
        total = total + 0.5 * (
            offset(disp_pad[component], unit(component, 1))
            - offset(disp_pad[component], unit(component, -1))
        )
    return total


def phase_update(phase_pad, potential, div_disp):
    phase = centre(phase_pad)
    trace = STIFF * (div_disp - 3.0 * EIGEN * interp(phase))
    over = potential - REST + OMEGA_THIRD * trace
    drive = jnp.exp(over) - jnp.exp(-over)
    change = (
        laplace(phase_pad)
        - 2.0 * phase * (1.0 - phase) * (1.0 - 2.0 * phase)
        - RATE * interp_slope(phase) * drive
    )
    return phase + TIME_STEP * change


def pin_ends(field, width, slab, low, high):
    if width == 0:
        return field
    lead_dims = field.ndim - 3
    planes = field.shape[lead_dims]
    first = lax.axis_index("grow") * slab - width
    position = first + lax.broadcasted_iota(jnp.int32, (planes, 1, 1), 0)
    limit = slab * lax.axis_size("grow")
    result = jnp.where(position < 0, low, field)
    return jnp.where(position >= limit, high, result)


def column_values(values):
    return jnp.array(values, jnp.float32).reshape(len(values), 1, 1, 1)


def strip(field, count):
    for repeat in range(count):
        field = centre(field)
    return field


def shards(labels, roughness, potential, displacement):
    slab = labels.shape[0]
    rim = SWEEPS + 1
    mark = labels.astype(jnp.float32)
    phase = mark * (1.0 - 0.3 * roughness) + (1.0 - mark) * (0.3 * roughness)
    low_five = column_values([1.0, 0.0, 0.0, 0.0, 0.0])
    high_five = column_values([0.0, V_HIGH, 0.0, 0.0, 0.0])
    for step_index in range(STEPS):
        packed = jnp.concatenate([phase[None], potential[None], displacement], axis=0)
        packed = extended(packed, (("grow", 1),), SWEEPS + 1, False)
        packed = pin_ends(packed, SWEEPS + 1, slab, low_five, high_five)
        packed = extended(packed, (("cy", 2), ("cz", 3)), SWEEPS + 1, True)
        phase_pad = packed[0]
        interp_pad = interp(phase_pad)
        conduct_pad = COND_EL + COND_LI * interp_pad
        pot_pad = strip(packed[1], 1)
        conduct_now = centre(conduct_pad)
        for repeat in range(SWEEPS):
            pot_pad = pin_ends(
                potential_sweep(pot_pad, conduct_now), SWEEPS - 1 - repeat, slab, 0.0, V_HIGH
            )
            if repeat + 1 < SWEEPS:
                conduct_now = centre(conduct_now)
        potential = pot_pad
        disp_pad = packed[2:]
        interp_now = interp_pad
        for repeat in range(SWEEPS):
            disp_pad = pin_ends(
                elastic_sweep(disp_pad, interp_now), SWEEPS - repeat, slab, 0.0, 0.0
            )
            if repeat + 1 < SWEEPS:
                interp_now = centre(interp_now)
        div_disp = divergence(disp_pad)
        displacement = centre(disp_pad)
        phase = phase_update(strip(phase_pad, rim - 1), potential, div_disp)
    stacked = jnp.concatenate([phase[None], potential[None], displacement], axis=0)
    arrived = from_behind(stacked, "grow", -1)
    fresh = jnp.array([0.0, V_HIGH, 0.0, 0.0, 0.0], jnp.float32).reshape(5, 1, 1, 1)
    is_last = lax.axis_index("grow") == lax.axis_size("grow") - 1
    arrived = jnp.where(is_last, fresh, arrived)
    return (arrived[0], arrived[1], arrived[2:])


REACH = STEPS * (SWEEPS + 1)
TILE = 8
FIELDS = 5
LAG = 2
TOGETHER = 12


def lanes(shape):
    return lax.broadcasted_iota(jnp.int32, shape, 1)


def from_lane(first):
    lane = lanes((TILE, LANES))
    return jnp.logical_and(lane >= first, lane < first + REACH)


LANES = 128


def turned(block, amount):
    return pltpu.roll(block, lax.rem(amount + 2 * LANES, LANES), 1)


def half_of(side):
    low = lanes((TILE, LANES)) < LANES // 2
    return jnp.logical_xor(low, side == 1)


def pack_halves(fields, upper, lower, mid, theirs, out):
    _, slab, _, _ = fields.shape
    for field in range(FIELDS):
        for plane in range(slab):
            for row in range(0, mid, TILE):
                one = fields[field, plane, pl.ds(upper + row, TILE), :]
                two = fields[field, plane, pl.ds(lower + row, TILE), :]
                to = pl.ds((field * slab + plane) * mid + row, TILE)
                out[to, :] = jnp.where(theirs, one, turned(two, LANES // 2))


def pack_strips(fields, base, out, start):
    _, slab, rows, _ = fields.shape
    for field in range(FIELDS):
        for plane in range(slab):
            packed = jnp.zeros((TILE, LANES), jnp.float32)
            for group in range(rows // TILE):
                block = fields[field, plane, pl.ds(group * TILE, TILE), :]
                block = turned(block, group * REACH - base)
                packed = jnp.where(from_lane(group * REACH), block, packed)
            out[pl.ds(start + (field * slab + plane) * TILE, TILE), :] = packed


def pack_rim_strips(above, below, base, out, start):
    per = LANES // REACH
    blocks = 2 * above.shape[0] // TILE
    for first in range(0, blocks, per):
        packed = jnp.zeros((TILE, LANES), jnp.float32)
        for which in range(first, min(first + per, blocks)):
            block = (above, below)[which % 2][pl.ds(which // 2 * TILE, TILE), :]
            to = which % per * REACH
            packed = jnp.where(from_lane(to), turned(block, to - base), packed)
        out[pl.ds(start + first // per * TILE, TILE), :] = packed


def strip_bases(side):
    outer = LANES - REACH
    return LANES // 2 - REACH + REACH * side, outer * (1 - side), outer * side


def split(rows):
    return rows // 4 - REACH, 3 * rows // 4 + REACH


def prepare_kernel(
    labels, roughness, potential, displacement,
    fields, halves, same, other, first, last, marks, rough, arrived,
):
    _, slab, rows, _ = fields.shape
    side = lax.axis_index("grow")
    count = FIELDS * slab
    copies = [
        pltpu.make_async_copy(source, target, arrived.at[which])
        for which, (source, target) in enumerate(
            (
                (labels, marks),
                (roughness, rough),
                (potential, fields.at[1]),
                (displacement, fields.at[pl.ds(2, 3)]),
            )
        )
    ]
    for copy in copies:
        copy.start()
    for copy in copies[:2]:
        copy.wait()
    for plane in range(slab):
        for row in range(0, rows, TILE):
            spot = (plane, pl.ds(row, TILE), slice(None))
            mark = marks[spot].astype(jnp.float32)
            part = 0.3 * rough[spot]
            fields[(0,) + spot] = mark * (1.0 - part) + (1.0 - mark) * part
    for copy in copies[2:]:
        copy.wait()
    start, stop = split(rows)
    mid = (stop - start) // 2
    pack_halves(fields, start, start + mid, mid, jnp.logical_not(half_of(side)), halves)
    for out, at, base in zip((halves, same, other), (count * mid, 0, 0), strip_bases(side)):
        pack_strips(fields, base, out, at)
    for field in range(FIELDS):
        for plane in range(slab):
            spot = pl.ds((field * slab + plane) * TILE, TILE)
            first[spot, :] = fields[field, plane, pl.ds(0, TILE), :]
            last[spot, :] = fields[field, plane, pl.ds(rows - TILE, TILE), :]


def rims_kernel(fields, above, below, same_first, other_first, halves, same, other):
    _, slab, rows, _ = fields.shape
    side = lax.axis_index("grow")
    theirs = jnp.logical_not(half_of(side))
    count = FIELDS * slab
    start, stop = split(rows)
    pack_halves(fields, 0, stop, start, theirs, halves)
    for which in range(count):
        spot = pl.ds(which * TILE, TILE)
        rims = jnp.where(theirs, above[spot, :], turned(below[spot, :], LANES // 2))
        halves[pl.ds(count * start + which * TILE, TILE), :] = rims
    starts = (count * (start + TILE), 0, 0)
    for out, at, base in zip((halves, same, other), starts, strip_bases(side)):
        pack_rim_strips(above, below, base, out, at)


def blocks_of(part, rows):
    start, stop = split(rows)
    if part == 0:
        return list(range(start, stop, TILE))
    inner = start + 2 * REACH
    return list(range(-REACH, inner, TILE)) + list(range(rows - inner, rows + REACH, TILE))


def packed_at(which, row, rows, count):
    if 0 <= row < rows:
        return False, which * TILE, row // TILE * REACH
    at, group = divmod(2 * which + int(row > 0), LANES // REACH)
    return True, at * TILE, group * REACH


def own_kernel(part, fields, *refs):
    out, natural = refs[-2:]
    same, *more = refs[:-2]
    same_rims, above, below = more or (None, None, None)
    _, slab, rows, _ = fields.shape
    count = FIELDS * slab
    outer = (LANES - REACH) * (1 - lax.axis_index("grow"))
    in_outer = from_lane(outer)
    segment = out.shape[2] - 2
    for field in range(FIELDS):
        for plane in range(slab):
            which = field * slab + plane
            for at, row in enumerate(blocks_of(part, rows)):
                of_rim, spot, lane = packed_at(which, row, rows, count)
                piece = (same_rims if of_rim else same)[pl.ds(spot, TILE), :]
                if of_rim:
                    near = (below if row > 0 else above)[pl.ds(which * TILE, TILE), :]
                else:
                    near = fields[field, plane, pl.ds(row, TILE), :]
                near = jnp.where(in_outer, turned(piece, outer - lane), near)
                natural[which, pl.ds(at * TILE, TILE), :] = near
            blocks = [natural[which, pl.ds(row, TILE, stride=segment), :] for row in range(segment)]
            blocks = [pltpu.roll(blocks[-1], 1, 0), *blocks, pltpu.roll(blocks[0], TILE - 1, 0)]
            for row, block in enumerate(blocks):
                out[field, plane, row] = block


def conduct_of(step):
    return COND_EL + COND_LI * step


def steps_kernel(part, near, other, halves, *refs):
    if part:
        other_rims, rest, _, *refs = refs
    result, message, natural, phase, phase_new, pot, pot_new, disp, disp_new = refs[:9]
    slopes, slopes_y, cond_x, cond_y, cond_y_back, cond_z = refs[9:]
    _, slab, rows, _ = result.shape
    all_rows = 2 * rows
    planes = 2 * slab
    side = lax.axis_index("grow")
    mine = half_of(side)
    count = FIELDS * slab
    inner = LANES // 2 - REACH * side
    outer = (LANES - REACH) * (1 - side)
    in_inner, in_outer = from_lane(inner), from_lane(outer)
    segment = phase.shape[1] - 2
    start, stop = split(all_rows)
    half = (stop - start) // 2
    blocks = blocks_of(part, all_rows)

    def arrived_half(which, row):
        if start <= row < stop:
            block = halves[pl.ds(which * half + (row - start) % half, TILE), :]
            return turned(block, LANES // 2) if row - start >= half else block
        if 0 <= row < all_rows:
            block = rest[pl.ds(which * start + row % stop, TILE), :]
        else:
            block = rest[pl.ds(count * start + which * TILE, TILE), :]
        return turned(block, LANES // 2) if row > 0 and row >= stop else block

    for field in range(FIELDS):
        for plane in range(slab):
            which = field * slab + plane
            for at, row in enumerate(blocks):
                of_rim, spot, lane = packed_at(which, row, all_rows, count)
                if of_rim:
                    strip = rest[pl.ds(count * (start + TILE) + spot, TILE), :]
                    beside = other_rims[pl.ds(spot, TILE), :]
                else:
                    strip = halves[pl.ds(count * half + spot, TILE), :]
                    beside = other[pl.ds(spot, TILE), :]
                block = jnp.where(in_inner, turned(strip, inner - lane), arrived_half(which, row))
                block = jnp.where(in_outer, turned(beside, outer - lane), block)
                natural[field, plane, pl.ds(at * TILE, TILE), :] = block

    def parts_of(phase, pot, disp):
        return (phase, pot, disp.at[0], disp.at[1], disp.at[2])

    def close(ref):
        for plane in range(planes):
            ref[plane, 0] = pltpu.roll(ref[plane, segment], 1, 0)
            ref[plane, segment + 1] = pltpu.roll(ref[plane, 1], TILE - 1, 0)

    for field, ref in enumerate(parts_of(phase, pot, disp)):
        for plane in range(slab):
            own, far = side * slab + plane, (1 - side) * slab + plane
            for row in range(segment + 2):
                ref[own, row] = near[field, plane, row]
            for row in range(segment):
                ref[far, 1 + row] = natural[field, plane, pl.ds(row, TILE, stride=segment), :]
            ref[far, 0] = pltpu.roll(ref[far, segment], 1, 0)
            ref[far, segment + 1] = pltpu.roll(ref[far, 1], TILE - 1, 0)

    def one_row(row, bodies):
        waiting = []
        running = [body(row) for body in bodies]
        while running:
            for body in list(running):
                stores = next(body, None)
                if stores is None:
                    running.remove(body)
                else:
                    waiting.append(stores)
            while len(waiting) > LAG * len(bodies) or (waiting and not running):
                for ref, lead, value in waiting.pop(0):
                    ref[lead + (row,)] = value

    def over_rows(*bodies):
        together = max(n for n in range(1, TOGETHER + 1) if segment % n == 0)

        def some(turn, carry):
            for more in range(together):
                one_row(1 + turn * together + more, bodies)
            return carry

        if together == segment:
            some(0, 0)
        else:
            lax.fori_loop(0, segment // together, some, 0)

    def up(block):
        return pltpu.roll(block, LANES - 1, 1)

    def down(block):
        return pltpu.roll(block, 1, 1)

    push = 0.5 * TAU_U * STIFF * EIGEN

    def conduct_pass(source):
        def body(row):
            face = 0.5 * TAU_P
            before = conduct_of(1.0)
            for plane in range(planes):
                step, ahead, back = (interp(source[plane, row + shift]) for shift in (0, 1, -1))
                here = conduct_of(step)
                yield [
                    (slopes, (plane,), push * step),
                    (slopes_y, (plane,), push * (ahead - back)),
                    (cond_x, (plane,), face * (before + here)),
                    (cond_y, (plane,), face * (here + conduct_of(ahead))),
                    (cond_y_back, (plane,), face * (here + conduct_of(back))),
                    (cond_z, (plane,), face * (here + up(here))),
                ]
                before = here
            yield [(cond_x, (planes,), face * (before + conduct_of(0.0)))]

        return body

    def potential_pass(old, new, low):
        def body(row):
            here = old[low, row]
            before = old[low - 1, row] if low else 0.0
            entering = cond_x[low, row] * (here - before)
            for plane in range(low, planes):
                after = old[plane + 1, row] if plane + 1 < planes else V_HIGH
                leaving = cond_x[plane + 1, row] * (after - here)
                along_y = cond_y[plane, row] * (old[plane, row + 1] - here)
                along_y -= cond_y_back[plane, row] * (here - old[plane, row - 1])
                along_z = cond_z[plane, row] * (up(here) - here)
                along_z -= down(along_z)
                yield [(new, (plane,), here + ((leaving - entering) + along_y + along_z))]
                here, entering = after, leaving

        return body

    grad = LAME_FIRST + SHEAR
    cross = 0.25 * TAU_U * grad
    side_on = TAU_U * SHEAR
    head_on = TAU_U * (SHEAR + grad)
    keep = 1.0 - TAU_U * (6.0 * SHEAR + 2.0 * grad)

    def elastic_pass(old, new, low):
        def body(row):
            def load(plane):
                if plane < 0 or plane >= planes:
                    return (0.0,) * 3, (0.0,) * 3, (0.0,) * 3, -push if plane < 0 else 0.0
                parts = [old[part, plane, row] for part in range(3)]
                ahead = [old[part, plane, row + 1] for part in range(3)]
                back = [old[part, plane, row - 1] for part in range(3)]
                sums = [one + two for one, two in zip(ahead, back)]
                diffs = [one - two for one, two in zip(ahead, back)]
                return parts, sums, diffs, cross * diffs[1] - slopes[plane, row]

            before, here = load(low - 1), load(low)
            for plane in range(low, planes):
                after = load(plane + 1)
                (a, b, c), sums, diffs, slope = here
                sum_x = [one + two for one, two in zip(after[0], before[0])]
                lift = cross * (after[0][2] - before[0][2])
                mid_a = side_on * a
                new_a = (
                    keep * a
                    + head_on * sum_x[0]
                    + side_on * sums[0]
                    + (up(mid_a + lift) + down(mid_a - lift))
                    + (after[3] - before[3])
                )
                lift = cross * diffs[2]
                mid_b = side_on * b
                new_b = (
                    keep * b
                    + head_on * sums[1]
                    + side_on * sum_x[1]
                    + (up(mid_b + lift) + down(mid_b - lift))
                    + (cross * (after[2][0] - before[2][0]) - slopes_y[plane, row])
                )
                lift = cross * (after[0][0] - before[0][0]) + slope
                mid_c = head_on * c
                new_c = (
                    keep * c
                    + side_on * (sum_x[2] + sums[2])
                    + (up(mid_c + lift) + down(mid_c - lift))
                )
                yield [(new, (part, plane), value) for part, value in enumerate((new_a, new_b, new_c))]
                before, here = here, after

        return body

    def phase_pass(source, pot_now, disp_now, low, new):
        def body(row):
            def load(plane):
                if plane < 0 or plane >= planes:
                    return (1.0 if plane < 0 else 0.0, 0.0)
                return (source[plane, row], disp_now[0, plane, row])

            before, here = load(low - 1), load(low)
            for plane in range(low, planes):
                after = load(plane + 1)
                p = here[0]
                c = disp_now[2, plane, row]
                div = (
                    (after[1] - before[1])
                    + (disp_now[1, plane, row + 1] - disp_now[1, plane, row - 1])
                    + (up(c) - down(c))
                )
                over = (
                    (pot_now[plane, row] - REST)
                    + (0.5 * OMEGA_THIRD * STIFF) * div
                    - (OMEGA_THIRD * STIFF * 3.0 * EIGEN) * interp(p)
                )
                drive = jnp.exp(over) - jnp.exp(-over)
                lap = (
                    (before[0] + after[0])
                    + (source[plane, row + 1] + source[plane, row - 1])
                    + (up(p) + down(p))
                    - 6.0 * p
                )
                well = p * (1.0 - p)
                change = lap - well * (2.0 * (1.0 - 2.0 * p) + (6.0 * RATE) * drive)
                yield [(new, (plane,), p + TIME_STEP * change)]
                before, here = here, after

        return body

    for step in range(STEPS):
        last = step == STEPS - 1
        over_rows(conduct_pass(phase))
        for sweep in range(SWEEPS):
            ahead = SWEEPS - 1 - sweep
            over_rows(
                potential_pass(pot, pot_new, max(0, slab - ahead) if last else 0),
                elastic_pass(disp, disp_new, max(0, slab - ahead - 1) if last else 0),
            )
            pot, pot_new, disp, disp_new = pot_new, pot, disp_new, disp
            for ref in (pot, disp.at[0], disp.at[1], disp.at[2]):
                close(ref)
        over_rows(phase_pass(phase, pot, disp, slab if last else 0, phase_new))
        phase, phase_new = phase_new, phase
        if not last:
            close(phase)
    outs = results_of(part, all_rows)
    for field, ref in enumerate(parts_of(phase, pot, disp)):
        for plane in range(slab):
            for row in range(segment):
                to = pl.ds(row, TILE, stride=segment)
                natural[field, plane, to, :] = ref[slab + plane, 1 + row]
            for at in range(len(outs) // 2):
                pair = []
                for place in (at, at + len(outs) // 2):
                    spot = pl.ds(blocks.index(outs[place]) * TILE, TILE)
                    pair.append(natural[field, plane, spot, :])
                    result[field, plane, pl.ds(place * TILE, TILE), :] = pair[-1]
                to = pl.ds(((field * slab + plane) * len(outs) // 2 + at) * TILE, TILE)
                message[to, :] = jnp.where(mine, pair[0], turned(pair[1], LANES // 2))


def results_of(part, rows):
    quarter = rows // 4
    if part == 0:
        return list(range(quarter, 3 * quarter, TILE))
    return list(range(0, quarter, TILE)) + list(range(3 * quarter, rows, TILE))


def finish_kernel(part, result, message, *refs):
    phase, potential, displacement, whole, arrived = refs[3 * part :]
    _, slab, rows, _ = result.shape
    side = lax.axis_index("grow")
    mine = half_of(side)
    fresh = side == lax.axis_size("grow") - 1
    half = rows // 2
    copies = []
    for field in range(FIELDS):
        for plane in range(slab):
            for row in range(0, rows, TILE):
                spot = pl.ds((field * slab + plane) * half + row % half, TILE)
                block = message[spot, :]
                block = turned(block, LANES // 2) if row >= half else block
                block = jnp.where(mine, result[field, plane, pl.ds(row, TILE), :], block)
                block = jnp.where(fresh, V_HIGH if field == 1 else 0.0, block)
                whole[field, plane, pl.ds(row, TILE), :] = block
        out = (phase, potential, displacement.at[0], displacement.at[1], displacement.at[2])[field]
        for source, target in (((0, 0), (half, 3 * half)) if part else ((0, half), (half, rows))):
            copy = pltpu.make_async_copy(
                whole.at[field, :, pl.ds(source, half), :],
                out.at[:, pl.ds(target, half), :],
                arrived.at[len(copies)],
            )
            copy.start()
            copies.append(copy)
    for copy in copies:
        copy.wait()


def call(kernel, outs, scratch=(), limit=48, **how):
    return pl.pallas_call(
        kernel,
        out_shape=[jax.ShapeDtypeStruct(shape, jnp.float32) for shape in outs],
        scratch_shapes=[
            pltpu.VMEM(one, jnp.float32) if isinstance(one, tuple) else one for one in scratch
        ],
        **{"cost_estimate": pl.CostEstimate(flops=1, bytes_accessed=1, transcendentals=0), **how},
        compiler_params=pltpu.CompilerParams(vmem_limit_bytes=limit * 1024 * 1024),
    )


def pair_shards(labels, roughness, potential, displacement):
    slab, rows, _ = labels.shape
    count = FIELDS * slab
    start, stop = split(rows)
    half = (stop - start) // 2
    spare = -(-2 * count * REACH // LANES) * TILE
    sizes = {name: lax.axis_size(name) for name in ("grow", "cy", "cz")}

    def index(grow, cy, cz):
        cy, cz = cy % sizes["cy"], cz % sizes["cz"]
        return (grow * sizes["cy"] + cy) * sizes["cz"] + cz

    everyone = [
        (grow, cy, cz)
        for grow in range(sizes["grow"])
        for cy in range(sizes["cy"])
        for cz in range(sizes["cz"])
    ]

    def send(block, route):
        pairs = [(index(*at), index(*route(*at))) for at in everyone]
        return lax.ppermute(block, ("grow", "cy", "cz"), pairs)

    def to_partner(block):
        return send(block, lambda grow, cy, cz: (1 - grow, cy, cz))

    def beside_same(block):
        return send(block, lambda grow, cy, cz: (grow, cy, cz - 1 if grow else cz + 1))

    def beside_other(block):
        return send(block, lambda grow, cy, cz: (1 - grow, cy, cz + 1 if grow else cz - 1))

    in_vmem, anywhere, hbm = (
        pl.BlockSpec(memory_space=space) for space in (pltpu.VMEM, pl.ANY, pltpu.HBM)
    )
    thin = (count * TILE, LANES)
    fields, halves, same, other, first, last = call(
        prepare_kernel,
        [(FIELDS,) + labels.shape, (count * (half + TILE), LANES)] + [thin] * 4,
        [pltpu.VMEM(labels.shape, labels.dtype), labels.shape, pltpu.SemaphoreType.DMA((4,))],
        limit=54,
        in_specs=[hbm] * 4,
    )(labels, roughness, potential, displacement)
    halves = to_partner(halves)
    other = beside_other(other)
    above = send(last, lambda grow, cy, cz: (grow, cy + 1, cz))
    below = send(first, lambda grow, cy, cz: (grow, cy - 1, cz))
    same = beside_same(same)
    rest, same_rims, other_rims = call(
        rims_kernel,
        [(count * (start + TILE) + spare, LANES)] + [(spare, LANES)] * 2,
        in_specs=[in_vmem] * 3 + [anywhere] * 2,
    )(fields, above, below, same, other)
    rest = to_partner(rest)
    other_rims = beside_other(other_rims)
    same_rims = beside_same(same_rims)
    results, messages, outs = [], [], []
    for part in range(2):
        span = len(blocks_of(part, rows)) * TILE
        deep = (2 * slab, span // TILE + 2, TILE, LANES)
        (near,) = call(
            functools.partial(own_kernel, part),
            [(FIELDS, slab) + deep[1:]],
            [(count, span, LANES)],
        )(fields, same, *([same_rims, above, below] if part else []))
        result, message = call(
            functools.partial(steps_kernel, part),
            [(FIELDS, slab, rows // 2, LANES), (count * rows // 4, LANES)],
            [(FIELDS, slab, span, LANES)]
            + [deep] * 4
            + [(3,) + deep] * 2
            + [deep, deep, (2 * slab + 1,) + deep[1:], deep, deep, deep],
            in_specs=[in_vmem] * (3 + 2 * part) + [anywhere] * part,
            cost_estimate=pl.CostEstimate(
                flops=STEPS * SWEEPS * 160 * span * 2 * slab * LANES,
                bytes_accessed=STEPS * SWEEPS * 40 * span * 2 * slab * LANES,
                transcendentals=STEPS * 2 * span * 2 * slab * LANES,
            ),
        )(near, other, halves, *([other_rims, rest, *results] if part else []))
        results.append(result)
        messages.append(from_behind(message, "grow", -1))
    for part in range(2):
        outs = call(
            functools.partial(finish_kernel, part),
            [labels.shape, labels.shape, displacement.shape],
            [(FIELDS, slab, rows // 2, LANES), pltpu.SemaphoreType.DMA((2 * FIELDS,))],
            in_specs=[in_vmem] * 2 + [hbm] * (3 * part),
            out_specs=[hbm] * 3,
            input_output_aliases={2 + which: which for which in range(3 * part)},
        )(results[part], messages[part], *outs)
    return outs


def fits_pair(labels):
    rows, columns = labels.shape[1:]
    blocks = rows % (8 * TILE) == 0 and rows // TILE * REACH <= LANES
    return lax.axis_size("grow") == 2 and columns == LANES and REACH == TILE and blocks


def whole(labels, roughness, potential, displacement):
    plan = pair_shards if fits_pair(labels) else shards
    return tuple(plan(labels, roughness, potential, displacement))


def solution(mesh):
    placed = (
        P("grow", "cy", "cz"),
        P("grow", "cy", "cz"),
        P("grow", "cy", "cz"),
        P(None, "grow", "cy", "cz"),
    )
    return jax.shard_map(
        whole,
        mesh=mesh,
        in_specs=placed,
        out_specs=(P("grow", "cy", "cz"), P("grow", "cy", "cz"), P(None, "grow", "cy", "cz")),
        check_vma=False,
    )
```

```python
import functools

import jax
import jax.numpy as jnp
from jax import lax
from jax.experimental import pallas as pl
from jax.experimental.pallas import tpu as pltpu
from jax.sharding import PartitionSpec as P

STEPS = 2
SWEEPS = 3


TAU_P = 0.15
TAU_U = 0.08
SHEAR = 1.0
LAME_FIRST = 1.5
STIFF = 6.5
EIGEN = 0.1
COND_EL = 0.1
COND_LI = 0.9
V_HIGH = 1.0
TIME_STEP = 0.05
REST = 0.5
OMEGA_THIRD = 0.1
RATE = 0.5


def extended(cells, sides, width, closed):
    for axis, dim in sides:
        count = lax.axis_size(axis)
        ends = count if closed else count - 1
        head = lax.slice_in_dim(cells, 0, width, axis=dim)
        tail = lax.slice_in_dim(cells, cells.shape[dim] - width, cells.shape[dim], axis=dim)
        cells = jnp.concatenate(
            [
                lax.ppermute(tail, axis, [(i, (i + 1) % count) for i in range(ends)]),
                cells,
                lax.ppermute(head, axis, [((i + 1) % count, i) for i in range(ends)]),
            ],
            axis=dim,
        )
    return cells


def from_behind(block, axis, distance):
    devices = range(lax.axis_size(axis))
    route = [(i - distance, i) for i in devices if i - distance in devices]
    return lax.ppermute(block, axis, route)


def unit(direction, sign):
    offsets = [0, 0, 0]
    offsets[direction] = sign
    return offsets


def offset(field, offsets):
    lead_dims = field.ndim - 3
    slices = [slice(None)] * lead_dims
    for direction in range(3):
        extent = field.shape[lead_dims + direction]
        slices.append(slice(1 + offsets[direction], extent - 1 + offsets[direction]))
    return field[tuple(slices)]


def centre(field):
    return offset(field, (0, 0, 0))


def laplace(field):
    total = -6.0 * centre(field)
    for direction in range(3):
        total = total + offset(field, unit(direction, 1)) + offset(field, unit(direction, -1))
    return total


def interp(phase):
    return phase * phase * (3.0 - 2.0 * phase)


def interp_slope(phase):
    return 6.0 * phase * (1.0 - phase)


def potential_sweep(potential_pad, conduct_pad):
    here = centre(potential_pad)
    conduct_here = centre(conduct_pad)
    flux = jnp.zeros_like(here)
    for direction in range(3):
        for sign in (1, -1):
            moved = unit(direction, sign)
            flux = flux + 0.5 * (offset(conduct_pad, moved) + conduct_here) * (
                offset(potential_pad, moved) - here
            )
    return here + TAU_P * flux


def cross_term(field, first, second):
    total = jnp.zeros_like(centre(field))
    for sign_first in (1, -1):
        for sign_second in (1, -1):
            offsets = [0, 0, 0]
            offsets[first] = sign_first
            offsets[second] = sign_second
            total = total + sign_first * sign_second * offset(field, offsets)
    return 0.25 * total


def elastic_sweep(disp_pad, interp_pad):
    updated = []
    for component in range(3):
        own = disp_pad[component]
        grad_div = (
            offset(own, unit(component, 1)) - 2.0 * centre(own) + offset(own, unit(component, -1))
        )
        for other in range(3):
            if other != component:
                grad_div = grad_div + cross_term(disp_pad[other], component, other)
        slope = 0.5 * (
            offset(interp_pad, unit(component, 1)) - offset(interp_pad, unit(component, -1))
        )
        force = SHEAR * laplace(own) + (LAME_FIRST + SHEAR) * grad_div - STIFF * EIGEN * slope
        updated.append(centre(own) + TAU_U * force)
    return jnp.stack(updated)


def divergence(disp_pad):
    total = jnp.zeros_like(centre(disp_pad[0]))
    for component in range(3):
        total = total + 0.5 * (
            offset(disp_pad[component], unit(component, 1))
            - offset(disp_pad[component], unit(component, -1))
        )
    return total


def phase_update(phase_pad, potential, div_disp):
    phase = centre(phase_pad)
    trace = STIFF * (div_disp - 3.0 * EIGEN * interp(phase))
    over = potential - REST + OMEGA_THIRD * trace
    drive = jnp.exp(over) - jnp.exp(-over)
    change = (
        laplace(phase_pad)
        - 2.0 * phase * (1.0 - phase) * (1.0 - 2.0 * phase)
        - RATE * interp_slope(phase) * drive
    )
    return phase + TIME_STEP * change


def pin_ends(field, width, slab, low, high):
    if width == 0:
        return field
    lead_dims = field.ndim - 3
    planes = field.shape[lead_dims]
    first = lax.axis_index("grow") * slab - width
    position = first + lax.broadcasted_iota(jnp.int32, (planes, 1, 1), 0)
    limit = slab * lax.axis_size("grow")
    result = jnp.where(position < 0, low, field)
    return jnp.where(position >= limit, high, result)


def column_values(values):
    return jnp.array(values, jnp.float32).reshape(len(values), 1, 1, 1)


def strip(field, count):
    for repeat in range(count):
        field = centre(field)
    return field


def shards(labels, roughness, potential, displacement):
    slab = labels.shape[0]
    rim = SWEEPS + 1
    mark = labels.astype(jnp.float32)
    phase = mark * (1.0 - 0.3 * roughness) + (1.0 - mark) * (0.3 * roughness)
    low_five = column_values([1.0, 0.0, 0.0, 0.0, 0.0])
    high_five = column_values([0.0, V_HIGH, 0.0, 0.0, 0.0])
    for step_index in range(STEPS):
        packed = jnp.concatenate([phase[None], potential[None], displacement], axis=0)
        packed = extended(packed, (("grow", 1),), SWEEPS + 1, False)
        packed = pin_ends(packed, SWEEPS + 1, slab, low_five, high_five)
        packed = extended(packed, (("cy", 2), ("cz", 3)), SWEEPS + 1, True)
        phase_pad = packed[0]
        interp_pad = interp(phase_pad)
        conduct_pad = COND_EL + COND_LI * interp_pad
        pot_pad = strip(packed[1], 1)
        conduct_now = centre(conduct_pad)
        for repeat in range(SWEEPS):
            pot_pad = pin_ends(
                potential_sweep(pot_pad, conduct_now), SWEEPS - 1 - repeat, slab, 0.0, V_HIGH
            )
            if repeat + 1 < SWEEPS:
                conduct_now = centre(conduct_now)
        potential = pot_pad
        disp_pad = packed[2:]
        interp_now = interp_pad
        for repeat in range(SWEEPS):
            disp_pad = pin_ends(
                elastic_sweep(disp_pad, interp_now), SWEEPS - repeat, slab, 0.0, 0.0
            )
            if repeat + 1 < SWEEPS:
                interp_now = centre(interp_now)
        div_disp = divergence(disp_pad)
        displacement = centre(disp_pad)
        phase = phase_update(strip(phase_pad, rim - 1), potential, div_disp)
    stacked = jnp.concatenate([phase[None], potential[None], displacement], axis=0)
    arrived = from_behind(stacked, "grow", -1)
    fresh = jnp.array([0.0, V_HIGH, 0.0, 0.0, 0.0], jnp.float32).reshape(5, 1, 1, 1)
    is_last = lax.axis_index("grow") == lax.axis_size("grow") - 1
    arrived = jnp.where(is_last, fresh, arrived)
    return (arrived[0], arrived[1], arrived[2:])


REACH = STEPS * (SWEEPS + 1)
TILE = 8
FIELDS = 5
LAG = 2
TOGETHER = 12


def lanes(shape):
    return lax.broadcasted_iota(jnp.int32, shape, 1)


def from_lane(first):
    lane = lanes((TILE, LANES))
    return jnp.logical_and(lane >= first, lane < first + REACH)


LANES = 128


def turned(block, amount):
    return pltpu.roll(block, lax.rem(amount + 2 * LANES, LANES), 1)


def half_of(side):
    low = lanes((TILE, LANES)) < LANES // 2
    return jnp.logical_xor(low, side == 1)


def pack_halves(fields, upper, lower, mid, theirs, out):
    _, slab, _, _ = fields.shape
    for field in range(FIELDS):
        for plane in range(slab):
            for row in range(0, mid, TILE):
                one = fields[field, plane, pl.ds(upper + row, TILE), :]
                two = fields[field, plane, pl.ds(lower + row, TILE), :]
                to = pl.ds((field * slab + plane) * mid + row, TILE)
                out[to, :] = jnp.where(theirs, one, turned(two, LANES // 2))


def pack_strips(fields, base, out, start):
    _, slab, rows, _ = fields.shape
    for field in range(FIELDS):
        for plane in range(slab):
            packed = jnp.zeros((TILE, LANES), jnp.float32)
            for group in range(rows // TILE):
                block = fields[field, plane, pl.ds(group * TILE, TILE), :]
                block = turned(block, group * REACH - base)
                packed = jnp.where(from_lane(group * REACH), block, packed)
            out[pl.ds(start + (field * slab + plane) * TILE, TILE), :] = packed


def pack_rim_strips(above, below, base, out, start):
    per = LANES // REACH
    blocks = 2 * above.shape[0] // TILE
    for first in range(0, blocks, per):
        packed = jnp.zeros((TILE, LANES), jnp.float32)
        for which in range(first, min(first + per, blocks)):
            block = (above, below)[which % 2][pl.ds(which // 2 * TILE, TILE), :]
            to = which % per * REACH
            packed = jnp.where(from_lane(to), turned(block, to - base), packed)
        out[pl.ds(start + first // per * TILE, TILE), :] = packed


def strip_bases(side):
    outer = LANES - REACH
    return LANES // 2 - REACH + REACH * side, outer * (1 - side), outer * side


def split(rows):
    return rows // 4 - REACH, 3 * rows // 4 + REACH


def prepare_kernel(
    labels, roughness, potential, displacement,
    fields, halves, same, other, first, last, marks, rough, arrived,
):
    _, slab, rows, _ = fields.shape
    side = lax.axis_index("grow")
    count = FIELDS * slab
    copies = [
        pltpu.make_async_copy(source, target, arrived.at[which])
        for which, (source, target) in enumerate(
            (
                (labels, marks),
                (roughness, rough),
                (potential, fields.at[1]),
                (displacement, fields.at[pl.ds(2, 3)]),
            )
        )
    ]
    for copy in copies:
        copy.start()
    for copy in copies[:2]:
        copy.wait()
    for plane in range(slab):
        for row in range(0, rows, TILE):
            spot = (plane, pl.ds(row, TILE), slice(None))
            mark = marks[spot].astype(jnp.float32)
            part = 0.3 * rough[spot]
            fields[(0,) + spot] = mark * (1.0 - part) + (1.0 - mark) * part
    for copy in copies[2:]:
        copy.wait()
    start, stop = split(rows)
    mid = (stop - start) // 2
    pack_halves(fields, start, start + mid, mid, jnp.logical_not(half_of(side)), halves)
    for out, at, base in zip((halves, same, other), (count * mid, 0, 0), strip_bases(side)):
        pack_strips(fields, base, out, at)
    for field in range(FIELDS):
        for plane in range(slab):
            spot = pl.ds((field * slab + plane) * TILE, TILE)
            first[spot, :] = fields[field, plane, pl.ds(0, TILE), :]
            last[spot, :] = fields[field, plane, pl.ds(rows - TILE, TILE), :]


def rims_kernel(fields, other_first, same_first, above, below, halves, same, other):
    _, slab, rows, _ = fields.shape
    side = lax.axis_index("grow")
    theirs = jnp.logical_not(half_of(side))
    count = FIELDS * slab
    start, stop = split(rows)
    pack_halves(fields, 0, stop, start, theirs, halves)
    for which in range(count):
        spot = pl.ds(which * TILE, TILE)
        rims = jnp.where(theirs, above[spot, :], turned(below[spot, :], LANES // 2))
        halves[pl.ds(count * start + which * TILE, TILE), :] = rims
    starts = (count * (start + TILE), 0, 0)
    for out, at, base in zip((halves, same, other), starts, strip_bases(side)):
        pack_rim_strips(above, below, base, out, at)


def blocks_of(part, rows):
    start, stop = split(rows)
    if part == 0:
        return list(range(start, stop, TILE))
    inner = start + 2 * REACH
    return list(range(-REACH, inner, TILE)) + list(range(rows - inner, rows + REACH, TILE))


def packed_at(which, row, rows, count):
    if 0 <= row < rows:
        return False, which * TILE, row // TILE * REACH
    at, group = divmod(2 * which + int(row > 0), LANES // REACH)
    return True, at * TILE, group * REACH


def own_kernel(part, fields, *refs):
    out, natural = refs[-2:]
    same, *more = refs[:-2]
    same_rims, above, below, _ = more or (None,) * 4
    _, slab, rows, _ = fields.shape
    count = FIELDS * slab
    outer = (LANES - REACH) * (1 - lax.axis_index("grow"))
    in_outer = from_lane(outer)
    segment = out.shape[2] - 2
    for field in range(FIELDS):
        for plane in range(slab):
            which = field * slab + plane
            for at, row in enumerate(blocks_of(part, rows)):
                of_rim, spot, lane = packed_at(which, row, rows, count)
                piece = (same_rims if of_rim else same)[pl.ds(spot, TILE), :]
                if of_rim:
                    near = (below if row > 0 else above)[pl.ds(which * TILE, TILE), :]
                else:
                    near = fields[field, plane, pl.ds(row, TILE), :]
                near = jnp.where(in_outer, turned(piece, outer - lane), near)
                natural[which, pl.ds(at * TILE, TILE), :] = near
            blocks = [natural[which, pl.ds(row, TILE, stride=segment), :] for row in range(segment)]
            blocks = [pltpu.roll(blocks[-1], 1, 0), *blocks, pltpu.roll(blocks[0], TILE - 1, 0)]
            for row, block in enumerate(blocks):
                out[field, plane, row] = block


def conduct_of(step):
    return COND_EL + COND_LI * step


def steps_kernel(part, near, other, halves, *refs):
    if part:
        other_rims, rest, _, *refs = refs
    result, message, natural, phase, phase_new, pot, pot_new, disp, disp_new = refs[:9]
    slopes, slopes_y, cond_x, cond_y, cond_y_back, cond_z = refs[9:]
    _, slab, rows, _ = result.shape
    all_rows = 2 * rows
    planes = 2 * slab
    side = lax.axis_index("grow")
    mine = half_of(side)
    count = FIELDS * slab
    inner = LANES // 2 - REACH * side
    outer = (LANES - REACH) * (1 - side)
    in_inner, in_outer = from_lane(inner), from_lane(outer)
    segment = phase.shape[1] - 2
    start, stop = split(all_rows)
    half = (stop - start) // 2
    blocks = blocks_of(part, all_rows)

    def arrived_half(which, row):
        if start <= row < stop:
            block = halves[pl.ds(which * half + (row - start) % half, TILE), :]
            return turned(block, LANES // 2) if row - start >= half else block
        if 0 <= row < all_rows:
            block = rest[pl.ds(which * start + row % stop, TILE), :]
        else:
            block = rest[pl.ds(count * start + which * TILE, TILE), :]
        return turned(block, LANES // 2) if row > 0 and row >= stop else block

    for field in range(FIELDS):
        for plane in range(slab):
            which = field * slab + plane
            for at, row in enumerate(blocks):
                of_rim, spot, lane = packed_at(which, row, all_rows, count)
                if of_rim:
                    strip = rest[pl.ds(count * (start + TILE) + spot, TILE), :]
                    beside = other_rims[pl.ds(spot, TILE), :]
                else:
                    strip = halves[pl.ds(count * half + spot, TILE), :]
                    beside = other[pl.ds(spot, TILE), :]
                block = jnp.where(in_inner, turned(strip, inner - lane), arrived_half(which, row))
                block = jnp.where(in_outer, turned(beside, outer - lane), block)
                natural[field, plane, pl.ds(at * TILE, TILE), :] = block

    def parts_of(phase, pot, disp):
        return (phase, pot, disp.at[0], disp.at[1], disp.at[2])

    def close(ref):
        for plane in range(planes):
            ref[plane, 0] = pltpu.roll(ref[plane, segment], 1, 0)
            ref[plane, segment + 1] = pltpu.roll(ref[plane, 1], TILE - 1, 0)

    for field, ref in enumerate(parts_of(phase, pot, disp)):
        for plane in range(slab):
            own, far = side * slab + plane, (1 - side) * slab + plane
            for row in range(segment + 2):
                ref[own, row] = near[field, plane, row]
            for row in range(segment):
                ref[far, 1 + row] = natural[field, plane, pl.ds(row, TILE, stride=segment), :]
            ref[far, 0] = pltpu.roll(ref[far, segment], 1, 0)
            ref[far, segment + 1] = pltpu.roll(ref[far, 1], TILE - 1, 0)

    def one_row(row, bodies):
        waiting = []
        running = [body(row) for body in bodies]
        while running:
            for body in list(running):
                stores = next(body, None)
                if stores is None:
                    running.remove(body)
                else:
                    waiting.append(stores)
            while len(waiting) > LAG * len(bodies) or (waiting and not running):
                for ref, lead, value in waiting.pop(0):
                    ref[lead + (row,)] = value

    def over_rows(*bodies):
        together = max(n for n in range(1, TOGETHER + 1) if segment % n == 0)

        def some(turn, carry):
            for more in range(together):
                one_row(1 + turn * together + more, bodies)
            return carry

        if together == segment:
            some(0, 0)
        else:
            lax.fori_loop(0, segment // together, some, 0)

    def up(block):
        return pltpu.roll(block, LANES - 1, 1)

    def down(block):
        return pltpu.roll(block, 1, 1)

    push = 0.5 * TAU_U * STIFF * EIGEN

    def conduct_pass(source):
        def body(row):
            face = 0.5 * TAU_P
            before = conduct_of(1.0)
            for plane in range(planes):
                step, ahead, back = (interp(source[plane, row + shift]) for shift in (0, 1, -1))
                here = conduct_of(step)
                yield [
                    (slopes, (plane,), push * step),
                    (slopes_y, (plane,), push * (ahead - back)),
                    (cond_x, (plane,), face * (before + here)),
                    (cond_y, (plane,), face * (here + conduct_of(ahead))),
                    (cond_y_back, (plane,), face * (here + conduct_of(back))),
                    (cond_z, (plane,), face * (here + up(here))),
                ]
                before = here
            yield [(cond_x, (planes,), face * (before + conduct_of(0.0)))]

        return body

    def potential_pass(old, new, low):
        def body(row):
            here = old[low, row]
            before = old[low - 1, row] if low else 0.0
            entering = cond_x[low, row] * (here - before)
            for plane in range(low, planes):
                after = old[plane + 1, row] if plane + 1 < planes else V_HIGH
                leaving = cond_x[plane + 1, row] * (after - here)
                along_y = cond_y[plane, row] * (old[plane, row + 1] - here)
                along_y -= cond_y_back[plane, row] * (here - old[plane, row - 1])
                along_z = cond_z[plane, row] * (up(here) - here)
                along_z -= down(along_z)
                yield [(new, (plane,), here + ((leaving - entering) + along_y + along_z))]
                here, entering = after, leaving

        return body

    grad = LAME_FIRST + SHEAR
    cross = 0.25 * TAU_U * grad
    side_on = TAU_U * SHEAR
    head_on = TAU_U * (SHEAR + grad)
    keep = 1.0 - TAU_U * (6.0 * SHEAR + 2.0 * grad)

    def elastic_pass(old, new, low):
        def body(row):
            def load(plane):
                if plane < 0 or plane >= planes:
                    return (0.0,) * 3, (0.0,) * 3, (0.0,) * 3, -push if plane < 0 else 0.0
                parts = [old[part, plane, row] for part in range(3)]
                ahead = [old[part, plane, row + 1] for part in range(3)]
                back = [old[part, plane, row - 1] for part in range(3)]
                sums = [one + two for one, two in zip(ahead, back)]
                diffs = [one - two for one, two in zip(ahead, back)]
                return parts, sums, diffs, cross * diffs[1] - slopes[plane, row]

            before, here = load(low - 1), load(low)
            for plane in range(low, planes):
                after = load(plane + 1)
                (a, b, c), sums, diffs, slope = here
                sum_x = [one + two for one, two in zip(after[0], before[0])]
                lift = cross * (after[0][2] - before[0][2])
                mid_a = side_on * a
                new_a = (
                    keep * a
                    + head_on * sum_x[0]
                    + side_on * sums[0]
                    + (up(mid_a + lift) + down(mid_a - lift))
                    + (after[3] - before[3])
                )
                lift = cross * diffs[2]
                mid_b = side_on * b
                new_b = (
                    keep * b
                    + head_on * sums[1]
                    + side_on * sum_x[1]
                    + (up(mid_b + lift) + down(mid_b - lift))
                    + (cross * (after[2][0] - before[2][0]) - slopes_y[plane, row])
                )
                lift = cross * (after[0][0] - before[0][0]) + slope
                mid_c = head_on * c
                new_c = (
                    keep * c
                    + side_on * (sum_x[2] + sums[2])
                    + (up(mid_c + lift) + down(mid_c - lift))
                )
                yield [(new, (part, plane), value) for part, value in enumerate((new_a, new_b, new_c))]
                before, here = here, after

        return body

    def phase_pass(source, pot_now, disp_now, low, new):
        def body(row):
            def load(plane):
                if plane < 0 or plane >= planes:
                    return (1.0 if plane < 0 else 0.0, 0.0)
                return (source[plane, row], disp_now[0, plane, row])

            before, here = load(low - 1), load(low)
            for plane in range(low, planes):
                after = load(plane + 1)
                p = here[0]
                c = disp_now[2, plane, row]
                div = (
                    (after[1] - before[1])
                    + (disp_now[1, plane, row + 1] - disp_now[1, plane, row - 1])
                    + (up(c) - down(c))
                )
                over = (
                    (pot_now[plane, row] - REST)
                    + (0.5 * OMEGA_THIRD * STIFF) * div
                    - (OMEGA_THIRD * STIFF * 3.0 * EIGEN) * interp(p)
                )
                drive = jnp.exp(over) - jnp.exp(-over)
                lap = (
                    (before[0] + after[0])
                    + (source[plane, row + 1] + source[plane, row - 1])
                    + (up(p) + down(p))
                    - 6.0 * p
                )
                well = p * (1.0 - p)
                change = lap - well * (2.0 * (1.0 - 2.0 * p) + (6.0 * RATE) * drive)
                yield [(new, (plane,), p + TIME_STEP * change)]
                before, here = here, after

        return body

    for step in range(STEPS):
        last = step == STEPS - 1
        over_rows(conduct_pass(phase))
        for sweep in range(SWEEPS):
            ahead = SWEEPS - 1 - sweep
            over_rows(
                potential_pass(pot, pot_new, max(0, slab - ahead) if last else 0),
                elastic_pass(disp, disp_new, max(0, slab - ahead - 1) if last else 0),
            )
            pot, pot_new, disp, disp_new = pot_new, pot, disp_new, disp
            for ref in (pot, disp.at[0], disp.at[1], disp.at[2]):
                close(ref)
        over_rows(phase_pass(phase, pot, disp, slab if last else 0, phase_new))
        phase, phase_new = phase_new, phase
        if not last:
            close(phase)
    outs = results_of(part, all_rows)
    for field, ref in enumerate(parts_of(phase, pot, disp)):
        for plane in range(slab):
            for row in range(segment):
                to = pl.ds(row, TILE, stride=segment)
                natural[field, plane, to, :] = ref[slab + plane, 1 + row]
            for at in range(len(outs) // 2):
                pair = []
                for place in (at, at + len(outs) // 2):
                    spot = pl.ds(blocks.index(outs[place]) * TILE, TILE)
                    pair.append(natural[field, plane, spot, :])
                    result[field, plane, pl.ds(place * TILE, TILE), :] = pair[-1]
                to = pl.ds(((field * slab + plane) * len(outs) // 2 + at) * TILE, TILE)
                message[to, :] = jnp.where(mine, pair[0], turned(pair[1], LANES // 2))


def results_of(part, rows):
    quarter = rows // 4
    if part == 0:
        return list(range(quarter, 3 * quarter, TILE))
    return list(range(0, quarter, TILE)) + list(range(3 * quarter, rows, TILE))


def finish_kernel(part, result, message, *refs):
    phase, potential, displacement, whole, arrived = refs[3 * part :]
    _, slab, rows, _ = result.shape
    side = lax.axis_index("grow")
    mine = half_of(side)
    fresh = side == lax.axis_size("grow") - 1
    half = rows // 2
    copies = []
    for field in range(FIELDS):
        for plane in range(slab):
            for row in range(0, rows, TILE):
                spot = pl.ds((field * slab + plane) * half + row % half, TILE)
                block = message[spot, :]
                block = turned(block, LANES // 2) if row >= half else block
                block = jnp.where(mine, result[field, plane, pl.ds(row, TILE), :], block)
                block = jnp.where(fresh, V_HIGH if field == 1 else 0.0, block)
                whole[field, plane, pl.ds(row, TILE), :] = block
        out = (phase, potential, displacement.at[0], displacement.at[1], displacement.at[2])[field]
        for source, target in (((0, 0), (half, 3 * half)) if part else ((0, half), (half, rows))):
            copy = pltpu.make_async_copy(
                whole.at[field, :, pl.ds(source, half), :],
                out.at[:, pl.ds(target, half), :],
                arrived.at[len(copies)],
            )
            copy.start()
            copies.append(copy)
    for copy in copies:
        copy.wait()


def call(kernel, outs, scratch=(), limit=48, **how):
    return pl.pallas_call(
        kernel,
        out_shape=[
            jax.ShapeDtypeStruct(one, jnp.float32) if isinstance(one, tuple) else one for one in outs
        ],
        scratch_shapes=[
            pltpu.VMEM(one, jnp.float32) if isinstance(one, tuple) else one for one in scratch
        ],
        **{"cost_estimate": pl.CostEstimate(flops=1, bytes_accessed=1, transcendentals=0), **how},
        compiler_params=pltpu.CompilerParams(vmem_limit_bytes=limit * 1024 * 1024),
    )


def pair_shards(labels, roughness, potential, displacement):
    slab, rows, _ = labels.shape
    count = FIELDS * slab
    start, stop = split(rows)
    half = (stop - start) // 2
    spare = -(-2 * count * REACH // LANES) * TILE
    sizes = {name: lax.axis_size(name) for name in ("grow", "cy", "cz")}

    def index(grow, cy, cz):
        cy, cz = cy % sizes["cy"], cz % sizes["cz"]
        return (grow * sizes["cy"] + cy) * sizes["cz"] + cz

    everyone = [
        (grow, cy, cz)
        for grow in range(sizes["grow"])
        for cy in range(sizes["cy"])
        for cz in range(sizes["cz"])
    ]

    def send(block, route):
        pairs = [(index(*at), index(*route(*at))) for at in everyone]
        return lax.ppermute(block, ("grow", "cy", "cz"), pairs)

    def to_partner(block):
        return send(block, lambda grow, cy, cz: (1 - grow, cy, cz))

    def beside_same(block):
        return send(block, lambda grow, cy, cz: (grow, cy, cz - 1 if grow else cz + 1))

    def beside_other(block):
        return send(block, lambda grow, cy, cz: (1 - grow, cy, cz + 1 if grow else cz - 1))

    in_vmem, anywhere, hbm = (
        pl.BlockSpec(memory_space=space) for space in (pltpu.VMEM, pl.ANY, pltpu.HBM)
    )
    thin = (count * TILE, LANES)
    fields, halves, same, other, first, last = call(
        prepare_kernel,
        [
            pltpu.VMEM(shape, jnp.float32)
            for shape in ((FIELDS,) + labels.shape, (count * (half + TILE), LANES), *[thin] * 4)
        ],
        [pltpu.VMEM(labels.shape, labels.dtype), labels.shape, pltpu.SemaphoreType.DMA((4,))],
        limit=54,
        in_specs=[hbm] * 4,
    )(labels, roughness, potential, displacement)
    halves = to_partner(halves)
    other = beside_other(other)
    above = send(last, lambda grow, cy, cz: (grow, cy + 1, cz))
    below = send(first, lambda grow, cy, cz: (grow, cy - 1, cz))
    same = beside_same(same)
    rest, same_rims, other_rims = call(
        rims_kernel,
        [(count * (start + TILE) + spare, LANES)] + [(spare, LANES)] * 2,
        in_specs=[in_vmem] + [anywhere] * 2 + [in_vmem] * 2,
    )(fields, other, same, above, below)
    rest = to_partner(rest)
    other_rims = beside_other(other_rims)
    same_rims = beside_same(same_rims)
    results, messages, outs = [], [], []
    for part in range(2):
        span = len(blocks_of(part, rows)) * TILE
        deep = (2 * slab, span // TILE + 2, TILE, LANES)
        (near,) = call(
            functools.partial(own_kernel, part),
            [(FIELDS, slab) + deep[1:]],
            [(count, span, LANES)],
            in_specs=[in_vmem] * (2 + 3 * part) + [anywhere] * part,
        )(fields, same, *([same_rims, above, below, *results] if part else []))
        result, message = call(
            functools.partial(steps_kernel, part),
            [(FIELDS, slab, rows // 2, LANES), (count * rows // 4, LANES)],
            [(FIELDS, slab, span, LANES)]
            + [deep] * 4
            + [(3,) + deep] * 2
            + [deep, deep, (2 * slab + 1,) + deep[1:], deep, deep, deep],
            in_specs=[in_vmem] * (3 + 2 * part) + [anywhere] * part,
            cost_estimate=pl.CostEstimate(
                flops=STEPS * SWEEPS * 160 * span * 2 * slab * LANES,
                bytes_accessed=STEPS * SWEEPS * 40 * span * 2 * slab * LANES,
                transcendentals=STEPS * 2 * span * 2 * slab * LANES,
            ),
        )(near, other, halves, *([other_rims, rest, *results] if part else []))
        results.append(result)
        messages.append(from_behind(message, "grow", -1))
    for part in range(2):
        outs = call(
            functools.partial(finish_kernel, part),
            [labels.shape, labels.shape, displacement.shape],
            [(FIELDS, slab, rows // 2, LANES), pltpu.SemaphoreType.DMA((2 * FIELDS,))],
            in_specs=[in_vmem] * 2 + [hbm] * (3 * part),
            out_specs=[hbm] * 3,
            input_output_aliases={2 + which: which for which in range(3 * part)},
        )(results[part], messages[part], *outs)
    return outs


def fits_pair(labels):
    rows, columns = labels.shape[1:]
    blocks = rows % (8 * TILE) == 0 and rows // TILE * REACH <= LANES
    return lax.axis_size("grow") == 2 and columns == LANES and REACH == TILE and blocks


def whole(labels, roughness, potential, displacement):
    plan = pair_shards if fits_pair(labels) else shards
    return tuple(plan(labels, roughness, potential, displacement))


def solution(mesh):
    placed = (
        P("grow", "cy", "cz"),
        P("grow", "cy", "cz"),
        P("grow", "cy", "cz"),
        P(None, "grow", "cy", "cz"),
    )
    return jax.shard_map(
        whole,
        mesh=mesh,
        in_specs=placed,
        out_specs=(P("grow", "cy", "cz"), P("grow", "cy", "cz"), P(None, "grow", "cy", "cz")),
        check_vma=False,
    )
```

```python
import functools

import jax
import jax.numpy as jnp
from jax import lax
from jax.experimental import pallas as pl
from jax.experimental.pallas import tpu as pltpu
from jax.sharding import PartitionSpec as P

STEPS = 2
SWEEPS = 3


TAU_P = 0.15
TAU_U = 0.08
SHEAR = 1.0
LAME_FIRST = 1.5
STIFF = 6.5
EIGEN = 0.1
COND_EL = 0.1
COND_LI = 0.9
V_HIGH = 1.0
TIME_STEP = 0.05
REST = 0.5
OMEGA_THIRD = 0.1
RATE = 0.5


def extended(cells, sides, width, closed):
    for axis, dim in sides:
        count = lax.axis_size(axis)
        ends = count if closed else count - 1
        head = lax.slice_in_dim(cells, 0, width, axis=dim)
        tail = lax.slice_in_dim(cells, cells.shape[dim] - width, cells.shape[dim], axis=dim)
        cells = jnp.concatenate(
            [
                lax.ppermute(tail, axis, [(i, (i + 1) % count) for i in range(ends)]),
                cells,
                lax.ppermute(head, axis, [((i + 1) % count, i) for i in range(ends)]),
            ],
            axis=dim,
        )
    return cells


def from_behind(block, axis, distance):
    devices = range(lax.axis_size(axis))
    route = [(i - distance, i) for i in devices if i - distance in devices]
    return lax.ppermute(block, axis, route)


def unit(direction, sign):
    offsets = [0, 0, 0]
    offsets[direction] = sign
    return offsets


def offset(field, offsets):
    lead_dims = field.ndim - 3
    slices = [slice(None)] * lead_dims
    for direction in range(3):
        extent = field.shape[lead_dims + direction]
        slices.append(slice(1 + offsets[direction], extent - 1 + offsets[direction]))
    return field[tuple(slices)]


def centre(field):
    return offset(field, (0, 0, 0))


def laplace(field):
    total = -6.0 * centre(field)
    for direction in range(3):
        total = total + offset(field, unit(direction, 1)) + offset(field, unit(direction, -1))
    return total


def interp(phase):
    return phase * phase * (3.0 - 2.0 * phase)


def interp_slope(phase):
    return 6.0 * phase * (1.0 - phase)


def potential_sweep(potential_pad, conduct_pad):
    here = centre(potential_pad)
    conduct_here = centre(conduct_pad)
    flux = jnp.zeros_like(here)
    for direction in range(3):
        for sign in (1, -1):
            moved = unit(direction, sign)
            flux = flux + 0.5 * (offset(conduct_pad, moved) + conduct_here) * (
                offset(potential_pad, moved) - here
            )
    return here + TAU_P * flux


def cross_term(field, first, second):
    total = jnp.zeros_like(centre(field))
    for sign_first in (1, -1):
        for sign_second in (1, -1):
            offsets = [0, 0, 0]
            offsets[first] = sign_first
            offsets[second] = sign_second
            total = total + sign_first * sign_second * offset(field, offsets)
    return 0.25 * total


def elastic_sweep(disp_pad, interp_pad):
    updated = []
    for component in range(3):
        own = disp_pad[component]
        grad_div = (
            offset(own, unit(component, 1)) - 2.0 * centre(own) + offset(own, unit(component, -1))
        )
        for other in range(3):
            if other != component:
                grad_div = grad_div + cross_term(disp_pad[other], component, other)
        slope = 0.5 * (
            offset(interp_pad, unit(component, 1)) - offset(interp_pad, unit(component, -1))
        )
        force = SHEAR * laplace(own) + (LAME_FIRST + SHEAR) * grad_div - STIFF * EIGEN * slope
        updated.append(centre(own) + TAU_U * force)
    return jnp.stack(updated)


def divergence(disp_pad):
    total = jnp.zeros_like(centre(disp_pad[0]))
    for component in range(3):
        total = total + 0.5 * (
            offset(disp_pad[component], unit(component, 1))
            - offset(disp_pad[component], unit(component, -1))
        )
    return total


def phase_update(phase_pad, potential, div_disp):
    phase = centre(phase_pad)
    trace = STIFF * (div_disp - 3.0 * EIGEN * interp(phase))
    over = potential - REST + OMEGA_THIRD * trace
    drive = jnp.exp(over) - jnp.exp(-over)
    change = (
        laplace(phase_pad)
        - 2.0 * phase * (1.0 - phase) * (1.0 - 2.0 * phase)
        - RATE * interp_slope(phase) * drive
    )
    return phase + TIME_STEP * change


def pin_ends(field, width, slab, low, high):
    if width == 0:
        return field
    lead_dims = field.ndim - 3
    planes = field.shape[lead_dims]
    first = lax.axis_index("grow") * slab - width
    position = first + lax.broadcasted_iota(jnp.int32, (planes, 1, 1), 0)
    limit = slab * lax.axis_size("grow")
    result = jnp.where(position < 0, low, field)
    return jnp.where(position >= limit, high, result)


def column_values(values):
    return jnp.array(values, jnp.float32).reshape(len(values), 1, 1, 1)


def strip(field, count):
    for repeat in range(count):
        field = centre(field)
    return field


def shards(labels, roughness, potential, displacement):
    slab = labels.shape[0]
    rim = SWEEPS + 1
    mark = labels.astype(jnp.float32)
    phase = mark * (1.0 - 0.3 * roughness) + (1.0 - mark) * (0.3 * roughness)
    low_five = column_values([1.0, 0.0, 0.0, 0.0, 0.0])
    high_five = column_values([0.0, V_HIGH, 0.0, 0.0, 0.0])
    for step_index in range(STEPS):
        packed = jnp.concatenate([phase[None], potential[None], displacement], axis=0)
        packed = extended(packed, (("grow", 1),), SWEEPS + 1, False)
        packed = pin_ends(packed, SWEEPS + 1, slab, low_five, high_five)
        packed = extended(packed, (("cy", 2), ("cz", 3)), SWEEPS + 1, True)
        phase_pad = packed[0]
        interp_pad = interp(phase_pad)
        conduct_pad = COND_EL + COND_LI * interp_pad
        pot_pad = strip(packed[1], 1)
        conduct_now = centre(conduct_pad)
        for repeat in range(SWEEPS):
            pot_pad = pin_ends(
                potential_sweep(pot_pad, conduct_now), SWEEPS - 1 - repeat, slab, 0.0, V_HIGH
            )
            if repeat + 1 < SWEEPS:
                conduct_now = centre(conduct_now)
        potential = pot_pad
        disp_pad = packed[2:]
        interp_now = interp_pad
        for repeat in range(SWEEPS):
            disp_pad = pin_ends(
                elastic_sweep(disp_pad, interp_now), SWEEPS - repeat, slab, 0.0, 0.0
            )
            if repeat + 1 < SWEEPS:
                interp_now = centre(interp_now)
        div_disp = divergence(disp_pad)
        displacement = centre(disp_pad)
        phase = phase_update(strip(phase_pad, rim - 1), potential, div_disp)
    stacked = jnp.concatenate([phase[None], potential[None], displacement], axis=0)
    arrived = from_behind(stacked, "grow", -1)
    fresh = jnp.array([0.0, V_HIGH, 0.0, 0.0, 0.0], jnp.float32).reshape(5, 1, 1, 1)
    is_last = lax.axis_index("grow") == lax.axis_size("grow") - 1
    arrived = jnp.where(is_last, fresh, arrived)
    return (arrived[0], arrived[1], arrived[2:])


REACH = STEPS * (SWEEPS + 1)
TILE = 8
FIELDS = 5
PER_TILE = 1
LAG = 2
TOGETHER = 12


def lanes(shape):
    return lax.broadcasted_iota(jnp.int32, shape, 1)


def from_lane(first):
    lane = lanes((TILE, LANES))
    return jnp.logical_and(lane >= first, lane < first + REACH)


LANES = 128


def turned(block, amount):
    return pltpu.roll(block, lax.rem(amount + 2 * LANES, LANES), 1)


def half_of(side):
    low = lanes((TILE, LANES)) < LANES // 2
    return jnp.logical_xor(low, side == 1)


def pack_halves(fields, upper, lower, mid, theirs, out):
    _, slab, _, _ = fields.shape
    for field in range(FIELDS):
        for plane in range(slab):
            for row in range(0, mid, TILE):
                one = fields[field, plane, pl.ds(upper + row, TILE), :]
                two = fields[field, plane, pl.ds(lower + row, TILE), :]
                to = pl.ds((field * slab + plane) * mid + row, TILE)
                out[to, :] = jnp.where(theirs, one, turned(two, LANES // 2))


def pack_strips(fields, base, out, start):
    _, slab, rows, _ = fields.shape
    for field in range(FIELDS):
        for plane in range(slab):
            packed = jnp.zeros((TILE, LANES), jnp.float32)
            for group in range(rows // TILE):
                block = fields[field, plane, pl.ds(group * TILE, TILE), :]
                block = turned(block, group * REACH - base)
                packed = jnp.where(from_lane(group * REACH), block, packed)
            out[pl.ds(start + (field * slab + plane) * TILE, TILE), :] = packed


def pack_rim_strips(above, below, base, out, start, per):
    blocks = 2 * above.shape[0] // TILE
    for first in range(0, blocks, per):
        packed = jnp.zeros((TILE, LANES), jnp.float32)
        for which in range(first, min(first + per, blocks)):
            block = (above, below)[which % 2][pl.ds(which // 2 * TILE, TILE), :]
            to = which % per * REACH
            packed = jnp.where(from_lane(to), turned(block, to - base), packed)
        out[pl.ds(start + first // per * TILE, TILE), :] = packed


def strip_bases(side):
    outer = LANES - REACH
    return LANES // 2 - REACH + REACH * side, outer * (1 - side), outer * side


def split(rows):
    edge = rows // TILE * 3 // 16 * TILE
    return edge - REACH, rows - edge + REACH


def prepare_kernel(
    labels, roughness, potential, displacement,
    fields, halves, same, other, first, last, marks, rough, arrived,
):
    _, slab, rows, _ = fields.shape
    side = lax.axis_index("grow")
    count = FIELDS * slab
    copies = [
        pltpu.make_async_copy(source, target, arrived.at[which])
        for which, (source, target) in enumerate(
            (
                (labels, marks),
                (roughness, rough),
                (potential, fields.at[1]),
                (displacement, fields.at[pl.ds(2, 3)]),
            )
        )
    ]
    for copy in copies:
        copy.start()
    for copy in copies[:2]:
        copy.wait()
    for plane in range(slab):
        for row in range(0, rows, TILE):
            spot = (plane, pl.ds(row, TILE), slice(None))
            mark = marks[spot].astype(jnp.float32)
            part = 0.3 * rough[spot]
            fields[(0,) + spot] = mark * (1.0 - part) + (1.0 - mark) * part
    for copy in copies[2:]:
        copy.wait()
    start, stop = split(rows)
    mid = (stop - start) // 2
    pack_halves(fields, start, start + mid, mid, jnp.logical_not(half_of(side)), halves)
    for out, at, base in zip((halves, same, other), (count * mid, 0, 0), strip_bases(side)):
        pack_strips(fields, base, out, at)
    for field in range(FIELDS):
        for plane in range(slab):
            spot = pl.ds((field * slab + plane) * TILE, TILE)
            first[spot, :] = fields[field, plane, pl.ds(0, TILE), :]
            last[spot, :] = fields[field, plane, pl.ds(rows - TILE, TILE), :]


def rims_kernel(fields, other_first, same_first, above, below, halves, same, other):
    _, slab, rows, _ = fields.shape
    side = lax.axis_index("grow")
    theirs = jnp.logical_not(half_of(side))
    count = FIELDS * slab
    start, stop = split(rows)
    pack_halves(fields, 0, stop, start, theirs, halves)
    for which in range(count):
        spot = pl.ds(which * TILE, TILE)
        rims = jnp.where(theirs, above[spot, :], turned(below[spot, :], LANES // 2))
        halves[pl.ds(count * start + which * TILE, TILE), :] = rims
    inner, *outer = strip_bases(side)
    pack_rim_strips(above, below, inner, halves, count * (start + TILE), LANES // REACH)
    for out, base in zip((same, other), outer):
        pack_rim_strips(above, below, base, out, 0, PER_TILE)


def blocks_of(part, rows):
    start, stop = split(rows)
    if part == 0:
        return list(range(start, stop, TILE))
    inner = start + 2 * REACH
    return list(range(-REACH, inner, TILE)) + list(range(rows - inner, rows + REACH, TILE))


def packed_at(which, row, rows, per):
    if 0 <= row < rows:
        return False, which * TILE, row // TILE * REACH
    at, group = divmod(2 * which + int(row > 0), per)
    return True, at * TILE, group * REACH


def own_kernel(part, fields, *refs):
    out, natural = refs[-2:]
    same, *more = refs[:-2]
    same_rims, above, below, _ = more or (None,) * 4
    _, slab, rows, _ = fields.shape
    count = FIELDS * slab
    outer = (LANES - REACH) * (1 - lax.axis_index("grow"))
    in_outer = from_lane(outer)
    segment = out.shape[2] - 2
    for field in range(FIELDS):
        for plane in range(slab):
            which = field * slab + plane
            for at, row in enumerate(blocks_of(part, rows)):
                of_rim, spot, lane = packed_at(which, row, rows, PER_TILE)
                piece = (same_rims if of_rim else same)[pl.ds(spot, TILE), :]
                if of_rim:
                    near = (below if row > 0 else above)[pl.ds(which * TILE, TILE), :]
                else:
                    near = fields[field, plane, pl.ds(row, TILE), :]
                near = jnp.where(in_outer, turned(piece, outer - lane), near)
                natural[which, pl.ds(at * TILE, TILE), :] = near
            blocks = [natural[which, pl.ds(row, TILE, stride=segment), :] for row in range(segment)]
            blocks = [pltpu.roll(blocks[-1], 1, 0), *blocks, pltpu.roll(blocks[0], TILE - 1, 0)]
            for row, block in enumerate(blocks):
                out[field, plane, row] = block


def conduct_of(step):
    return COND_EL + COND_LI * step


def steps_kernel(part, all_rows, near, other, halves, *refs):
    if part:
        other_rims, rest, _, *refs = refs
    result, message, natural, phase, phase_new, pot, pot_new, disp, disp_new = refs[:9]
    slopes, slopes_y, cond_x, cond_y, cond_y_back, cond_z = refs[9:]
    slab = result.shape[1]
    planes = 2 * slab
    side = lax.axis_index("grow")
    mine = half_of(side)
    count = FIELDS * slab
    inner = LANES // 2 - REACH * side
    outer = (LANES - REACH) * (1 - side)
    in_inner, in_outer = from_lane(inner), from_lane(outer)
    segment = phase.shape[1] - 2
    start, stop = split(all_rows)
    half = (stop - start) // 2
    blocks = blocks_of(part, all_rows)

    def arrived_half(which, row):
        if start <= row < stop:
            block = halves[pl.ds(which * half + (row - start) % half, TILE), :]
            return turned(block, LANES // 2) if row - start >= half else block
        if 0 <= row < all_rows:
            block = rest[pl.ds(which * start + row % stop, TILE), :]
        else:
            block = rest[pl.ds(count * start + which * TILE, TILE), :]
        return turned(block, LANES // 2) if row > 0 and row >= stop else block

    for field in range(FIELDS):
        for plane in range(slab):
            which = field * slab + plane
            for at, row in enumerate(blocks):
                of_rim, spot, lane = packed_at(which, row, all_rows, LANES // REACH)
                back = outer - lane
                if of_rim:
                    strip = rest[pl.ds(count * (start + TILE) + spot, TILE), :]
                    _, spot, beside_lane = packed_at(which, row, all_rows, PER_TILE)
                    beside, back = other_rims[pl.ds(spot, TILE), :], outer - beside_lane
                else:
                    strip = halves[pl.ds(count * half + spot, TILE), :]
                    beside = other[pl.ds(spot, TILE), :]
                block = jnp.where(in_inner, turned(strip, inner - lane), arrived_half(which, row))
                block = jnp.where(in_outer, turned(beside, back), block)
                natural[field, plane, pl.ds(at * TILE, TILE), :] = block

    def parts_of(phase, pot, disp):
        return (phase, pot, disp.at[0], disp.at[1], disp.at[2])

    def close(ref):
        for plane in range(planes):
            ref[plane, 0] = pltpu.roll(ref[plane, segment], 1, 0)
            ref[plane, segment + 1] = pltpu.roll(ref[plane, 1], TILE - 1, 0)

    for field, ref in enumerate(parts_of(phase, pot, disp)):
        for plane in range(slab):
            own, far = side * slab + plane, (1 - side) * slab + plane
            for row in range(segment + 2):
                ref[own, row] = near[field, plane, row]
            for row in range(segment):
                ref[far, 1 + row] = natural[field, plane, pl.ds(row, TILE, stride=segment), :]
            ref[far, 0] = pltpu.roll(ref[far, segment], 1, 0)
            ref[far, segment + 1] = pltpu.roll(ref[far, 1], TILE - 1, 0)

    def one_row(row, bodies):
        waiting = []
        running = [body(row) for body in bodies]
        while running:
            for body in list(running):
                stores = next(body, None)
                if stores is None:
                    running.remove(body)
                else:
                    waiting.append(stores)
            while len(waiting) > LAG * len(bodies) or (waiting and not running):
                for ref, lead, value in waiting.pop(0):
                    ref[lead + (row,)] = value

    def over_rows(*bodies):
        together = max(n for n in range(1, TOGETHER + 1) if segment % n == 0)

        def some(turn, carry):
            for more in range(together):
                one_row(1 + turn * together + more, bodies)
            return carry

        if together == segment:
            some(0, 0)
        else:
            lax.fori_loop(0, segment // together, some, 0)

    def up(block):
        return pltpu.roll(block, LANES - 1, 1)

    def down(block):
        return pltpu.roll(block, 1, 1)

    push = 0.5 * TAU_U * STIFF * EIGEN

    def conduct_pass(source):
        def body(row):
            face = 0.5 * TAU_P
            before = conduct_of(1.0)
            for plane in range(planes):
                step, ahead, back = (interp(source[plane, row + shift]) for shift in (0, 1, -1))
                here = conduct_of(step)
                yield [
                    (slopes, (plane,), push * step),
                    (slopes_y, (plane,), push * (ahead - back)),
                    (cond_x, (plane,), face * (before + here)),
                    (cond_y, (plane,), face * (here + conduct_of(ahead))),
                    (cond_y_back, (plane,), face * (here + conduct_of(back))),
                    (cond_z, (plane,), face * (here + up(here))),
                ]
                before = here
            yield [(cond_x, (planes,), face * (before + conduct_of(0.0)))]

        return body

    def potential_pass(old, new, low):
        def body(row):
            here = old[low, row]
            before = old[low - 1, row] if low else 0.0
            entering = cond_x[low, row] * (here - before)
            for plane in range(low, planes):
                after = old[plane + 1, row] if plane + 1 < planes else V_HIGH
                leaving = cond_x[plane + 1, row] * (after - here)
                along_y = cond_y[plane, row] * (old[plane, row + 1] - here)
                along_y -= cond_y_back[plane, row] * (here - old[plane, row - 1])
                along_z = cond_z[plane, row] * (up(here) - here)
                along_z -= down(along_z)
                yield [(new, (plane,), here + ((leaving - entering) + along_y + along_z))]
                here, entering = after, leaving

        return body

    grad = LAME_FIRST + SHEAR
    cross = 0.25 * TAU_U * grad
    side_on = TAU_U * SHEAR
    head_on = TAU_U * (SHEAR + grad)
    keep = 1.0 - TAU_U * (6.0 * SHEAR + 2.0 * grad)

    def elastic_pass(old, new, low):
        def body(row):
            def load(plane):
                if plane < 0 or plane >= planes:
                    return (0.0,) * 3, (0.0,) * 3, (0.0,) * 3, -push if plane < 0 else 0.0
                parts = [old[part, plane, row] for part in range(3)]
                ahead = [old[part, plane, row + 1] for part in range(3)]
                back = [old[part, plane, row - 1] for part in range(3)]
                sums = [one + two for one, two in zip(ahead, back)]
                diffs = [one - two for one, two in zip(ahead, back)]
                return parts, sums, diffs, cross * diffs[1] - slopes[plane, row]

            before, here = load(low - 1), load(low)
            for plane in range(low, planes):
                after = load(plane + 1)
                (a, b, c), sums, diffs, slope = here
                sum_x = [one + two for one, two in zip(after[0], before[0])]
                lift = cross * (after[0][2] - before[0][2])
                mid_a = side_on * a
                new_a = (
                    keep * a
                    + head_on * sum_x[0]
                    + side_on * sums[0]
                    + (up(mid_a + lift) + down(mid_a - lift))
                    + (after[3] - before[3])
                )
                lift = cross * diffs[2]
                mid_b = side_on * b
                new_b = (
                    keep * b
                    + head_on * sums[1]
                    + side_on * sum_x[1]
                    + (up(mid_b + lift) + down(mid_b - lift))
                    + (cross * (after[2][0] - before[2][0]) - slopes_y[plane, row])
                )
                lift = cross * (after[0][0] - before[0][0]) + slope
                mid_c = head_on * c
                new_c = (
                    keep * c
                    + side_on * (sum_x[2] + sums[2])
                    + (up(mid_c + lift) + down(mid_c - lift))
                )
                yield [(new, (part, plane), value) for part, value in enumerate((new_a, new_b, new_c))]
                before, here = here, after

        return body

    def phase_pass(source, pot_now, disp_now, low, new):
        def body(row):
            def load(plane):
                if plane < 0 or plane >= planes:
                    return (1.0 if plane < 0 else 0.0, 0.0)
                return (source[plane, row], disp_now[0, plane, row])

            before, here = load(low - 1), load(low)
            for plane in range(low, planes):
                after = load(plane + 1)
                p = here[0]
                c = disp_now[2, plane, row]
                div = (
                    (after[1] - before[1])
                    + (disp_now[1, plane, row + 1] - disp_now[1, plane, row - 1])
                    + (up(c) - down(c))
                )
                over = (
                    (pot_now[plane, row] - REST)
                    + (0.5 * OMEGA_THIRD * STIFF) * div
                    - (OMEGA_THIRD * STIFF * 3.0 * EIGEN) * interp(p)
                )
                drive = jnp.exp(over) - jnp.exp(-over)
                lap = (
                    (before[0] + after[0])
                    + (source[plane, row + 1] + source[plane, row - 1])
                    + (up(p) + down(p))
                    - 6.0 * p
                )
                well = p * (1.0 - p)
                change = lap - well * (2.0 * (1.0 - 2.0 * p) + (6.0 * RATE) * drive)
                yield [(new, (plane,), p + TIME_STEP * change)]
                before, here = here, after

        return body

    for step in range(STEPS):
        last = step == STEPS - 1
        over_rows(conduct_pass(phase))
        for sweep in range(SWEEPS):
            ahead = SWEEPS - 1 - sweep
            over_rows(
                potential_pass(pot, pot_new, max(0, slab - ahead) if last else 0),
                elastic_pass(disp, disp_new, max(0, slab - ahead - 1) if last else 0),
            )
            pot, pot_new, disp, disp_new = pot_new, pot, disp_new, disp
            for ref in (pot, disp.at[0], disp.at[1], disp.at[2]):
                close(ref)
        over_rows(phase_pass(phase, pot, disp, slab if last else 0, phase_new))
        phase, phase_new = phase_new, phase
        if not last:
            close(phase)
    outs = results_of(part, all_rows)
    for field, ref in enumerate(parts_of(phase, pot, disp)):
        for plane in range(slab):
            for row in range(segment):
                to = pl.ds(row, TILE, stride=segment)
                natural[field, plane, to, :] = ref[slab + plane, 1 + row]
            for at in range(len(outs) // 2):
                pair = []
                for place in (at, at + len(outs) // 2):
                    spot = pl.ds(blocks.index(outs[place]) * TILE, TILE)
                    pair.append(natural[field, plane, spot, :])
                    result[field, plane, pl.ds(place * TILE, TILE), :] = pair[-1]
                to = pl.ds(((field * slab + plane) * len(outs) // 2 + at) * TILE, TILE)
                message[to, :] = jnp.where(mine, pair[0], turned(pair[1], LANES // 2))


def results_of(part, rows):
    start, stop = split(rows)
    edge = start + REACH
    if part == 0:
        return list(range(edge, rows - edge, TILE))
    return list(range(0, edge, TILE)) + list(range(rows - edge, rows, TILE))


def finish_kernel(part, result, message, *refs):
    phase, potential, displacement, whole, arrived = refs[3 * part :]
    _, slab, rows, _ = result.shape
    side = lax.axis_index("grow")
    mine = half_of(side)
    fresh = side == lax.axis_size("grow") - 1
    half = rows // 2
    edge = (phase.shape[1] - rows) // 2
    targets = (0, phase.shape[1] - half) if part else (edge, edge + half)
    copies = []
    for field in range(FIELDS):
        for plane in range(slab):
            for row in range(0, rows, TILE):
                spot = pl.ds((field * slab + plane) * half + row % half, TILE)
                block = message[spot, :]
                block = turned(block, LANES // 2) if row >= half else block
                block = jnp.where(mine, result[field, plane, pl.ds(row, TILE), :], block)
                block = jnp.where(fresh, V_HIGH if field == 1 else 0.0, block)
                whole[field, plane, pl.ds(row, TILE), :] = block
        out = (phase, potential, displacement.at[0], displacement.at[1], displacement.at[2])[field]
        for source, target in zip((0, half), targets):
            copy = pltpu.make_async_copy(
                whole.at[field, :, pl.ds(source, half), :],
                out.at[:, pl.ds(target, half), :],
                arrived.at[len(copies)],
            )
            copy.start()
            copies.append(copy)
    for copy in copies:
        copy.wait()


def call(kernel, outs, scratch=(), limit=48, **how):
    return pl.pallas_call(
        kernel,
        out_shape=[
            jax.ShapeDtypeStruct(one, jnp.float32) if isinstance(one, tuple) else one for one in outs
        ],
        scratch_shapes=[
            pltpu.VMEM(one, jnp.float32) if isinstance(one, tuple) else one for one in scratch
        ],
        **{"cost_estimate": pl.CostEstimate(flops=1, bytes_accessed=1, transcendentals=0), **how},
        compiler_params=pltpu.CompilerParams(vmem_limit_bytes=limit * 1024 * 1024),
    )


def pair_shards(labels, roughness, potential, displacement):
    slab, rows, _ = labels.shape
    count = FIELDS * slab
    start, stop = split(rows)
    half = (stop - start) // 2
    spare = -(-2 * count * REACH // LANES) * TILE
    sizes = {name: lax.axis_size(name) for name in ("grow", "cy", "cz")}

    def index(grow, cy, cz):
        cy, cz = cy % sizes["cy"], cz % sizes["cz"]
        return (grow * sizes["cy"] + cy) * sizes["cz"] + cz

    everyone = [
        (grow, cy, cz)
        for grow in range(sizes["grow"])
        for cy in range(sizes["cy"])
        for cz in range(sizes["cz"])
    ]

    def send(block, route):
        pairs = [(index(*at), index(*route(*at))) for at in everyone]
        return lax.ppermute(block, ("grow", "cy", "cz"), pairs)

    def to_partner(block):
        return send(block, lambda grow, cy, cz: (1 - grow, cy, cz))

    def beside_same(block):
        return send(block, lambda grow, cy, cz: (grow, cy, cz - 1 if grow else cz + 1))

    def beside_other(block):
        return send(block, lambda grow, cy, cz: (1 - grow, cy, cz + 1 if grow else cz - 1))

    in_vmem, anywhere, hbm = (
        pl.BlockSpec(memory_space=space) for space in (pltpu.VMEM, pl.ANY, pltpu.HBM)
    )
    thin = (count * TILE, LANES)
    fields, halves, same, other, first, last = call(
        prepare_kernel,
        [
            pltpu.VMEM(shape, jnp.float32)
            for shape in ((FIELDS,) + labels.shape, (count * (half + TILE), LANES), *[thin] * 4)
        ],
        [pltpu.VMEM(labels.shape, labels.dtype), labels.shape, pltpu.SemaphoreType.DMA((4,))],
        limit=54,
        in_specs=[hbm] * 4,
    )(labels, roughness, potential, displacement)
    halves = to_partner(halves)
    other = beside_other(other)
    above = send(last, lambda grow, cy, cz: (grow, cy + 1, cz))
    below = send(first, lambda grow, cy, cz: (grow, cy - 1, cz))
    same = beside_same(same)
    rest, same_rims, other_rims = call(
        rims_kernel,
        [(count * (start + TILE) + spare, LANES)] + [(2 * count // PER_TILE * TILE, LANES)] * 2,
        in_specs=[in_vmem] + [anywhere] * 2 + [in_vmem] * 2,
    )(fields, other, same, above, below)
    rest = to_partner(rest)
    other_rims = beside_other(other_rims)
    same_rims = beside_same(same_rims)
    results, messages, outs = [], [], []
    for part in range(2):
        span, done = (len(of(part, rows)) * TILE for of in (blocks_of, results_of))
        deep = (2 * slab, span // TILE + 2, TILE, LANES)
        (near,) = call(
            functools.partial(own_kernel, part),
            [(FIELDS, slab) + deep[1:]],
            [(count, span, LANES)],
            in_specs=[in_vmem] * (2 + 3 * part) + [anywhere] * part,
        )(fields, same, *([same_rims, above, below, *results] if part else []))
        result, message = call(
            functools.partial(steps_kernel, part, rows),
            [(FIELDS, slab, done, LANES), (count * done // 2, LANES)],
            [(FIELDS, slab, span, LANES)]
            + [deep] * 4
            + [(3,) + deep] * 2
            + [deep, deep, (2 * slab + 1,) + deep[1:], deep, deep, deep],
            in_specs=[in_vmem] * (3 + 2 * part) + [anywhere] * part,
            cost_estimate=pl.CostEstimate(
                flops=STEPS * SWEEPS * 160 * span * 2 * slab * LANES,
                bytes_accessed=STEPS * SWEEPS * 40 * span * 2 * slab * LANES,
                transcendentals=STEPS * 2 * span * 2 * slab * LANES,
            ),
        )(near, other, halves, *([other_rims, rest, *results] if part else []))
        results.append(result)
        messages.append(from_behind(message, "grow", -1))
    for part in range(2):
        outs = call(
            functools.partial(finish_kernel, part),
            [labels.shape, labels.shape, displacement.shape],
            [results[part].shape, pltpu.SemaphoreType.DMA((2 * FIELDS,))],
            in_specs=[in_vmem] * 2 + [hbm] * (3 * part),
            out_specs=[hbm] * 3,
            input_output_aliases={2 + which: which for which in range(3 * part)},
        )(results[part], messages[part], *outs)
    return outs


def fits_pair(labels):
    rows, columns = labels.shape[1:]
    start, stop = split(rows)
    blocks = rows % (2 * TILE) == 0 and rows // TILE * REACH <= LANES and start >= TILE
    return lax.axis_size("grow") == 2 and columns == LANES and REACH == TILE and blocks


def whole(labels, roughness, potential, displacement):
    plan = pair_shards if fits_pair(labels) else shards
    return tuple(plan(labels, roughness, potential, displacement))


def solution(mesh):
    placed = (
        P("grow", "cy", "cz"),
        P("grow", "cy", "cz"),
        P("grow", "cy", "cz"),
        P(None, "grow", "cy", "cz"),
    )
    return jax.shard_map(
        whole,
        mesh=mesh,
        in_specs=placed,
        out_specs=(P("grow", "cy", "cz"), P("grow", "cy", "cz"), P(None, "grow", "cy", "cz")),
        check_vma=False,
    )
```

```python
import functools

import jax
import jax.numpy as jnp
from jax import lax
from jax.experimental import pallas as pl
from jax.experimental.pallas import tpu as pltpu
from jax.sharding import PartitionSpec as P

STEPS = 2
SWEEPS = 3


TAU_P = 0.15
TAU_U = 0.08
SHEAR = 1.0
LAME_FIRST = 1.5
STIFF = 6.5
EIGEN = 0.1
COND_EL = 0.1
COND_LI = 0.9
V_HIGH = 1.0
TIME_STEP = 0.05
REST = 0.5
OMEGA_THIRD = 0.1
RATE = 0.5


def extended(cells, sides, width, closed):
    for axis, dim in sides:
        count = lax.axis_size(axis)
        ends = count if closed else count - 1
        head = lax.slice_in_dim(cells, 0, width, axis=dim)
        tail = lax.slice_in_dim(cells, cells.shape[dim] - width, cells.shape[dim], axis=dim)
        cells = jnp.concatenate(
            [
                lax.ppermute(tail, axis, [(i, (i + 1) % count) for i in range(ends)]),
                cells,
                lax.ppermute(head, axis, [((i + 1) % count, i) for i in range(ends)]),
            ],
            axis=dim,
        )
    return cells


def from_behind(block, axis, distance):
    devices = range(lax.axis_size(axis))
    route = [(i - distance, i) for i in devices if i - distance in devices]
    return lax.ppermute(block, axis, route)


def unit(direction, sign):
    offsets = [0, 0, 0]
    offsets[direction] = sign
    return offsets


def offset(field, offsets):
    lead_dims = field.ndim - 3
    slices = [slice(None)] * lead_dims
    for direction in range(3):
        extent = field.shape[lead_dims + direction]
        slices.append(slice(1 + offsets[direction], extent - 1 + offsets[direction]))
    return field[tuple(slices)]


def centre(field):
    return offset(field, (0, 0, 0))


def laplace(field):
    total = -6.0 * centre(field)
    for direction in range(3):
        total = total + offset(field, unit(direction, 1)) + offset(field, unit(direction, -1))
    return total


def interp(phase):
    return phase * phase * (3.0 - 2.0 * phase)


def interp_slope(phase):
    return 6.0 * phase * (1.0 - phase)


def potential_sweep(potential_pad, conduct_pad):
    here = centre(potential_pad)
    conduct_here = centre(conduct_pad)
    flux = jnp.zeros_like(here)
    for direction in range(3):
        for sign in (1, -1):
            moved = unit(direction, sign)
            flux = flux + 0.5 * (offset(conduct_pad, moved) + conduct_here) * (
                offset(potential_pad, moved) - here
            )
    return here + TAU_P * flux


def cross_term(field, first, second):
    total = jnp.zeros_like(centre(field))
    for sign_first in (1, -1):
        for sign_second in (1, -1):
            offsets = [0, 0, 0]
            offsets[first] = sign_first
            offsets[second] = sign_second
            total = total + sign_first * sign_second * offset(field, offsets)
    return 0.25 * total


def elastic_sweep(disp_pad, interp_pad):
    updated = []
    for component in range(3):
        own = disp_pad[component]
        grad_div = (
            offset(own, unit(component, 1)) - 2.0 * centre(own) + offset(own, unit(component, -1))
        )
        for other in range(3):
            if other != component:
                grad_div = grad_div + cross_term(disp_pad[other], component, other)
        slope = 0.5 * (
            offset(interp_pad, unit(component, 1)) - offset(interp_pad, unit(component, -1))
        )
        force = SHEAR * laplace(own) + (LAME_FIRST + SHEAR) * grad_div - STIFF * EIGEN * slope
        updated.append(centre(own) + TAU_U * force)
    return jnp.stack(updated)


def divergence(disp_pad):
    total = jnp.zeros_like(centre(disp_pad[0]))
    for component in range(3):
        total = total + 0.5 * (
            offset(disp_pad[component], unit(component, 1))
            - offset(disp_pad[component], unit(component, -1))
        )
    return total


def phase_update(phase_pad, potential, div_disp):
    phase = centre(phase_pad)
    trace = STIFF * (div_disp - 3.0 * EIGEN * interp(phase))
    over = potential - REST + OMEGA_THIRD * trace
    drive = jnp.exp(over) - jnp.exp(-over)
    change = (
        laplace(phase_pad)
        - 2.0 * phase * (1.0 - phase) * (1.0 - 2.0 * phase)
        - RATE * interp_slope(phase) * drive
    )
    return phase + TIME_STEP * change


def pin_ends(field, width, slab, low, high):
    if width == 0:
        return field
    lead_dims = field.ndim - 3
    planes = field.shape[lead_dims]
    first = lax.axis_index("grow") * slab - width
    position = first + lax.broadcasted_iota(jnp.int32, (planes, 1, 1), 0)
    limit = slab * lax.axis_size("grow")
    result = jnp.where(position < 0, low, field)
    return jnp.where(position >= limit, high, result)


def column_values(values):
    return jnp.array(values, jnp.float32).reshape(len(values), 1, 1, 1)


def strip(field, count):
    for repeat in range(count):
        field = centre(field)
    return field


def shards(labels, roughness, potential, displacement):
    slab = labels.shape[0]
    rim = SWEEPS + 1
    mark = labels.astype(jnp.float32)
    phase = mark * (1.0 - 0.3 * roughness) + (1.0 - mark) * (0.3 * roughness)
    low_five = column_values([1.0, 0.0, 0.0, 0.0, 0.0])
    high_five = column_values([0.0, V_HIGH, 0.0, 0.0, 0.0])
    for step_index in range(STEPS):
        packed = jnp.concatenate([phase[None], potential[None], displacement], axis=0)
        packed = extended(packed, (("grow", 1),), SWEEPS + 1, False)
        packed = pin_ends(packed, SWEEPS + 1, slab, low_five, high_five)
        packed = extended(packed, (("cy", 2), ("cz", 3)), SWEEPS + 1, True)
        phase_pad = packed[0]
        interp_pad = interp(phase_pad)
        conduct_pad = COND_EL + COND_LI * interp_pad
        pot_pad = strip(packed[1], 1)
        conduct_now = centre(conduct_pad)
        for repeat in range(SWEEPS):
            pot_pad = pin_ends(
                potential_sweep(pot_pad, conduct_now), SWEEPS - 1 - repeat, slab, 0.0, V_HIGH
            )
            if repeat + 1 < SWEEPS:
                conduct_now = centre(conduct_now)
        potential = pot_pad
        disp_pad = packed[2:]
        interp_now = interp_pad
        for repeat in range(SWEEPS):
            disp_pad = pin_ends(
                elastic_sweep(disp_pad, interp_now), SWEEPS - repeat, slab, 0.0, 0.0
            )
            if repeat + 1 < SWEEPS:
                interp_now = centre(interp_now)
        div_disp = divergence(disp_pad)
        displacement = centre(disp_pad)
        phase = phase_update(strip(phase_pad, rim - 1), potential, div_disp)
    stacked = jnp.concatenate([phase[None], potential[None], displacement], axis=0)
    arrived = from_behind(stacked, "grow", -1)
    fresh = jnp.array([0.0, V_HIGH, 0.0, 0.0, 0.0], jnp.float32).reshape(5, 1, 1, 1)
    is_last = lax.axis_index("grow") == lax.axis_size("grow") - 1
    arrived = jnp.where(is_last, fresh, arrived)
    return (arrived[0], arrived[1], arrived[2:])


REACH = STEPS * (SWEEPS + 1)
TILE = 8
FIELDS = 5
LAG = 2
TOGETHER = 12


def lanes(shape):
    return lax.broadcasted_iota(jnp.int32, shape, 1)


def from_lane(first):
    lane = lanes((TILE, LANES))
    return jnp.logical_and(lane >= first, lane < first + REACH)


LANES = 128


def turned(block, amount):
    return pltpu.roll(block, lax.rem(amount + 2 * LANES, LANES), 1)


def half_of(side):
    low = lanes((TILE, LANES)) < LANES // 2
    return jnp.logical_xor(low, side == 1)


def pack_halves(fields, upper, lower, mid, theirs, out):
    _, slab, _, _ = fields.shape
    for field in range(FIELDS):
        for plane in range(slab):
            for row in range(0, mid, TILE):
                one = fields[field, plane, pl.ds(upper + row, TILE), :]
                two = fields[field, plane, pl.ds(lower + row, TILE), :]
                to = pl.ds((field * slab + plane) * mid + row, TILE)
                out[to, :] = jnp.where(theirs, one, turned(two, LANES // 2))


def pack_strips(fields, base, out, start):
    _, slab, rows, _ = fields.shape
    for field in range(FIELDS):
        for plane in range(slab):
            packed = jnp.zeros((TILE, LANES), jnp.float32)
            for group in range(rows // TILE):
                block = fields[field, plane, pl.ds(group * TILE, TILE), :]
                block = turned(block, group * REACH - base)
                packed = jnp.where(from_lane(group * REACH), block, packed)
            out[pl.ds(start + (field * slab + plane) * TILE, TILE), :] = packed


def pack_rim_strips(above, below, base, out, start):
    per = LANES // REACH
    blocks = 2 * above.shape[0] // TILE
    for first in range(0, blocks, per):
        packed = jnp.zeros((TILE, LANES), jnp.float32)
        for which in range(first, min(first + per, blocks)):
            block = (above, below)[which % 2][pl.ds(which // 2 * TILE, TILE), :]
            to = which % per * REACH
            packed = jnp.where(from_lane(to), turned(block, to - base), packed)
        out[pl.ds(start + first // per * TILE, TILE), :] = packed


def strip_bases(side):
    outer = LANES - REACH
    return LANES // 2 - REACH + REACH * side, outer * (1 - side), outer * side


def split(rows):
    return rows // 4 - REACH, 3 * rows // 4 + REACH


def prepare_kernel(
    labels, roughness, potential, displacement,
    fields, halves, same, other, first, last, marks, rough, arrived,
):
    _, slab, rows, _ = fields.shape
    side = lax.axis_index("grow")
    count = FIELDS * slab
    copies = [
        pltpu.make_async_copy(source, target, arrived.at[which])
        for which, (source, target) in enumerate(
            (
                (labels, marks),
                (roughness, rough),
                (potential, fields.at[1]),
                (displacement, fields.at[pl.ds(2, 3)]),
            )
        )
    ]
    for copy in copies:
        copy.start()
    for copy in copies[:2]:
        copy.wait()
    for plane in range(slab):
        for row in range(0, rows, TILE):
            spot = (plane, pl.ds(row, TILE), slice(None))
            mark = marks[spot].astype(jnp.float32)
            part = 0.3 * rough[spot]
            fields[(0,) + spot] = mark * (1.0 - part) + (1.0 - mark) * part
    for copy in copies[2:]:
        copy.wait()
    start, stop = split(rows)
    mid = (stop - start) // 2
    pack_halves(fields, start, start + mid, mid, jnp.logical_not(half_of(side)), halves)
    for out, at, base in zip((halves, same, other), (count * mid, 0, 0), strip_bases(side)):
        pack_strips(fields, base, out, at)
    for field in range(FIELDS):
        for plane in range(slab):
            spot = pl.ds((field * slab + plane) * TILE, TILE)
            first[spot, :] = fields[field, plane, pl.ds(0, TILE), :]
            last[spot, :] = fields[field, plane, pl.ds(rows - TILE, TILE), :]


def rims_kernel(fields, other_first, same_first, above, below, halves, same, other):
    _, slab, rows, _ = fields.shape
    side = lax.axis_index("grow")
    theirs = jnp.logical_not(half_of(side))
    count = FIELDS * slab
    start, stop = split(rows)
    pack_halves(fields, 0, stop, start, theirs, halves)
    for which in range(count):
        spot = pl.ds(which * TILE, TILE)
        rims = jnp.where(theirs, above[spot, :], turned(below[spot, :], LANES // 2))
        halves[pl.ds(count * start + which * TILE, TILE), :] = rims
    starts = (count * (start + TILE), 0, 0)
    for out, at, base in zip((halves, same, other), starts, strip_bases(side)):
        pack_rim_strips(above, below, base, out, at)


def blocks_of(part, rows):
    start, stop = split(rows)
    if part == 0:
        return list(range(start, stop, TILE))
    inner = start + 2 * REACH
    return list(range(-REACH, inner, TILE)) + list(range(rows - inner, rows + REACH, TILE))


def packed_at(which, row, rows, count):
    if 0 <= row < rows:
        return False, which * TILE, row // TILE * REACH
    at, group = divmod(2 * which + int(row > 0), LANES // REACH)
    return True, at * TILE, group * REACH


def own_kernel(part, fields, *refs):
    out, natural = refs[-2:]
    same, *more = refs[:-2]
    same_rims, above, below, _ = more or (None,) * 4
    _, slab, rows, _ = fields.shape
    count = FIELDS * slab
    outer = (LANES - REACH) * (1 - lax.axis_index("grow"))
    in_outer = from_lane(outer)
    segment = out.shape[2] - 2
    for field in range(FIELDS):
        for plane in range(slab):
            which = field * slab + plane
            for at, row in enumerate(blocks_of(part, rows)):
                of_rim, spot, lane = packed_at(which, row, rows, count)
                piece = (same_rims if of_rim else same)[pl.ds(spot, TILE), :]
                if of_rim:
                    near = (below if row > 0 else above)[pl.ds(which * TILE, TILE), :]
                else:
                    near = fields[field, plane, pl.ds(row, TILE), :]
                near = jnp.where(in_outer, turned(piece, outer - lane), near)
                natural[which, pl.ds(at * TILE, TILE), :] = near
            blocks = [natural[which, pl.ds(row, TILE, stride=segment), :] for row in range(segment)]
            blocks = [pltpu.roll(blocks[-1], 1, 0), *blocks, pltpu.roll(blocks[0], TILE - 1, 0)]
            for row, block in enumerate(blocks):
                out[field, plane, row] = block


def face_conduct(step):
    return 0.5 * TAU_P * COND_EL + 0.5 * TAU_P * COND_LI * step


def steps_kernel(part, near, other, halves, *refs):
    if part:
        other_rims, rest, _, *refs = refs
    result, message, natural, phase, phase_new, pot, pot_new, disp, disp_new = refs[:9]
    slopes, slopes_y, cond_x, cond_y, cond_z = refs[9:]
    _, slab, rows, _ = result.shape
    all_rows = 2 * rows
    planes = 2 * slab
    side = lax.axis_index("grow")
    mine = half_of(side)
    count = FIELDS * slab
    inner = LANES // 2 - REACH * side
    outer = (LANES - REACH) * (1 - side)
    in_inner, in_outer = from_lane(inner), from_lane(outer)
    segment = phase.shape[1] - 2
    start, stop = split(all_rows)
    half = (stop - start) // 2
    blocks = blocks_of(part, all_rows)

    def arrived_half(which, row):
        if start <= row < stop:
            block = halves[pl.ds(which * half + (row - start) % half, TILE), :]
            return turned(block, LANES // 2) if row - start >= half else block
        if 0 <= row < all_rows:
            block = rest[pl.ds(which * start + row % stop, TILE), :]
        else:
            block = rest[pl.ds(count * start + which * TILE, TILE), :]
        return turned(block, LANES // 2) if row > 0 and row >= stop else block

    for field in range(FIELDS):
        for plane in range(slab):
            which = field * slab + plane
            for at, row in enumerate(blocks):
                of_rim, spot, lane = packed_at(which, row, all_rows, count)
                if of_rim:
                    strip = rest[pl.ds(count * (start + TILE) + spot, TILE), :]
                    beside = other_rims[pl.ds(spot, TILE), :]
                else:
                    strip = halves[pl.ds(count * half + spot, TILE), :]
                    beside = other[pl.ds(spot, TILE), :]
                block = jnp.where(in_inner, turned(strip, inner - lane), arrived_half(which, row))
                block = jnp.where(in_outer, turned(beside, outer - lane), block)
                natural[field, plane, pl.ds(at * TILE, TILE), :] = block

    def parts_of(phase, pot, disp):
        return (phase, pot, disp.at[0], disp.at[1], disp.at[2])

    def close(ref):
        for plane in range(planes):
            ref[plane, 0] = pltpu.roll(ref[plane, segment], 1, 0)
            ref[plane, segment + 1] = pltpu.roll(ref[plane, 1], TILE - 1, 0)

    for field, ref in enumerate(parts_of(phase, pot, disp)):
        for plane in range(slab):
            own, far = side * slab + plane, (1 - side) * slab + plane
            for row in range(segment + 2):
                ref[own, row] = near[field, plane, row]
            for row in range(segment):
                ref[far, 1 + row] = natural[field, plane, pl.ds(row, TILE, stride=segment), :]
            ref[far, 0] = pltpu.roll(ref[far, segment], 1, 0)
            ref[far, segment + 1] = pltpu.roll(ref[far, 1], TILE - 1, 0)

    def one_row(row, bodies):
        waiting = []
        running = [body(row) for body in bodies]
        while running:
            for body in list(running):
                stores = next(body, None)
                if stores is None:
                    running.remove(body)
                else:
                    waiting.append(stores)
            while len(waiting) > LAG * len(bodies) or (waiting and not running):
                for ref, lead, value in waiting.pop(0):
                    ref[lead + (row,)] = value

    def over_rows(*bodies):
        together = max(n for n in range(1, TOGETHER + 1) if segment % n == 0)

        def some(turn, carry):
            for more in range(together):
                one_row(1 + turn * together + more, bodies)
            return carry

        if together == segment:
            some(0, 0)
        else:
            lax.fori_loop(0, segment // together, some, 0)

    def up(block):
        return pltpu.roll(block, LANES - 1, 1)

    def down(block):
        return pltpu.roll(block, 1, 1)

    push = 0.5 * STIFF * EIGEN / SHEAR

    def conduct_pass(source):
        known = {}

        def step_at(plane, row):
            if not isinstance(row, int):
                return interp(source[plane, row])
            if (plane, row) not in known:
                known[plane, row] = interp(source[plane, row])
            return known[plane, row]

        def body(row):
            before = face_conduct(1.0)
            for plane in range(planes):
                step, ahead, back = (step_at(plane, row + shift) for shift in (0, 1, -1))
                here = face_conduct(step)
                yield [
                    (slopes, (plane,), push * step),
                    (slopes_y, (plane,), push * (ahead - back)),
                    (cond_x, (plane,), before + here),
                    (cond_y, (plane,), here + face_conduct(ahead)),
                    (cond_z, (plane,), here + up(here)),
                ]
                before = here
            yield [(cond_x, (planes,), before + face_conduct(0.0))]

        for plane in range(planes):
            first, second = (face_conduct(step_at(plane, row)) for row in (0, 1))
            cond_y[plane, 0] = first + second
        return body

    def potential_pass(old, new, low):
        def body(row):
            here = old[low, row]
            before = old[low - 1, row] if low else 0.0
            entering = cond_x[low, row] * (here - before)
            for plane in range(low, planes):
                after = old[plane + 1, row] if plane + 1 < planes else V_HIGH
                leaving = cond_x[plane + 1, row] * (after - here)
                along_y = cond_y[plane, row] * (old[plane, row + 1] - here)
                along_y -= cond_y[plane, row - 1] * (here - old[plane, row - 1])
                along_z = cond_z[plane, row] * (up(here) - here)
                along_z -= down(along_z)
                yield [(new, (plane,), here + ((leaving - entering) + along_y + along_z))]
                here, entering = after, leaving

        return body

    grad = LAME_FIRST + SHEAR
    cross = 0.25 * grad / SHEAR
    head_on = 1.0 + grad / SHEAR
    scale = TAU_U * SHEAR
    keep = 1.0 - TAU_U * (6.0 * SHEAR + 2.0 * grad)

    def elastic_pass(old, new, low):
        def body(row):
            def load(plane):
                if plane < 0 or plane >= planes:
                    return (0.0,) * 3, (0.0,) * 3, (0.0,) * 3, -push if plane < 0 else 0.0
                parts = [old[part, plane, row] for part in range(3)]
                ahead = [old[part, plane, row + 1] for part in range(3)]
                back = [old[part, plane, row - 1] for part in range(3)]
                sums = [one + two for one, two in zip(ahead, back)]
                diffs = [one - two for one, two in zip(ahead, back)]
                return parts, sums, diffs, cross * diffs[1] - slopes[plane, row]

            before, here = load(low - 1), load(low)
            for plane in range(low, planes):
                after = load(plane + 1)
                (a, b, c), sums, diffs, slope = here
                sum_x = [one + two for one, two in zip(after[0], before[0])]
                lift = cross * (after[0][2] - before[0][2])
                force = (head_on * sum_x[0] + sums[0]) + (after[3] - before[3])
                force += up(a + lift) + down(a - lift)
                new_a = keep * a + scale * force
                lift = cross * diffs[2]
                force = cross * (after[2][0] - before[2][0]) - slopes_y[plane, row]
                force += head_on * sums[1] + sum_x[1]
                force += up(b + lift) + down(b - lift)
                new_b = keep * b + scale * force
                lift = cross * (after[0][0] - before[0][0]) + slope
                mid_c = head_on * c
                force = sum_x[2] + sums[2]
                force += up(mid_c + lift) + down(mid_c - lift)
                new_c = keep * c + scale * force
                yield [(new, (part, plane), value) for part, value in enumerate((new_a, new_b, new_c))]
                before, here = here, after

        return body

    def phase_pass(source, pot_now, disp_now, low, new):
        def body(row):
            def load(plane):
                if plane < 0 or plane >= planes:
                    return (1.0 if plane < 0 else 0.0, 0.0)
                return (source[plane, row], disp_now[0, plane, row])

            before, here = load(low - 1), load(low)
            for plane in range(low, planes):
                after = load(plane + 1)
                p = here[0]
                c = disp_now[2, plane, row]
                div = (
                    (after[1] - before[1])
                    + (disp_now[1, plane, row + 1] - disp_now[1, plane, row - 1])
                    + (up(c) - down(c))
                )
                over = (
                    (pot_now[plane, row] - REST)
                    + (0.5 * OMEGA_THIRD * STIFF) * div
                    - (OMEGA_THIRD * STIFF * 3.0 * EIGEN) * interp(p)
                )
                drive = jnp.exp(over) - jnp.exp(-over)
                lap = (
                    (before[0] + after[0])
                    + (source[plane, row + 1] + source[plane, row - 1])
                    + (up(p) + down(p))
                    - 6.0 * p
                )
                well = p * (1.0 - p)
                change = lap - well * (2.0 * (1.0 - 2.0 * p) + (6.0 * RATE) * drive)
                yield [(new, (plane,), p + TIME_STEP * change)]
                before, here = here, after

        return body

    for step in range(STEPS):
        last = step == STEPS - 1
        over_rows(conduct_pass(phase))
        for sweep in range(SWEEPS):
            ahead = SWEEPS - 1 - sweep
            over_rows(
                potential_pass(pot, pot_new, max(0, slab - ahead) if last else 0),
                elastic_pass(disp, disp_new, max(0, slab - ahead - 1) if last else 0),
            )
            pot, pot_new, disp, disp_new = pot_new, pot, disp_new, disp
            for ref in (pot, disp.at[0], disp.at[1], disp.at[2]):
                close(ref)
        over_rows(phase_pass(phase, pot, disp, slab if last else 0, phase_new))
        phase, phase_new = phase_new, phase
        if not last:
            close(phase)
    outs = results_of(part, all_rows)
    for field, ref in enumerate(parts_of(phase, pot, disp)):
        for plane in range(slab):
            for row in range(segment):
                to = pl.ds(row, TILE, stride=segment)
                natural[field, plane, to, :] = ref[slab + plane, 1 + row]
            for at in range(len(outs) // 2):
                pair = []
                for place in (at, at + len(outs) // 2):
                    spot = pl.ds(blocks.index(outs[place]) * TILE, TILE)
                    pair.append(natural[field, plane, spot, :])
                    result[field, plane, pl.ds(place * TILE, TILE), :] = pair[-1]
                to = pl.ds(((field * slab + plane) * len(outs) // 2 + at) * TILE, TILE)
                message[to, :] = jnp.where(mine, pair[0], turned(pair[1], LANES // 2))


def results_of(part, rows):
    quarter = rows // 4
    if part == 0:
        return list(range(quarter, 3 * quarter, TILE))
    return list(range(0, quarter, TILE)) + list(range(3 * quarter, rows, TILE))


def finish_kernel(part, result, message, *refs):
    phase, potential, displacement, whole, arrived = refs[3 * part :]
    _, slab, rows, _ = result.shape
    side = lax.axis_index("grow")
    mine = half_of(side)
    fresh = side == lax.axis_size("grow") - 1
    half = rows // 2
    copies = []
    for field in range(FIELDS):
        for plane in range(slab):
            for row in range(0, rows, TILE):
                spot = pl.ds((field * slab + plane) * half + row % half, TILE)
                block = message[spot, :]
                block = turned(block, LANES // 2) if row >= half else block
                block = jnp.where(mine, result[field, plane, pl.ds(row, TILE), :], block)
                block = jnp.where(fresh, V_HIGH if field == 1 else 0.0, block)
                whole[field, plane, pl.ds(row, TILE), :] = block
        out = (phase, potential, displacement.at[0], displacement.at[1], displacement.at[2])[field]
        for source, target in (((0, 0), (half, 3 * half)) if part else ((0, half), (half, rows))):
            copy = pltpu.make_async_copy(
                whole.at[field, :, pl.ds(source, half), :],
                out.at[:, pl.ds(target, half), :],
                arrived.at[len(copies)],
            )
            copy.start()
            copies.append(copy)
    for copy in copies:
        copy.wait()


def call(kernel, outs, scratch=(), limit=48, **how):
    return pl.pallas_call(
        kernel,
        out_shape=[
            jax.ShapeDtypeStruct(one, jnp.float32) if isinstance(one, tuple) else one for one in outs
        ],
        scratch_shapes=[
            pltpu.VMEM(one, jnp.float32) if isinstance(one, tuple) else one for one in scratch
        ],
        **{"cost_estimate": pl.CostEstimate(flops=1, bytes_accessed=1, transcendentals=0), **how},
        compiler_params=pltpu.CompilerParams(vmem_limit_bytes=limit * 1024 * 1024),
    )


def pair_shards(labels, roughness, potential, displacement):
    slab, rows, _ = labels.shape
    count = FIELDS * slab
    start, stop = split(rows)
    half = (stop - start) // 2
    spare = -(-2 * count * REACH // LANES) * TILE
    sizes = {name: lax.axis_size(name) for name in ("grow", "cy", "cz")}

    def index(grow, cy, cz):
        cy, cz = cy % sizes["cy"], cz % sizes["cz"]
        return (grow * sizes["cy"] + cy) * sizes["cz"] + cz

    everyone = [
        (grow, cy, cz)
        for grow in range(sizes["grow"])
        for cy in range(sizes["cy"])
        for cz in range(sizes["cz"])
    ]

    def send(block, route):
        pairs = [(index(*at), index(*route(*at))) for at in everyone]
        return lax.ppermute(block, ("grow", "cy", "cz"), pairs)

    def to_partner(block):
        return send(block, lambda grow, cy, cz: (1 - grow, cy, cz))

    def beside_same(block):
        return send(block, lambda grow, cy, cz: (grow, cy, cz - 1 if grow else cz + 1))

    def beside_other(block):
        return send(block, lambda grow, cy, cz: (1 - grow, cy, cz + 1 if grow else cz - 1))

    in_vmem, anywhere, hbm = (
        pl.BlockSpec(memory_space=space) for space in (pltpu.VMEM, pl.ANY, pltpu.HBM)
    )
    thin = (count * TILE, LANES)
    fields, halves, same, other, first, last = call(
        prepare_kernel,
        [
            pltpu.VMEM(shape, jnp.float32)
            for shape in ((FIELDS,) + labels.shape, (count * (half + TILE), LANES), *[thin] * 4)
        ],
        [pltpu.VMEM(labels.shape, labels.dtype), labels.shape, pltpu.SemaphoreType.DMA((4,))],
        limit=54,
        in_specs=[hbm] * 4,
    )(labels, roughness, potential, displacement)
    halves = to_partner(halves)
    other = beside_other(other)
    above = send(last, lambda grow, cy, cz: (grow, cy + 1, cz))
    below = send(first, lambda grow, cy, cz: (grow, cy - 1, cz))
    same = beside_same(same)
    rest, same_rims, other_rims = call(
        rims_kernel,
        [(count * (start + TILE) + spare, LANES)] + [(spare, LANES)] * 2,
        in_specs=[in_vmem] + [anywhere] * 2 + [in_vmem] * 2,
    )(fields, other, same, above, below)
    rest = to_partner(rest)
    other_rims = beside_other(other_rims)
    same_rims = beside_same(same_rims)
    results, messages, outs = [], [], []
    for part in range(2):
        span = len(blocks_of(part, rows)) * TILE
        deep = (2 * slab, span // TILE + 2, TILE, LANES)
        (near,) = call(
            functools.partial(own_kernel, part),
            [(FIELDS, slab) + deep[1:]],
            [(count, span, LANES)],
            in_specs=[in_vmem] * (2 + 3 * part) + [anywhere] * part,
        )(fields, same, *([same_rims, above, below, *results] if part else []))
        result, message = call(
            functools.partial(steps_kernel, part),
            [(FIELDS, slab, rows // 2, LANES), (count * rows // 4, LANES)],
            [(FIELDS, slab, span, LANES)]
            + [deep] * 4
            + [(3,) + deep] * 2
            + [deep, deep, (2 * slab + 1,) + deep[1:], deep, deep],
            in_specs=[in_vmem] * (3 + 2 * part) + [anywhere] * part,
            cost_estimate=pl.CostEstimate(
                flops=STEPS * SWEEPS * 160 * span * 2 * slab * LANES,
                bytes_accessed=STEPS * SWEEPS * 40 * span * 2 * slab * LANES,
                transcendentals=STEPS * 2 * span * 2 * slab * LANES,
            ),
        )(near, other, halves, *([other_rims, rest, *results] if part else []))
        results.append(result)
        messages.append(from_behind(message, "grow", -1))
    for part in range(2):
        outs = call(
            functools.partial(finish_kernel, part),
            [labels.shape, labels.shape, displacement.shape],
            [(FIELDS, slab, rows // 2, LANES), pltpu.SemaphoreType.DMA((2 * FIELDS,))],
            in_specs=[in_vmem] * 2 + [hbm] * (3 * part),
            out_specs=[hbm] * 3,
            input_output_aliases={2 + which: which for which in range(3 * part)},
        )(results[part], messages[part], *outs)
    return outs


def fits_pair(labels):
    rows, columns = labels.shape[1:]
    blocks = rows % (8 * TILE) == 0 and rows // TILE * REACH <= LANES
    return lax.axis_size("grow") == 2 and columns == LANES and REACH == TILE and blocks


def whole(labels, roughness, potential, displacement):
    plan = pair_shards if fits_pair(labels) else shards
    return tuple(plan(labels, roughness, potential, displacement))


def solution(mesh):
    placed = (
        P("grow", "cy", "cz"),
        P("grow", "cy", "cz"),
        P("grow", "cy", "cz"),
        P(None, "grow", "cy", "cz"),
    )
    return jax.shard_map(
        whole,
        mesh=mesh,
        in_specs=placed,
        out_specs=(P("grow", "cy", "cz"), P("grow", "cy", "cz"), P(None, "grow", "cy", "cz")),
        check_vma=False,
    )
```
